32 devices in a mesh: tile: 16 (over z, y, core), layer: 2 (over x).
Axes of the slice: x: 2, y: 2, z: 4, core: 2. Of those that a mesh axis runs over, the one named last changes fastest.
Arguments:
- class_index: int32 [2, 2, 256, 8192], P('layer', None, 'tile'), may hold values from 0 to 15
- class_conductance: float32 [2, 16], P('layer'), may hold values from 0.5 to 8
- loads: float32 [2, 256, 8192], P('layer', 'tile'), may hold values from -4 to 4
- start_volts: float32 [2, 256, 8192], P('layer', 'tile'), may hold values from 0.8 to 1
- via_cells: int32 [2, 131072], P('layer', 'tile'), may hold values from 0 to 15, as said below
- via_counts: int32 [2, 131072], P('layer', 'tile'), may hold values from 0 to 4
Outputs:
- volts: float32 [2, 256, 8192], P('layer', 'tile')
The draws below stay inside these ranges and needn't reach their ends.
Inputs may be any that keep to these rules, and one draw needn't show every extreme that they name: `via_cells`: each slot names a row of its own strip; slot s sits in column s % 8192, so each column of a strip holds exactly one slot of each layer.
All inputs are finite; a program needn't handle non-finite values.
Results may differ from the reference program's by a relative error of at most 0.00002.
Values sent between devices are 32-bit elements; how exact they have to be, the bound alone decides.
No kernel may reach another device: no remote copies, remote signals or barrier semaphores. Data moves between devices by JAX's collectives and lax.ppermute only.
A program may use at most 64 MiB of HBM per device.

```python
import math
import jax
import jax.numpy as jnp

ROWS = 16
COLS = 8192
CLASSES = 16
OUTER = 2
SWEEPS = 3
VIAS_DEV = 8192
LAYERS = 2
TILES = 16


def draw_via_cells(key, part):
    values = jax.random.randint(key, (LAYERS, TILES * VIAS_DEV), 0, ROWS, dtype=jnp.int32)
    values = values.at[0, 0].set(ROWS - 1)
    values = values.at[0, 1].set(0)
    return values


def plant(drawn, stream_key, smallest, high):
    place = [jax.random.randint(jax.random.fold_in(stream_key, axis), (), 0, length) for axis, length in enumerate(drawn.shape)]
    longest = drawn.shape.index(max(drawn.shape))
    neighbour = place[:longest] + [(place[longest] + 1) % drawn.shape[longest]] + place[longest + 1:]
    return drawn.at[tuple(place)].set(smallest).at[tuple(neighbour)].set(high)


def levels(own_key, shape, cuts, low, high):
    gain, own = 1.0, jax.random.fold_in(own_key, 6)
    for dim, shards_of in cuts:
        steps = jnp.exp(jax.random.uniform(jax.random.fold_in(own, dim), (shards_of,), jnp.float32, low / len(cuts), high / len(cuts)))
        gain = gain * jnp.repeat(steps, shape[dim] // shards_of).reshape([-1 if axis == dim else 1 for axis in range(len(shape))])
    return gain


def centred(key, shape, spread, most, split=(), kind=jnp.bfloat16):
    array = jax.random.normal(key, shape, jnp.float32) * spread
    if len(split) > 0:
        array = levels(key, shape, split, -0.22, 0.18) * array
    return jnp.clip(array, min=-most, max=most).astype(kind)


def setup_inputs(seed: int = 0) -> dict:
    keys = jax.random.split(jax.random.key(seed), 7)
    return {
        "class_index": plant(jax.random.randint(keys[0], (LAYERS, 2, ROWS * TILES, COLS), 0, CLASSES), jax.random.fold_in(keys[0], 1), 0, CLASSES - 1).astype(jnp.int32),
        "class_conductance": jnp.clip(jnp.exp(math.log(8.0) - 2.7725887 * jax.random.uniform(keys[1], (LAYERS, CLASSES), jnp.float32) ** levels(keys[1], (LAYERS, CLASSES), ((0, 2),), -0.2, 0.2)), 0.5, 8.0),
        "loads": centred(keys[2], (LAYERS, ROWS * TILES, COLS), 0.3, 4.0, ((0, 2), (1, 16)), jnp.float32),
        "start_volts": jnp.clip(0.8 + 0.19999999 * jax.random.uniform(keys[3], (LAYERS, ROWS * TILES, COLS), jnp.float32) ** levels(keys[3], (LAYERS, ROWS * TILES, COLS), ((0, 2), (1, 16)), -0.2, 0.2), 0.8, 1.0),
        "via_cells": draw_via_cells(jax.random.fold_in(keys[6], 71), 0),
        "via_counts": plant(jax.random.randint(keys[5], (LAYERS, TILES * VIAS_DEV), 0, 5), jax.random.fold_in(keys[5], 1), 0, 4).astype(jnp.int32),
    }


VIA_UNIT = 2.0
LOWER_BOUND = 0.05
UPPER_BOUND = 2.0


def chebyshev_terms(count):
    centre_value = 0.5 * (UPPER_BOUND + LOWER_BOUND)
    half_width = 0.5 * (UPPER_BOUND - LOWER_BOUND)
    sigma = centre_value / half_width
    rho_last = 1.0 / sigma
    terms = [(0.0, 1.0 / centre_value)]
    for index in range(1, count):
        rho_next = 1.0 / (2.0 * sigma - rho_last)
        terms.append((rho_next * rho_last, 2.0 * rho_next / half_width))
        rho_last = rho_next
    return terms


def lookup(class_codes, class_table):
    result = jnp.zeros(class_codes.shape, jnp.float32)
    for code in range(CLASSES):
        result = result + jnp.where(class_codes == code, class_table[code], jnp.float32(0.0))
    return result


def neighbours(padded, vertical_links, across):
    span = padded.shape[0]
    centre_cells = padded[1:span - 1]
    vertical = vertical_links[0:span - 2] * padded[0:span - 2] + vertical_links[1:span - 1] * padded[2:span]
    right_flow = jnp.pad(centre_cells[:, 1:], ((0, 0), (0, 1))) * across
    left_flow = jnp.pad(centre_cells[:, :-1] * across[:, :-1], ((0, 0), (1, 0)))
    return vertical + right_flow + left_flow


def relax_sweep(padded, vertical_links, across, right_side, inverse_diag, previous, factors):
    centre_cells = padded[1:-1]
    residual = inverse_diag * (right_side + neighbours(padded, vertical_links, across)) - centre_cells
    if previous is None:
        update = factors[1] * residual
    else:
        update = factors[0] * previous + factors[1] * residual
    return centre_cells + update, update


def reference(class_index, class_conductance, loads, start_volts, via_cells, via_counts):
    row_total = ROWS * TILES
    cell_total = row_total * COLS
    slots = jnp.arange(TILES * VIAS_DEV, dtype=jnp.int32)
    strip_row = (slots // VIAS_DEV) * ROWS
    slot_col = slots % COLS
    weights = VIA_UNIT * via_counts.astype(jnp.float32)
    factors = chebyshev_terms(SWEEPS)
    col_ids = jax.lax.broadcasted_iota(jnp.int32, (row_total, COLS), 1)
    row_ids = jax.lax.broadcasted_iota(jnp.int32, (row_total, COLS), 0)
    global_cells = [(strip_row + via_cells[layer_index]) * COLS + slot_col for layer_index in range(LAYERS)]
    across_all, links_all, inverse_all = [], [], []
    for layer_index in range(LAYERS):
        conductance = lookup(class_index[layer_index], class_conductance[layer_index])
        across = jnp.where(col_ids < COLS - 1, conductance[0], jnp.float32(0.0))
        downward = jnp.where(row_ids < row_total - 1, conductance[1], jnp.float32(0.0))
        vertical_links = jnp.concatenate([jnp.zeros((1, COLS), jnp.float32), downward], axis=0)
        via_diag = jnp.zeros((cell_total,), jnp.float32).at[global_cells[layer_index]].add(weights[layer_index])
        if layer_index > 0:
            via_diag = via_diag.at[global_cells[layer_index - 1]].add(weights[layer_index - 1])
        diagonal = across + jnp.pad(across[:, :-1], ((0, 0), (1, 0))) + vertical_links[:-1] + vertical_links[1:] + via_diag.reshape(row_total, COLS)
        across_all.append(across)
        links_all.append(vertical_links)
        inverse_all.append(1.0 / diagonal)
    volts = [start_volts[layer_index] for layer_index in range(LAYERS)]
    for outer_index in range(OUTER):
        renewed = []
        for layer_index in range(LAYERS):
            if layer_index < LAYERS - 1:
                above = volts[layer_index + 1].reshape(-1)[global_cells[layer_index]]
            else:
                above = jnp.ones((TILES * VIAS_DEV,), jnp.float32)
            source = jnp.zeros((cell_total,), jnp.float32).at[global_cells[layer_index]].add(weights[layer_index] * above)
            if layer_index > 0:
                below = volts[layer_index - 1].reshape(-1)[global_cells[layer_index - 1]]
                source = source.at[global_cells[layer_index - 1]].add(weights[layer_index - 1] * below)
            right_side = source.reshape(row_total, COLS) - loads[layer_index]
            current = volts[layer_index]
            update = None
            for sweep_index in range(SWEEPS):
                padded = jnp.pad(current, ((1, 1), (0, 0)))
                current, update = relax_sweep(padded, links_all[layer_index], across_all[layer_index], right_side, inverse_all[layer_index], update, factors[sweep_index])
            renewed.append(current)
        volts = renewed
    return jnp.stack(volts)
```

```python
import functools

import jax
import jax.numpy as jnp
from jax import lax
from jax.experimental import pallas as pl
from jax.experimental.pallas import tpu as pltpu
from jax.sharding import PartitionSpec as P

OUTER = 2
SWEEPS = 3
VIA_UNIT = 2.0
LOWER_BOUND = 0.05
UPPER_BOUND = 2.0
LANES = 128


def chebyshev_terms(count):
    centre_value = 0.5 * (UPPER_BOUND + LOWER_BOUND)
    half_width = 0.5 * (UPPER_BOUND - LOWER_BOUND)
    sigma = centre_value / half_width
    rho_last = 1.0 / sigma
    terms = [(0.0, 1.0 / centre_value)]
    for index in range(1, count):
        rho_next = 1.0 / (2.0 * sigma - rho_last)
        terms.append((rho_next * rho_last, 2.0 * rho_next / half_width))
        rho_last = rho_next
    return terms


FACTORS = chebyshev_terms(SWEEPS)


def column_right(row):
    lane = lax.broadcasted_iota(jnp.int32, row.shape, 1)
    turned = pltpu.roll(row, LANES - 1, 1)
    return jnp.where(lane == LANES - 1, pltpu.roll(turned, row.shape[0] - 1, 0), turned)


def column_left(row):
    lane = lax.broadcasted_iota(jnp.int32, row.shape, 1)
    turned = pltpu.roll(row, 1, 1)
    return jnp.where(lane == 0, pltpu.roll(turned, 1, 0), turned)


def beside(x, across):
    return across * column_right(x) + column_left(across * x)


def place():
    return lax.axis_index("tile"), lax.axis_index("layer")


def marked(cells, row, value):
    return jnp.where(cells == row, value, 0.0)


def pick(x_ref, cells, rows):
    total = jnp.zeros(cells.shape, jnp.float32)
    for row in range(rows):
        total = total + marked(cells, row, x_ref[row])
    return total


def weight_of(counts):
    return VIA_UNIT * counts.astype(jnp.float32)


def unpack_kernel(index_ref, table_ref, loads_ref, volts_ref, across_ref, down_ref, loads_out, x_ref):
    rows, cols = loads_ref.shape
    lines = cols // LANES
    tile, _ = place()
    last_tile = tile == lax.axis_size("tile") - 1
    table = jnp.broadcast_to(table_ref[...], (8, LANES))
    lane = lax.broadcasted_iota(jnp.int32, (8, LANES), 1)
    sub = lax.broadcasted_iota(jnp.int32, (8, LANES), 0)
    for top in range(0, rows, 8):
        part = pl.ds(top, 8)
        for line in range(lines):
            here = pl.ds(line * LANES, LANES)
            across = jnp.take_along_axis(table, index_ref[0, part, here], axis=1, mode="promise_in_bounds")
            if line == lines - 1:
                across = jnp.where(lane == LANES - 1, 0.0, across)
            across_ref[part, line, :] = across
            down = jnp.take_along_axis(table, index_ref[1, part, here], axis=1, mode="promise_in_bounds")
            if top + 8 == rows:
                down = jnp.where((sub == 7) & last_tile, 0.0, down)
            down_ref[part, line, :] = down
            loads_out[part, line, :] = loads_ref[part, here]
            x_ref[part, line, :] = volts_ref[part, here]


def links_kernel(single, rows, x_ref, own_ref, count_ref, low_ref, *out_refs):
    _, layer = place()
    own, low = own_ref[...], low_ref[...]
    weight = weight_of(count_ref[...])
    if single:
        out_refs[0][0] = pick(x_ref, jnp.where(layer == 0, own, low), rows)
        out_refs[0][1] = weight
    else:
        out_refs[0][0] = pick(x_ref, own, rows)
        out_refs[0][1] = weight
        out_refs[1][0] = pick(x_ref, low, rows)


def via_terms(own_ref, count_ref, low_ref, low_weight, from_above, from_below):
    _, layer = place()
    on_top = layer == lax.axis_size("layer") - 1
    own_weight = weight_of(count_ref[...])
    low_weight = jnp.where(layer == 0, 0.0, low_weight)
    own_source = own_weight * jnp.where(on_top, 1.0, from_above)
    low_source = low_weight * from_below
    own, low = own_ref[...], low_ref[...]

    def via(row):
        return marked(own, row, own_weight) + marked(low, row, low_weight)

    def source(row):
        return marked(own, row, own_source) + marked(low, row, low_source)

    return via, source


def send_by_parity(first_ref, second_ref, slot, top, bottom):
    tile, _ = place()
    even = lax.rem(tile, 2) == 0
    first_ref[slot] = jnp.where(even, bottom, top)
    second_ref[slot] = jnp.where(even, top, bottom)


def taken_by_parity(first_ref, second_ref, slot):
    tile, _ = place()
    even = lax.rem(tile, 2) == 0
    first, second = first_ref[slot], second_ref[slot]
    return jnp.where(even, second, first), jnp.where(even, first, second)


def edge_one(x_ref, across_ref, down_ref, row, right_side, inverse):
    x = x_ref[row]
    flow = beside(x, across_ref[row]) + down_ref[row] * x_ref[row + 1] + down_ref[row - 1] * x_ref[row - 1]
    return x + FACTORS[0][1] * (inverse * (right_side + flow) - x)


def edges(x_ref, across_ref, down_ref, right_side, inverse_1, inverse_n, rows):
    top_side, bottom_side = right_side(0), right_side(rows - 1)
    below_top = down_ref[0]
    above_bottom = down_ref[rows - 2]
    top_1 = edge_one(x_ref, across_ref, down_ref, 1, right_side(1), inverse_1)
    bottom_1 = edge_one(x_ref, across_ref, down_ref, rows - 2, right_side(rows - 2), inverse_n)
    return (
        (x_ref[0], x_ref[rows - 1]),
        (top_side + below_top * x_ref[1], bottom_side + above_bottom * x_ref[rows - 2]),
        (top_side + below_top * top_1, bottom_side + above_bottom * bottom_1),
    )


def first_edges_kernel(
    rows, x_ref, across_ref, down_ref, loads_ref, own_ref, count_ref, low_ref, above_ref, below_ref, first_ref, second_ref
):
    via, source = via_terms(own_ref, count_ref, low_ref, below_ref[1], above_ref[0], below_ref[0])

    def right_side(row):
        return source(row) - loads_ref[row]

    def diagonal(row, links):
        across = across_ref[row]
        total = across + column_left(across)
        for link in links:
            total = total + down_ref[link]
        return total + via(row)

    values = edges(
        x_ref,
        across_ref,
        down_ref,
        right_side,
        1.0 / diagonal(1, (0, 1)),
        1.0 / diagonal(rows - 2, (rows - 3, rows - 2)),
        rows,
    )
    for slot, (top, bottom) in enumerate(values):
        send_by_parity(first_ref, second_ref, slot, top, bottom)
    send_by_parity(first_ref, second_ref, 3, diagonal(0, (0,)), diagonal(rows - 1, (rows - 2,)))
    send_by_parity(first_ref, second_ref, 4, across_ref[0], across_ref[rows - 1])
    send_by_parity(first_ref, second_ref, 5, down_ref[0], down_ref[rows - 1])


def next_edges_kernel(
    rows,
    x_ref,
    across_ref,
    down_ref,
    loads_ref,
    inverse_ref,
    own_ref,
    count_ref,
    low_ref,
    weight_ref,
    above_ref,
    below_ref,
    first_ref,
    second_ref,
):
    _, source = via_terms(own_ref, count_ref, low_ref, weight_ref[1], above_ref[0], below_ref[0])

    def right_side(row):
        return source(row) - loads_ref[row]

    values = edges(x_ref, across_ref, down_ref, right_side, inverse_ref[2], inverse_ref[rows - 1], rows)
    for slot, (top, bottom) in enumerate(values):
        send_by_parity(first_ref, second_ref, slot, top, bottom)


def step_body(x_ref, across_ref, down_ref, side_ref, inverse_ref, halo, even_ref, odd_ref, update_ref, write, rows):
    (top_x, top_q, top_across, link), (low_x, low_q, low_across) = halo
    low_link = down_ref[rows - 1]

    def fill(row, carry):
        even_ref[row + 1] = x_ref[row]
        return carry

    even_ref[0] = top_x
    even_ref[rows + 1] = low_x
    lax.fori_loop(0, rows, fill, 0)
    up_ref = down_ref
    buffers = [even_ref, odd_ref, even_ref, odd_ref]
    for sweep in range(SWEEPS):
        source, target = buffers[sweep], buffers[sweep + 1]
        keep, gain = FACTORS[sweep]
        last = sweep == SWEEPS - 1

        def relax(at, flow, side):
            x = source[at]
            update = gain * (inverse_ref[at] * (side + flow) - x)
            if sweep > 0:
                update = update + keep * update_ref[at]
            if not last:
                update_ref[at] = update
            return x + update

        if not last:
            flow = beside(source[0], top_across) + link * source[1]
            target[0] = relax(0, flow, top_q[sweep])
            flow = beside(source[rows + 1], low_across) + low_link * source[rows]
            target[rows + 1] = relax(rows + 1, flow, low_q[sweep])

        def one_row(row, above):
            flow = beside(source[row + 1], across_ref[row])
            flow = flow + down_ref[row] * source[row + 2] + above * source[row]
            value = relax(row + 1, flow, side_ref[row])
            if last:
                write(row, value)
            else:
                target[row + 1] = value

        one_row(0, link)

        def body(row, carry):
            one_row(row, up_ref[row - 1])
            return carry

        lax.fori_loop(1, rows, body, 0)


def first_step_kernel(
    single,
    rows,
    x_ref,
    across_ref,
    down_ref,
    loads_ref,
    own_ref,
    count_ref,
    low_ref,
    above_ref,
    below_ref,
    first_ref,
    second_ref,
    next_ref,
    inverse_ref,
    halo_ref,
    *rest,
):
    sends, (side_ref, even_ref, odd_ref, update_ref) = rest[:-4], rest[-4:]
    tile, layer = place()
    via, source = via_terms(own_ref, count_ref, low_ref, below_ref[1], above_ref[0], below_ref[0])
    top_x, low_x = taken_by_parity(first_ref, second_ref, 0)
    top_q0, low_q0 = taken_by_parity(first_ref, second_ref, 1)
    top_q1, low_q1 = taken_by_parity(first_ref, second_ref, 2)
    top_diag, low_diag = taken_by_parity(first_ref, second_ref, 3)
    top_across, low_across = taken_by_parity(first_ref, second_ref, 4)
    link, _ = taken_by_parity(first_ref, second_ref, 5)
    link = jnp.where(tile == 0, 0.0, link)
    halo_ref[0] = top_across
    halo_ref[1] = low_across
    halo_ref[2] = link
    inverse_ref[0] = 1.0 / (top_diag + link)
    inverse_ref[rows + 1] = 1.0 / (low_diag + down_ref[rows - 1])

    def setup(row, above):
        across = across_ref[row]
        diagonal = across + column_left(across) + down_ref[row] + above + via(row)
        inverse_ref[row + 1] = 1.0 / diagonal
        side_ref[row] = source(row) - loads_ref[row]

    setup(0, link)

    def body(row, carry):
        setup(row, down_ref[row - 1])
        return carry

    lax.fori_loop(1, rows, body, 0)

    def write(row, value):
        next_ref[row] = value

    halo = (top_x, (top_q0, top_q1), top_across, link), (low_x, (low_q0, low_q1), low_across)
    step_body(x_ref, across_ref, down_ref, side_ref, inverse_ref, halo, even_ref, odd_ref, update_ref, write, rows)
    own, low = own_ref[...], low_ref[...]
    if single:
        sends[0][0] = pick(next_ref, jnp.where(layer == 0, own, low), rows)
    else:
        sends[0][0] = pick(next_ref, own, rows)
        sends[1][0] = pick(next_ref, low, rows)


def last_step_kernel(
    rows,
    x_ref,
    across_ref,
    down_ref,
    loads_ref,
    inverse_ref,
    halo_ref,
    own_ref,
    count_ref,
    low_ref,
    weight_ref,
    above_ref,
    below_ref,
    first_ref,
    second_ref,
    out_ref,
    side_ref,
    even_ref,
    odd_ref,
    update_ref,
    last_ref,
):
    _, source = via_terms(own_ref, count_ref, low_ref, weight_ref[1], above_ref[0], below_ref[0])
    top_x, low_x = taken_by_parity(first_ref, second_ref, 0)
    top_q0, low_q0 = taken_by_parity(first_ref, second_ref, 1)
    top_q1, low_q1 = taken_by_parity(first_ref, second_ref, 2)

    def body(row, carry):
        side_ref[row] = source(row) - loads_ref[row]
        return carry

    lax.fori_loop(0, rows, body, 0)

    def write(row, value):
        last_ref[row] = value

    halo = (top_x, (top_q0, top_q1), halo_ref[0], halo_ref[2]), (low_x, (low_q0, low_q1), halo_ref[1])
    step_body(x_ref, across_ref, down_ref, side_ref, inverse_ref, halo, even_ref, odd_ref, update_ref, write, rows)
    for top in range(0, rows, 8):
        for line in range(out_ref.shape[1] // LANES):
            out_ref[pl.ds(top, 8), pl.ds(line * LANES, LANES)] = last_ref[pl.ds(top, 8), line, :]


def call(kernel, name, outs, scratch, *args):
    spec = pl.BlockSpec(memory_space=pltpu.VMEM)
    return pl.pallas_call(
        kernel,
        out_shape=[jax.ShapeDtypeStruct(shape, jnp.float32) for shape in outs],
        in_specs=[spec] * len(args),
        out_specs=[spec] * len(outs),
        scratch_shapes=[pltpu.VMEM(shape, jnp.float32) for shape in scratch],
        compiler_params=pltpu.CompilerParams(vmem_limit_bytes=40 * 1024 * 1024),
        name=name,
    )(*args)


def routes(tiles, layers):
    def at(tile, layer):
        return tile * layers + layer % layers

    everywhere = [(tile, layer) for tile in range(tiles) for layer in range(layers)]
    up = [(at(t, l), at(t, l + 1)) for t, l in everywhere]
    down = [(at(t, l), at(t, l - 1)) for t, l in everywhere]
    first, second = [], []
    for t, l in everywhere:
        first.append((at(t, l), at(t ^ 1, l)))
        beyond = t + 1 if t % 2 else t - 1
        if 0 <= beyond < tiles:
            second.append((at(t, l), at(beyond, l)))
        else:
            second.append((at(t, l), at(t, l + 1)))
    return up, down, first, second


def local(class_index, class_conductance, loads, start_volts, via_cells, via_counts):
    rows, cols = loads.shape[1:]
    lines = cols // LANES
    tiles, layers = lax.axis_size("tile"), lax.axis_size("layer")
    up, down, first, second = routes(tiles, layers)
    single = layers == 2
    move = functools.partial(lax.ppermute, axis_name=("tile", "layer"))
    field = (rows, lines, LANES)
    padded = (rows + 2, lines, LANES)

    def rows_of(count):
        return (count, lines, LANES)

    def between_layers(sends):
        if single:
            got = move(sends[0], perm=up)
            return got, got
        return move(sends[1], perm=down), move(sends[0], perm=up)

    own = via_cells.reshape(lines, LANES)
    counts = via_counts.reshape(lines, LANES)
    low = move(own, perm=up)
    table = jnp.pad(class_conductance, ((0, 0), (0, LANES - class_conductance.shape[1])))
    across, downward, load, x = call(
        unpack_kernel, "unpack", [field] * 4, [], class_index[0], table, loads[0], start_volts[0]
    )
    sends = call(
        functools.partial(links_kernel, single, rows),
        "links",
        [rows_of(2)] if single else [rows_of(2), rows_of(1)],
        [],
        x,
        own,
        counts,
        low,
    )
    above, below = between_layers(sends)
    weights = below
    sent = call(
        functools.partial(first_edges_kernel, rows),
        "first_edges",
        [rows_of(6)] * 2,
        [],
        *(x, across, downward, load, own, counts, low, above, below),
    )
    got = [move(sent[0], perm=first), move(sent[1], perm=second)]
    x, inverse, halo, *sends = call(
        functools.partial(first_step_kernel, single, rows),
        "first_step",
        [field, padded, rows_of(3)] + ([rows_of(1)] if single else [rows_of(1)] * 2),
        [field, padded, padded, padded],
        *(x, across, downward, load, own, counts, low, above, below, *got),
    )
    above, below = between_layers(sends)
    sent = call(
        functools.partial(next_edges_kernel, rows),
        "next_edges",
        [rows_of(3)] * 2,
        [],
        *(x, across, downward, load, inverse, own, counts, low, weights, above, below),
    )
    got = [move(sent[0], perm=first), move(sent[1], perm=second)]
    (volts,) = call(
        functools.partial(last_step_kernel, rows),
        "last_step",
        [(rows, cols)],
        [field, padded, padded, padded, field],
        *(x, across, downward, load, inverse, halo, own, counts, low, weights, above, below, *got),
    )
    return volts[None]


def solution(mesh):
    placed = (
        P("layer", None, "tile", None),
        P("layer", None),
        P("layer", "tile", None),
        P("layer", "tile", None),
        P("layer", "tile"),
        P("layer", "tile"),
    )
    return jax.shard_map(
        local, mesh=mesh, in_specs=placed, out_specs=P("layer", "tile", None), check_vma=False
    )
```

```python
import functools

import jax
import jax.numpy as jnp
from jax import lax
from jax.experimental import pallas as pl
from jax.experimental.pallas import tpu as pltpu
from jax.sharding import PartitionSpec as P

OUTER = 2
SWEEPS = 3
VIA_UNIT = 2.0
LOWER_BOUND = 0.05
UPPER_BOUND = 2.0
LANES = 128


def chebyshev_terms(count):
    centre_value = 0.5 * (UPPER_BOUND + LOWER_BOUND)
    half_width = 0.5 * (UPPER_BOUND - LOWER_BOUND)
    sigma = centre_value / half_width
    rho_last = 1.0 / sigma
    terms = [(0.0, 1.0 / centre_value)]
    for index in range(1, count):
        rho_next = 1.0 / (2.0 * sigma - rho_last)
        terms.append((rho_next * rho_last, 2.0 * rho_next / half_width))
        rho_last = rho_next
    return terms


FACTORS = chebyshev_terms(SWEEPS)


def column_right(row):
    lane = lax.broadcasted_iota(jnp.int32, row.shape, 1)
    turned = pltpu.roll(row, LANES - 1, 1)
    return jnp.where(lane == LANES - 1, pltpu.roll(turned, row.shape[0] - 1, 0), turned)


def column_left(row):
    lane = lax.broadcasted_iota(jnp.int32, row.shape, 1)
    turned = pltpu.roll(row, 1, 1)
    return jnp.where(lane == 0, pltpu.roll(turned, 1, 0), turned)


def beside(x, across):
    return across * column_right(x) + column_left(across * x)


def place():
    return lax.axis_index("tile"), lax.axis_index("layer")


def marked(cells, row, value):
    return jnp.where(cells == row, value, 0.0)


def pick(x_ref, cells, rows):
    total = jnp.zeros(cells.shape, jnp.float32)
    for row in range(rows):
        total = total + marked(cells, row, x_ref[row])
    return total


def weight_of(counts):
    return VIA_UNIT * counts.astype(jnp.float32)


def copies(pairs, sems):
    made = []
    for index, (source, target) in enumerate(pairs):
        copy = pltpu.make_async_copy(source, target, sems.at[index])
        copy.start()
        made.append(copy)
    return made


def chunks_of(cols, count):
    width = cols // count
    return [(first, width) for first in range(0, cols, width)]


def unpack_volts_kernel(count, volts_ref, x_ref, held, sems):
    rows, cols = held.shape
    chunks = chunks_of(cols, count)
    arriving = copies([(volts_ref.at[0, :, pl.ds(*c)], held.at[:, pl.ds(*c)]) for c in chunks], sems)
    for (first, width), copy in zip(chunks, arriving):
        copy.wait()
        for top in range(0, rows, 8):
            for start in range(first, first + width, LANES):
                x_ref[pl.ds(top, 8), start // LANES, :] = held[pl.ds(top, 8), pl.ds(start, LANES)]


def unpack_kernel(
    count, index_ref, table_ref, loads_ref, after_ref, across_ref, down_ref, loads_out, index_held, loads_held, sems
):
    rows, cols = loads_held.shape
    tile, _ = place()
    last_tile = tile == lax.axis_size("tile") - 1
    chunks = chunks_of(cols, count)
    pairs = []
    for c in chunks:
        pairs.append((index_ref.at[0, :, :, pl.ds(*c)], index_held.at[:, :, pl.ds(*c)]))
        pairs.append((loads_ref.at[0, :, pl.ds(*c)], loads_held.at[:, pl.ds(*c)]))
    arriving = copies(pairs, sems)
    table = jnp.broadcast_to(table_ref[...], (8, LANES))
    lane = lax.broadcasted_iota(jnp.int32, (8, LANES), 1)
    sub = lax.broadcasted_iota(jnp.int32, (8, LANES), 0)
    for number, (first, width) in enumerate(chunks):
        arriving[2 * number].wait()
        arriving[2 * number + 1].wait()
        for top in range(0, rows, 8):
            part = pl.ds(top, 8)
            for start in range(first, first + width, LANES):
                here, line = pl.ds(start, LANES), start // LANES
                across = jnp.take_along_axis(table, index_held[0, part, here], axis=1, mode="promise_in_bounds")
                if start + LANES == cols:
                    across = jnp.where(lane == LANES - 1, 0.0, across)
                across_ref[part, line, :] = across
                down = jnp.take_along_axis(table, index_held[1, part, here], axis=1, mode="promise_in_bounds")
                if top + 8 == rows:
                    down = jnp.where((sub == 7) & last_tile, 0.0, down)
                down_ref[part, line, :] = down
                loads_out[part, line, :] = loads_held[part, here]


def links_kernel(single, rows, x_ref, own_ref, count_ref, low_ref, *out_refs):
    for out_ref, cells in zip(out_refs, chosen(single, own_ref[...], low_ref[...])):
        out_ref[0] = pick(x_ref, cells, rows)
    out_refs[0][1] = weight_of(count_ref[...])


def via_terms(own_ref, count_ref, low_ref, low_weight, from_above, from_below):
    _, layer = place()
    on_top = layer == lax.axis_size("layer") - 1
    own_weight = weight_of(count_ref[...])
    low_weight = jnp.where(layer == 0, 0.0, low_weight)
    own_source = own_weight * jnp.where(on_top, 1.0, from_above)
    low_source = low_weight * from_below
    own, low = own_ref[...], low_ref[...]

    def via(row):
        return marked(own, row, own_weight) + marked(low, row, low_weight)

    def source(row):
        return marked(own, row, own_source) + marked(low, row, low_source)

    return via, source


def send_by_parity(first_ref, second_ref, slot, top, bottom):
    tile, _ = place()
    even = lax.rem(tile, 2) == 0
    first_ref[slot] = jnp.where(even, bottom, top)
    second_ref[slot] = jnp.where(even, top, bottom)


def taken_by_parity(first_ref, second_ref, slot):
    tile, _ = place()
    even = lax.rem(tile, 2) == 0
    first, second = first_ref[slot], second_ref[slot]
    return jnp.where(even, second, first), jnp.where(even, first, second)


def edge_one(x_ref, across_ref, down_ref, row, right_side, inverse):
    x = x_ref[row]
    flow = beside(x, across_ref[row]) + down_ref[row] * x_ref[row + 1] + down_ref[row - 1] * x_ref[row - 1]
    return x + FACTORS[0][1] * (inverse * (right_side + flow) - x)


def edges(x_ref, across_ref, down_ref, right_side, inverse_1, inverse_n, rows):
    top_side, bottom_side = right_side(0), right_side(rows - 1)
    below_top = down_ref[0]
    above_bottom = down_ref[rows - 2]
    top_1 = edge_one(x_ref, across_ref, down_ref, 1, right_side(1), inverse_1)
    bottom_1 = edge_one(x_ref, across_ref, down_ref, rows - 2, right_side(rows - 2), inverse_n)
    return (
        (x_ref[0], x_ref[rows - 1]),
        (top_side + below_top * x_ref[1], bottom_side + above_bottom * x_ref[rows - 2]),
        (top_side + below_top * top_1, bottom_side + above_bottom * bottom_1),
    )


def first_edges_kernel(
    rows, x_ref, across_ref, down_ref, loads_ref, own_ref, count_ref, low_ref, above_ref, below_ref, first_ref, second_ref
):
    via, source = via_terms(own_ref, count_ref, low_ref, below_ref[1], above_ref[0], below_ref[0])

    def right_side(row):
        return source(row) - loads_ref[row]

    def diagonal(row, links):
        across = across_ref[row]
        total = across + column_left(across)
        for link in links:
            total = total + down_ref[link]
        return total + via(row)

    values = edges(
        x_ref,
        across_ref,
        down_ref,
        right_side,
        1.0 / diagonal(1, (0, 1)),
        1.0 / diagonal(rows - 2, (rows - 3, rows - 2)),
        rows,
    )
    for slot, (top, bottom) in enumerate(values):
        send_by_parity(first_ref, second_ref, slot, top, bottom)
    send_by_parity(first_ref, second_ref, 3, diagonal(0, (0,)), diagonal(rows - 1, (rows - 2,)))
    send_by_parity(first_ref, second_ref, 4, across_ref[0], across_ref[rows - 1])
    send_by_parity(first_ref, second_ref, 5, down_ref[0], down_ref[rows - 1])


def next_edges_kernel(
    rows,
    x_ref,
    across_ref,
    down_ref,
    loads_ref,
    inverse_ref,
    own_ref,
    count_ref,
    low_ref,
    weight_ref,
    above_ref,
    below_ref,
    first_ref,
    second_ref,
):
    _, source = via_terms(own_ref, count_ref, low_ref, weight_ref[1], above_ref[0], below_ref[0])

    def right_side(row):
        return source(row) - loads_ref[row]

    values = edges(x_ref, across_ref, down_ref, right_side, inverse_ref[1], inverse_ref[rows - 2], rows)
    for slot, (top, bottom) in enumerate(values):
        send_by_parity(first_ref, second_ref, slot, top, bottom)


def relaxed(x, flow, side, inverse, previous, sweep):
    keep, gain = FACTORS[sweep]
    update = gain * (inverse * (side + flow) - x)
    if sweep > 0:
        update = update + keep * previous
    return x + update, update


def chosen(single, own, low):
    _, layer = place()
    return [jnp.where(layer == 0, own, low)] if single else [own, low]


def inner_rows(rows, x_ref, across_ref, down_ref, side_ref, inverse_ref, work, update_ref, core_ref, keep_ref):
    sources = [x_ref, *work]
    targets = [*work, core_ref]
    for sweep in range(SWEEPS):
        source, target = sources[sweep], targets[sweep]
        for row in range(sweep + 1, rows - 1 - sweep):
            x = source[row]
            flow = beside(x, across_ref[row]) + down_ref[row] * source[row + 1] + down_ref[row - 1] * source[row - 1]
            previous = update_ref[row] if sweep > 0 else None
            value, update = relaxed(x, flow, side_ref[row], inverse_ref[row], previous, sweep)
            target[row] = value
            if sweep < SWEEPS - 1:
                update_ref[row] = update
                for side, depth in ((0, row), (1, rows - 1 - row)):
                    slot = 3 * (2 * sweep + side)
                    if depth == sweep + 1:
                        keep_ref[slot] = value
                        keep_ref[slot + 2] = update
                    if depth == sweep + 2:
                        keep_ref[slot + 1] = value


def outer_rows(side, rows, halo, link, inverse_edge, x_ref, across_ref, down_ref, side_ref, inverse, keep_ref):
    edge_x, edge_q, edge_across = halo

    def row_of(depth):
        return depth if side == 0 else rows - 1 - depth

    def link_out(depth):
        if depth == 0:
            return link
        return down_ref[depth - 1] if side == 0 else down_ref[rows - 1 - depth]

    def link_in(depth):
        return down_ref[depth] if side == 0 else down_ref[rows - 2 - depth]

    values = {-1: edge_x}
    updates = {}
    for depth in range(SWEEPS + 1):
        values[depth] = x_ref[row_of(depth)]
    for sweep in range(SWEEPS):
        found, changed = {}, {}
        if sweep < SWEEPS - 1:
            flow = beside(edge_value := values[-1], edge_across) + link * values[0]
            found[-1], changed[-1] = relaxed(
                edge_value, flow, edge_q[sweep], inverse_edge, updates.get(-1), sweep
            )
        for depth in range(sweep + 1):
            row = row_of(depth)
            x = values[depth]
            flow = beside(x, across_ref[row]) + link_out(depth) * values[depth - 1] + link_in(depth) * values[depth + 1]
            found[depth], changed[depth] = relaxed(
                x, flow, side_ref[row], inverse(row), updates.get(depth), sweep
            )
        if sweep < SWEEPS - 1:
            slot = 3 * (2 * sweep + side)
            found[sweep + 1] = keep_ref[slot]
            changed[sweep + 1] = keep_ref[slot + 2]
            found[sweep + 2] = keep_ref[slot + 1]
        values, updates = found, changed
    return {row_of(depth): value for depth, value in values.items()}


KEPT = 6 * (SWEEPS - 1)


def first_inner_kernel(
    single,
    rows,
    x_ref,
    across_ref,
    down_ref,
    loads_ref,
    own_ref,
    count_ref,
    low_ref,
    above_ref,
    below_ref,
    after_ref,
    core_ref,
    side_ref,
    inverse_ref,
    keep_ref,
    picked_ref,
    *scratch,
):
    via, source = via_terms(own_ref, count_ref, low_ref, below_ref[1], above_ref[0], below_ref[0])
    for row in range(rows):
        side_ref[row] = source(row) - loads_ref[row]
        across = across_ref[row]
        diagonal = across + column_left(across) + down_ref[row] + via(row)
        if row > 0:
            diagonal = diagonal + down_ref[row - 1]
            inverse_ref[row] = 1.0 / diagonal
        else:
            inverse_ref[row] = diagonal
    inner_rows(
        rows, x_ref, across_ref, down_ref, side_ref, inverse_ref, scratch[:-1], scratch[-1], core_ref, keep_ref
    )
    for index, cells in enumerate(chosen(single, own_ref[...], low_ref[...])):
        total = jnp.zeros(cells.shape, jnp.float32)
        for row in range(SWEEPS, rows - SWEEPS):
            total = total + marked(cells, row, core_ref[row])
        picked_ref[index] = total


def first_outer_kernel(
    single,
    rows,
    x_ref,
    across_ref,
    down_ref,
    side_ref,
    inverse_ref,
    keep_ref,
    picked_ref,
    own_ref,
    low_ref,
    first_ref,
    second_ref,
    core_ref,
    next_ref,
    halo_ref,
    *sends,
):
    tile, _ = place()
    top_x, low_x = taken_by_parity(first_ref, second_ref, 0)
    top_q0, low_q0 = taken_by_parity(first_ref, second_ref, 1)
    top_q1, low_q1 = taken_by_parity(first_ref, second_ref, 2)
    top_diag, low_diag = taken_by_parity(first_ref, second_ref, 3)
    top_across, low_across = taken_by_parity(first_ref, second_ref, 4)
    link, _ = taken_by_parity(first_ref, second_ref, 5)
    link = jnp.where(tile == 0, 0.0, link)
    low_link = down_ref[rows - 1]
    top_inverse = 1.0 / (top_diag + link)
    low_inverse = 1.0 / (low_diag + low_link)
    inverse_0 = 1.0 / (inverse_ref[0] + link)
    for slot, value in enumerate((top_across, low_across, link, top_inverse, low_inverse, inverse_0)):
        halo_ref[slot] = value

    def inverse(row):
        return inverse_0 if row == 0 else inverse_ref[row]

    shared = (x_ref, across_ref, down_ref, side_ref, inverse, keep_ref)
    outer = outer_rows(0, rows, (top_x, (top_q0, top_q1), top_across), link, top_inverse, *shared)
    outer.update(
        outer_rows(1, rows, (low_x, (low_q0, low_q1), low_across), low_link, low_inverse, *shared)
    )
    for row, value in outer.items():
        next_ref[row] = value
    for index, cells in enumerate(chosen(single, own_ref[...], low_ref[...])):
        total = picked_ref[index]
        for row, value in outer.items():
            total = total + marked(cells, row, value)
        sends[index][0] = total


def last_inner_kernel(
    rows,
    x_ref,
    across_ref,
    down_ref,
    loads_ref,
    inverse_ref,
    own_ref,
    count_ref,
    low_ref,
    weight_ref,
    above_ref,
    below_ref,
    after_ref,
    core_ref,
    side_ref,
    keep_ref,
    *scratch,
):
    _, source = via_terms(own_ref, count_ref, low_ref, weight_ref[1], above_ref[0], below_ref[0])
    for row in range(rows):
        side_ref[row] = source(row) - loads_ref[row]
    inner_rows(
        rows, x_ref, across_ref, down_ref, side_ref, inverse_ref, scratch[:-1], scratch[-1], core_ref, keep_ref
    )


def last_outer_kernel(
    count,
    rows,
    x_ref,
    across_ref,
    down_ref,
    side_ref,
    inverse_ref,
    keep_ref,
    halo_ref,
    first_ref,
    second_ref,
    core_ref,
    out_ref,
    next_ref,
    held,
    sems,
):
    top_x, low_x = taken_by_parity(first_ref, second_ref, 0)
    top_q0, low_q0 = taken_by_parity(first_ref, second_ref, 1)
    top_q1, low_q1 = taken_by_parity(first_ref, second_ref, 2)

    def inverse(row):
        return halo_ref[5] if row == 0 else inverse_ref[row]

    shared = (x_ref, across_ref, down_ref, side_ref, inverse, keep_ref)
    outer = outer_rows(0, rows, (top_x, (top_q0, top_q1), halo_ref[0]), halo_ref[2], halo_ref[3], *shared)
    outer.update(
        outer_rows(1, rows, (low_x, (low_q0, low_q1), halo_ref[1]), down_ref[rows - 1], halo_ref[4], *shared)
    )
    for row, value in outer.items():
        next_ref[row] = value
    leaving = []
    for number, (first, width) in enumerate(chunks_of(held.shape[1], count)):
        for top in range(0, rows, 8):
            for start in range(first, first + width, LANES):
                held[pl.ds(top, 8), pl.ds(start, LANES)] = next_ref[pl.ds(top, 8), start // LANES, :]
        part = pl.ds(first, width)
        copy = pltpu.make_async_copy(held.at[:, part], out_ref.at[:, part], sems.at[number])
        copy.start()
        leaving.append(copy)
    for copy in leaving:
        copy.wait()


def call(kernel, name, ins, outs, scratch=(), aliases=None):
    spaces = {"vmem": pltpu.VMEM, "hbm": pltpu.HBM, "any": pl.ANY}
    return pl.pallas_call(
        kernel,
        out_shape=[jax.ShapeDtypeStruct(shape, jnp.float32) for _, shape in outs],
        in_specs=[pl.BlockSpec(memory_space=spaces[space]) for space, _ in ins],
        out_specs=[pl.BlockSpec(memory_space=spaces[space]) for space, _ in outs],
        scratch_shapes=list(scratch),
        input_output_aliases=aliases or {},
        compiler_params=pltpu.CompilerParams(vmem_limit_bytes=40 * 1024 * 1024),
        name=name,
    )(*(array for _, array in ins))


def routes(tiles, layers):
    def at(tile, layer):
        return tile * layers + layer % layers

    everywhere = [(tile, layer) for tile in range(tiles) for layer in range(layers)]
    up = [(at(t, l), at(t, l + 1)) for t, l in everywhere]
    down = [(at(t, l), at(t, l - 1)) for t, l in everywhere]
    first, second = [], []
    for t, l in everywhere:
        first.append((at(t, l), at(t ^ 1, l)))
        beyond = t + 1 if t % 2 else t - 1
        if 0 <= beyond < tiles:
            second.append((at(t, l), at(beyond, l)))
        else:
            second.append((at(t, l), at(t, l + 1)))
    return up, down, first, second


CHUNKS = 4


def local(class_index, class_conductance, loads, start_volts, via_cells, via_counts):
    rows, cols = loads.shape[1:]
    lines = cols // LANES
    tiles, layers = lax.axis_size("tile"), lax.axis_size("layer")
    up, down, first, second = routes(tiles, layers)
    single = layers == 2
    move = functools.partial(lax.ppermute, axis_name=("tile", "layer"))

    def rows_of(count):
        return (count, lines, LANES)

    def held(shape, kind=jnp.float32):
        return pltpu.VMEM(shape, kind)

    def flags(count):
        return pltpu.SemaphoreType.DMA((count,))

    def vmem(*arrays):
        return [("vmem", array) for array in arrays]

    def between_layers(sends):
        if single:
            got = move(sends[0], perm=up)
            return got, got
        return move(sends[1], perm=down), move(sends[0], perm=up)

    def beside_tile(sent):
        return move(sent[0], perm=first), move(sent[1], perm=second)

    field = ("vmem", rows_of(rows))
    work = [held(rows_of(rows))] * SWEEPS
    pick_count = 1 if single else 2
    picks = [("vmem", rows_of(1))] * pick_count

    own = via_cells.reshape(lines, LANES)
    counts = via_counts.reshape(lines, LANES)
    low = move(own, perm=up)
    table = jnp.pad(class_conductance, ((0, 0), (0, LANES - class_conductance.shape[1])))
    (x,) = call(
        functools.partial(unpack_volts_kernel, CHUNKS),
        "unpack_volts",
        [("hbm", start_volts)],
        [field],
        [held((rows, cols)), flags(CHUNKS)],
    )
    sends = call(
        functools.partial(links_kernel, single, rows),
        "links",
        vmem(x, own, counts, low),
        [("vmem", rows_of(2))] if single else [("vmem", rows_of(2)), ("vmem", rows_of(1))],
    )
    above, below = between_layers(sends)
    weights = below
    across, downward, load = call(
        functools.partial(unpack_kernel, CHUNKS),
        "unpack",
        [("hbm", class_index), ("vmem", table), ("hbm", loads), ("any", sends[0])],
        [field] * 3,
        [held((2, rows, cols), jnp.int32), held((rows, cols)), flags(2 * CHUNKS)],
    )
    vias = (own, counts, low)
    sent = call(
        functools.partial(first_edges_kernel, rows),
        "first_edges",
        vmem(x, across, downward, load, *vias, above, below),
        [("vmem", rows_of(6))] * 2,
    )
    got = beside_tile(sent)
    core, side, inverse, keep, picked = call(
        functools.partial(first_inner_kernel, single, rows),
        "first_inner",
        vmem(x, across, downward, load, *vias, above, below) + [("any", sent[1])],
        [field, field, field, ("vmem", rows_of(KEPT)), ("vmem", rows_of(pick_count))],
        work,
    )
    x, halo, *sends = call(
        functools.partial(first_outer_kernel, single, rows),
        "first_outer",
        vmem(x, across, downward, side, inverse, keep, picked, own, low, *got, core),
        [field, ("vmem", rows_of(6))] + picks,
        aliases={11: 0},
    )
    above, below = between_layers(sends)
    sent = call(
        functools.partial(next_edges_kernel, rows),
        "next_edges",
        vmem(x, across, downward, load, inverse, *vias, weights, above, below),
        [("vmem", rows_of(3))] * 2,
    )
    got = beside_tile(sent)
    core, side, keep = call(
        functools.partial(last_inner_kernel, rows),
        "last_inner",
        vmem(x, across, downward, load, inverse, *vias, weights, above, below) + [("any", sent[1])],
        [field, field, ("vmem", rows_of(KEPT))],
        work,
    )
    volts, _ = call(
        functools.partial(last_outer_kernel, CHUNKS, rows),
        "last_outer",
        vmem(x, across, downward, side, inverse, keep, halo, *got, core),
        [("hbm", (rows, cols)), field],
        [held((rows, cols)), flags(CHUNKS)],
        aliases={9: 1},
    )
    return volts[None]


def solution(mesh):
    placed = (
        P("layer", None, "tile", None),
        P("layer", None),
        P("layer", "tile", None),
        P("layer", "tile", None),
        P("layer", "tile"),
        P("layer", "tile"),
    )
    return jax.shard_map(
        local, mesh=mesh, in_specs=placed, out_specs=P("layer", "tile", None), check_vma=False
    )
```

```python
import functools

import jax
import jax.numpy as jnp
from jax import lax
from jax.experimental import pallas as pl
from jax.experimental.pallas import tpu as pltpu
from jax.sharding import PartitionSpec as P

OUTER = 2
SWEEPS = 3
VIA_UNIT = 2.0
LOWER_BOUND = 0.05
UPPER_BOUND = 2.0
LANES = 128
CHUNKS = 2


def chebyshev_terms(count):
    centre_value = 0.5 * (UPPER_BOUND + LOWER_BOUND)
    half_width = 0.5 * (UPPER_BOUND - LOWER_BOUND)
    sigma = centre_value / half_width
    rho_last = 1.0 / sigma
    terms = [(0.0, 1.0 / centre_value)]
    for index in range(1, count):
        rho_next = 1.0 / (2.0 * sigma - rho_last)
        terms.append((rho_next * rho_last, 2.0 * rho_next / half_width))
        rho_last = rho_next
    return terms


FACTORS = chebyshev_terms(SWEEPS)


def column_right(row):
    lane = lax.broadcasted_iota(jnp.int32, row.shape, 1)
    turned = pltpu.roll(row, LANES - 1, 1)
    return jnp.where(lane == LANES - 1, pltpu.roll(turned, row.shape[0] - 1, 0), turned)


def column_left(row):
    lane = lax.broadcasted_iota(jnp.int32, row.shape, 1)
    turned = pltpu.roll(row, 1, 1)
    return jnp.where(lane == 0, pltpu.roll(turned, 1, 0), turned)


def beside(x, across):
    return across * column_right(x) + column_left(across * x)


def place():
    return lax.axis_index("tile"), lax.axis_index("layer")


def marked(cells, row, value):
    return jnp.where(cells == row, value, 0.0)


def pick(x_ref, cells, rows):
    total = jnp.zeros(cells.shape, jnp.float32)
    for row in range(rows):
        total = total + marked(cells, row, x_ref[row])
    return total


def weight_of(counts):
    return VIA_UNIT * counts.astype(jnp.float32)


def chunks_of(cols, count):
    width = cols // count
    return [(first, width) for first in range(0, cols, width)]


def unpack_volts_kernel(volts_ref, x_ref):
    rows, cols = volts_ref.shape[1:]
    for top in range(0, rows, 8):
        for start in range(0, cols, LANES):
            x_ref[pl.ds(top, 8), start // LANES, :] = volts_ref[0, pl.ds(top, 8), pl.ds(start, LANES)]


def unpack_kernel(index_ref, table_ref, loads_ref, across_ref, down_ref, loads_out):
    rows, cols = loads_ref.shape[1:]
    tile, _ = place()
    last_tile = tile == lax.axis_size("tile") - 1
    table = jnp.broadcast_to(table_ref[...], (8, LANES))
    lane = lax.broadcasted_iota(jnp.int32, (8, LANES), 1)
    sub = lax.broadcasted_iota(jnp.int32, (8, LANES), 0)
    for top in range(0, rows, 8):
        part = pl.ds(top, 8)
        for start in range(0, cols, LANES):
            here, line = pl.ds(start, LANES), start // LANES
            across = jnp.take_along_axis(table, index_ref[0, 0, part, here], axis=1, mode="promise_in_bounds")
            if start + LANES == cols:
                across = jnp.where(lane == LANES - 1, 0.0, across)
            across_ref[part, line, :] = across
            down = jnp.take_along_axis(table, index_ref[0, 1, part, here], axis=1, mode="promise_in_bounds")
            if top + 8 == rows:
                down = jnp.where((sub == 7) & last_tile, 0.0, down)
            down_ref[part, line, :] = down
            loads_out[part, line, :] = loads_ref[0, part, here]


def links_kernel(single, rows, x_ref, own_ref, count_ref, low_ref, *out_refs):
    for out_ref, cells in zip(out_refs, chosen(single, own_ref[...], low_ref[...])):
        out_ref[0] = pick(x_ref, cells, rows)
    out_refs[0][1] = weight_of(count_ref[...])


def via_terms(own_ref, count_ref, low_ref, low_weight, from_above, from_below):
    _, layer = place()
    on_top = layer == lax.axis_size("layer") - 1
    own_weight = weight_of(count_ref[...])
    low_weight = jnp.where(layer == 0, 0.0, low_weight)
    fixed_source = jnp.where(on_top, own_weight, 0.0)
    own, low = own_ref[...], low_ref[...]

    def via(row):
        return marked(own, row, own_weight) + marked(low, row, low_weight)

    def fixed(row):
        return marked(own, row, fixed_source)

    if from_above is None:
        return via, fixed, None
    own_source = jnp.where(on_top, 0.0, own_weight * from_above)
    low_source = low_weight * from_below

    def moving(row):
        return marked(own, row, own_source) + marked(low, row, low_source)

    return via, fixed, moving


def send_by_parity(first_ref, second_ref, slot, top, bottom):
    tile, _ = place()
    even = lax.rem(tile, 2) == 0
    first_ref[slot] = jnp.where(even, bottom, top)
    second_ref[slot] = jnp.where(even, top, bottom)


def taken_by_parity(first_ref, second_ref, slot):
    tile, _ = place()
    even = lax.rem(tile, 2) == 0
    first, second = first_ref[slot], second_ref[slot]
    return jnp.where(even, second, first), jnp.where(even, first, second)


def edge_flow(x_ref, across_ref, down_ref, row):
    return beside(x_ref[row], across_ref[row]) + down_ref[row] * x_ref[row + 1] + down_ref[row - 1] * x_ref[row - 1]


def edge_ends(rows):
    return (0, 1, 0), (rows - 1, rows - 2, rows - 2)


def edges(x_ref, across_ref, down_ref, right_side, inverses, rows):
    found = []
    for (edge, within, link), inverse in zip(edge_ends(rows), inverses):
        x = x_ref[within]
        flow = edge_flow(x_ref, across_ref, down_ref, within)
        later = x + FACTORS[0][1] * (inverse * (right_side(within) + flow) - x)
        found.append((right_side(edge) + down_ref[link] * x, right_side(edge) + down_ref[link] * later))
    return tuple(zip(*found))


def still_edges_kernel(x_ref, across_ref, down_ref, after_ref, first_ref, second_ref):
    rows = x_ref.shape[0]
    for slot, ref in enumerate((x_ref, across_ref, down_ref)):
        send_by_parity(first_ref, second_ref, slot, ref[0], ref[rows - 1])


def first_edges_kernel(
    rows, x_ref, across_ref, down_ref, loads_ref, own_ref, count_ref, low_ref, above_ref, below_ref, first_ref, second_ref
):
    via, fixed, moving = via_terms(own_ref, count_ref, low_ref, below_ref[1], above_ref[0], below_ref[0])

    def right_side(row):
        return fixed(row) + moving(row) - loads_ref[row]

    def diagonal(row, links):
        across = across_ref[row]
        total = across + column_left(across)
        for link in links:
            total = total + down_ref[link]
        return total + via(row)

    inverses = 1.0 / diagonal(1, (0, 1)), 1.0 / diagonal(rows - 2, (rows - 3, rows - 2))
    for slot, pair in enumerate(edges(x_ref, across_ref, down_ref, right_side, inverses, rows)):
        send_by_parity(first_ref, second_ref, slot, *pair)
    send_by_parity(first_ref, second_ref, 2, diagonal(0, (0,)), diagonal(rows - 1, (rows - 2,)))


def next_early_kernel(
    single,
    rows,
    x_ref,
    across_ref,
    down_ref,
    loads_ref,
    inverse_ref,
    own_ref,
    count_ref,
    low_ref,
    weight_ref,
    after_ref,
    first_ref,
    second_ref,
    *factor_refs,
):
    _, layer = place()
    _, fixed, _ = via_terms(own_ref, count_ref, low_ref, weight_ref[1], None, None)

    def right_side(row):
        return fixed(row) - loads_ref[row]

    send_by_parity(first_ref, second_ref, 0, x_ref[0], x_ref[rows - 1])
    inverses = inverse_ref[1], inverse_ref[rows - 2]
    for slot, pair in enumerate(edges(x_ref, across_ref, down_ref, right_side, inverses, rows)):
        send_by_parity(first_ref, second_ref, 1 + slot, *pair)
    if single:
        cells = jnp.where(layer == 0, own_ref[...], low_ref[...])
        weight = jnp.where(layer == 0, weight_of(count_ref[...]), weight_ref[1])
        send_by_parity(first_ref, second_ref, 3, marked(cells, 0, 1.0), marked(cells, rows - 1, 1.0))
        factors = []
        for (edge, within, link), inverse in zip(edge_ends(rows), inverses):
            share = FACTORS[0][1] * inverse * down_ref[link]
            factors.append(marked(cells, edge, weight) + marked(cells, within, weight * share))
        send_by_parity(*factor_refs, 0, *factors)


def next_late_kernel(
    rows, down_ref, inverse_ref, own_ref, count_ref, low_ref, weight_ref, above_ref, below_ref, first_ref, second_ref
):
    _, _, moving = via_terms(own_ref, count_ref, low_ref, weight_ref[1], above_ref[0], below_ref[0])
    found = []
    for edge, within, link in edge_ends(rows):
        change = moving(edge)
        share = FACTORS[0][1] * inverse_ref[within] * down_ref[link]
        found.append((change, change + share * moving(within)))
    for slot, pair in enumerate(zip(*found)):
        send_by_parity(first_ref, second_ref, slot, *pair)


def next_late_single_kernel(first_factor_ref, second_factor_ref, volts_ref, first_ref, second_ref):
    first_ref[0] = first_factor_ref[0] * volts_ref[0]
    second_ref[0] = second_factor_ref[0] * volts_ref[0]


def relaxed(x, flow, side, inverse, previous, sweep):
    keep, gain = FACTORS[sweep]
    update = gain * (inverse * (side + flow) - x)
    if sweep > 0:
        update = update + keep * previous
    return x + update, update


def chosen(single, own, low):
    _, layer = place()
    return [jnp.where(layer == 0, own, low)] if single else [own, low]


def inner_rows(
    rows, outside, x_ref, across_ref, down_ref, side_ref, inverse_ref, work, update_ref, core_ref, keep_ref
):
    sources = [x_ref, *work]
    targets = [*work, core_ref]
    for sweep in range(SWEEPS):
        source, target = sources[sweep], targets[sweep]
        for row in range(sweep, rows - sweep):
            x = source[row]
            flow = beside(x, across_ref[row])
            if row == 0:
                flow = flow + outside[0]
            else:
                flow = flow + down_ref[row - 1] * source[row - 1]
            if row == rows - 1:
                flow = flow + outside[1]
            else:
                flow = flow + down_ref[row] * source[row + 1]
            previous = update_ref[row] if sweep > 0 else None
            value, update = relaxed(x, flow, side_ref[row], inverse_ref[row], previous, sweep)
            target[row] = value
            if sweep < SWEEPS - 1:
                update_ref[row] = update
                for side, depth in ((0, row), (1, rows - 1 - row)):
                    slot = 3 * (2 * sweep + side)
                    if depth == sweep:
                        keep_ref[slot] = value
                        keep_ref[slot + 2] = update
                    if depth == sweep + 1:
                        keep_ref[slot + 1] = value


def outer_rows(side, rows, halo, link, inverse_edge, x_ref, across_ref, down_ref, side_ref, inverse_ref, keep_ref):
    edge_x, edge_q, edge_across = halo

    def row_of(depth):
        return depth if side == 0 else rows - 1 - depth

    def link_out(depth):
        if depth == 0:
            return link
        return down_ref[depth - 1] if side == 0 else down_ref[rows - 1 - depth]

    def link_in(depth):
        return down_ref[depth] if side == 0 else down_ref[rows - 2 - depth]

    values = {-1: edge_x, 0: x_ref[row_of(0)]}
    updates = {}
    for sweep in range(SWEEPS):
        found, changed = {}, {}
        if sweep < SWEEPS - 1:
            x = values[-1]
            flow = beside(x, edge_across) + link * values[0]
            found[-1], changed[-1] = relaxed(x, flow, edge_q[sweep], inverse_edge, updates.get(-1), sweep)
        for depth in range(sweep):
            row = row_of(depth)
            x = values[depth]
            flow = beside(x, across_ref[row]) + link_out(depth) * values[depth - 1] + link_in(depth) * values[depth + 1]
            found[depth], changed[depth] = relaxed(x, flow, side_ref[row], inverse_ref[row], updates[depth], sweep)
        if sweep < SWEEPS - 1:
            slot = 3 * (2 * sweep + side)
            found[sweep] = keep_ref[slot]
            changed[sweep] = keep_ref[slot + 2]
            found[sweep + 1] = keep_ref[slot + 1]
        values, updates = found, changed
    return {row_of(depth): value for depth, value in values.items()}


KEPT = 6 * (SWEEPS - 1)


def first_inner_kernel(
    single,
    rows,
    x_ref,
    across_ref,
    down_ref,
    loads_ref,
    own_ref,
    count_ref,
    low_ref,
    above_ref,
    below_ref,
    first_ref,
    second_ref,
    after_ref,
    core_ref,
    side_ref,
    inverse_ref,
    keep_ref,
    halo_ref,
    picked_ref,
    *scratch,
):
    tile, _ = place()
    via, fixed, moving = via_terms(own_ref, count_ref, low_ref, below_ref[1], above_ref[0], below_ref[0])
    top_x, low_x = taken_by_parity(first_ref, second_ref, 0)
    top_across, low_across = taken_by_parity(first_ref, second_ref, 1)
    link, _ = taken_by_parity(first_ref, second_ref, 2)
    link = jnp.where(tile == 0, 0.0, link)
    for slot, value in enumerate((top_across, low_across, link, top_x, low_x)):
        halo_ref[slot] = value
    for row in range(rows):
        side_ref[row] = fixed(row) + moving(row) - loads_ref[row]
        across = across_ref[row]
        diagonal = across + column_left(across) + down_ref[row] + via(row)
        diagonal = diagonal + (down_ref[row - 1] if row > 0 else link)
        inverse_ref[row] = 1.0 / diagonal
    outside = link * top_x, down_ref[rows - 1] * low_x
    shared = (x_ref, across_ref, down_ref, side_ref, inverse_ref)
    inner_rows(rows, outside, *shared, scratch[:-1], scratch[-1], core_ref, keep_ref)
    for index, cells in enumerate(chosen(single, own_ref[...], low_ref[...])):
        total = jnp.zeros(cells.shape, jnp.float32)
        for row in range(SWEEPS - 1, rows - SWEEPS + 1):
            total = total + marked(cells, row, core_ref[row])
        picked_ref[index] = total


def first_outer_kernel(
    single,
    rows,
    x_ref,
    across_ref,
    down_ref,
    side_ref,
    inverse_ref,
    keep_ref,
    halo_ref,
    picked_ref,
    own_ref,
    low_ref,
    first_ref,
    second_ref,
    core_ref,
    next_ref,
    edge_ref,
    *sends,
):
    top_q0, low_q0 = taken_by_parity(first_ref, second_ref, 0)
    top_q1, low_q1 = taken_by_parity(first_ref, second_ref, 1)
    top_diag, low_diag = taken_by_parity(first_ref, second_ref, 2)
    link, low_link = halo_ref[2], down_ref[rows - 1]
    top_inverse = 1.0 / (top_diag + link)
    low_inverse = 1.0 / (low_diag + low_link)
    edge_ref[0] = top_inverse
    edge_ref[1] = low_inverse
    shared = (x_ref, across_ref, down_ref, side_ref, inverse_ref, keep_ref)
    outer = outer_rows(0, rows, (halo_ref[3], (top_q0, top_q1), halo_ref[0]), link, top_inverse, *shared)
    outer.update(
        outer_rows(1, rows, (halo_ref[4], (low_q0, low_q1), halo_ref[1]), low_link, low_inverse, *shared)
    )
    for row, value in outer.items():
        next_ref[row] = value
    for index, cells in enumerate(chosen(single, own_ref[...], low_ref[...])):
        total = picked_ref[index]
        for row, value in outer.items():
            total = total + marked(cells, row, value)
        sends[index][0] = total


def last_inner_kernel(
    rows,
    x_ref,
    across_ref,
    down_ref,
    loads_ref,
    inverse_ref,
    halo_ref,
    own_ref,
    count_ref,
    low_ref,
    weight_ref,
    above_ref,
    below_ref,
    first_ref,
    second_ref,
    after_ref,
    core_ref,
    side_ref,
    keep_ref,
    *scratch,
):
    _, fixed, moving = via_terms(own_ref, count_ref, low_ref, weight_ref[1], above_ref[0], below_ref[0])
    for row in range(rows):
        side_ref[row] = fixed(row) + moving(row) - loads_ref[row]
    top_x, low_x = taken_by_parity(first_ref, second_ref, 0)
    outside = halo_ref[2] * top_x, down_ref[rows - 1] * low_x
    shared = (x_ref, across_ref, down_ref, side_ref, inverse_ref)
    inner_rows(rows, outside, *shared, scratch[:-1], scratch[-1], core_ref, keep_ref)


def last_outer_kernel(
    single,
    rows,
    x_ref,
    across_ref,
    down_ref,
    side_ref,
    inverse_ref,
    keep_ref,
    halo_ref,
    edge_ref,
    early_first_ref,
    early_second_ref,
    first_ref,
    second_ref,
    core_ref,
    out_ref,
    next_ref,
    held,
    sems,
):
    early = [taken_by_parity(early_first_ref, early_second_ref, slot) for slot in range(4 if single else 3)]
    late = [taken_by_parity(first_ref, second_ref, slot) for slot in range(1 if single else 2)]
    leaving = []
    for side in range(2):
        if single:
            changes = early[3][side] * late[0][side], late[0][side]
        else:
            changes = late[0][side], late[1][side]
        sides = early[1][side] + changes[0], early[2][side] + changes[1]
        outer = outer_rows(
            side,
            rows,
            (early[0][side], sides, halo_ref[side]),
            halo_ref[2] if side == 0 else down_ref[rows - 1],
            edge_ref[side],
            *(x_ref, across_ref, down_ref, side_ref, inverse_ref, keep_ref),
        )
        for row, value in outer.items():
            next_ref[row] = value
        half = rows // 2
        for first, width in chunks_of(held.shape[1], CHUNKS):
            for top in range(side * half, side * half + half, 8):
                for start in range(first, first + width, LANES):
                    held[pl.ds(top, 8), pl.ds(start, LANES)] = next_ref[pl.ds(top, 8), start // LANES, :]
            part = pl.ds(side * half, half), pl.ds(first, width)
            copy = pltpu.make_async_copy(held.at[part], out_ref.at[part], sems.at[len(leaving)])
            copy.start()
            leaving.append(copy)
    for copy in leaving:
        copy.wait()


def call(kernel, name, ins, outs, scratch=(), aliases=None):
    spaces = {"vmem": pltpu.VMEM, "hbm": pltpu.HBM, "any": pl.ANY}
    return pl.pallas_call(
        kernel,
        out_shape=[jax.ShapeDtypeStruct(shape, jnp.float32) for _, shape in outs],
        in_specs=[pl.BlockSpec(memory_space=spaces[space]) for space, _ in ins],
        out_specs=[pl.BlockSpec(memory_space=spaces[space]) for space, _ in outs],
        scratch_shapes=list(scratch),
        input_output_aliases=aliases or {},
        compiler_params=pltpu.CompilerParams(vmem_limit_bytes=40 * 1024 * 1024),
        name=name,
    )(*(array for _, array in ins))


def routes(tiles, layers):
    def at(tile, layer):
        return tile * layers + layer % layers

    everywhere = [(tile, layer) for tile in range(tiles) for layer in range(layers)]
    up = [(at(t, l), at(t, l + 1)) for t, l in everywhere]
    down = [(at(t, l), at(t, l - 1)) for t, l in everywhere]
    first, second = [], []
    for t, l in everywhere:
        first.append((at(t, l), at(t ^ 1, l)))
        beyond = t + 1 if t % 2 else t - 1
        if 0 <= beyond < tiles:
            second.append((at(t, l), at(beyond, l)))
        else:
            second.append((at(t, l), at(t, l + 1)))
    return up, down, first, second


def local(class_index, class_conductance, loads, start_volts, via_cells, via_counts):
    rows, cols = loads.shape[1:]
    lines = cols // LANES
    tiles, layers = lax.axis_size("tile"), lax.axis_size("layer")
    up, down, first, second = routes(tiles, layers)
    single = layers == 2
    move = functools.partial(lax.ppermute, axis_name=("tile", "layer"))

    def rows_of(count):
        return (count, lines, LANES)

    def vmem(*arrays):
        return [("vmem", array) for array in arrays]

    def between_layers(sends):
        if single:
            got = move(sends[0], perm=up)
            return got, got
        return move(sends[1], perm=down), move(sends[0], perm=up)

    def beside_tile(sent):
        return move(sent[0], perm=first), move(sent[1], perm=second)

    field = ("vmem", rows_of(rows))
    work = [pltpu.VMEM(rows_of(rows), jnp.float32)] * SWEEPS
    pick_count = 1 if single else 2
    picks = [("vmem", rows_of(1))] * pick_count

    own = via_cells.reshape(lines, LANES)
    counts = via_counts.reshape(lines, LANES)
    low = move(own, perm=up)
    table = jnp.pad(class_conductance, ((0, 0), (0, LANES - class_conductance.shape[1])))
    across, downward, load = call(unpack_kernel, "unpack", vmem(class_index, table, loads), [field] * 3)
    (x,) = call(unpack_volts_kernel, "unpack_volts", vmem(start_volts), [field])
    vias = (own, counts, low)
    sends = call(
        functools.partial(links_kernel, single, rows),
        "links",
        vmem(x, own, counts, low),
        [("vmem", rows_of(2))] if single else [("vmem", rows_of(2)), ("vmem", rows_of(1))],
    )
    above, below = between_layers(sends)
    weights = below
    sent = call(
        still_edges_kernel,
        "still_edges",
        vmem(x, across, downward) + [("any", sends[0])],
        [("vmem", rows_of(3))] * 2,
    )
    early = beside_tile(sent)
    sent = call(
        functools.partial(first_edges_kernel, rows),
        "first_edges",
        vmem(x, across, downward, load, *vias, above, below),
        [("vmem", rows_of(3))] * 2,
    )
    got = beside_tile(sent)
    core, side, inverse, keep, halo, picked = call(
        functools.partial(first_inner_kernel, single, rows),
        "first_inner",
        vmem(x, across, downward, load, *vias, above, below, *early) + [("any", sent[1])],
        [field, field, field, ("vmem", rows_of(KEPT)), ("vmem", rows_of(5)), ("vmem", rows_of(pick_count))],
        work,
    )
    x, edge, *sends = call(
        functools.partial(first_outer_kernel, single, rows),
        "first_outer",
        vmem(x, across, downward, side, inverse, keep, halo, picked, own, low, *got, core),
        [field, ("vmem", rows_of(2))] + picks,
        aliases={12: 0},
    )
    above, below = between_layers(sends)
    early_rows, late_rows = (4, 1) if single else (3, 2)
    sent = call(
        functools.partial(next_early_kernel, single, rows),
        "next_early",
        vmem(x, across, downward, load, inverse, *vias, weights) + [("any", sends[0])],
        [("vmem", rows_of(early_rows))] * 2 + [("vmem", rows_of(1))] * (2 if single else 0),
    )
    early = beside_tile(sent[:2])
    if single:
        late = call(
            next_late_single_kernel,
            "next_late",
            vmem(*sent[2:], above),
            [("vmem", rows_of(late_rows))] * 2,
        )
    else:
        late = call(
            functools.partial(next_late_kernel, rows),
            "next_late",
            vmem(downward, inverse, *vias, weights, above, below),
            [("vmem", rows_of(late_rows))] * 2,
        )
    got = beside_tile(late)
    core, side, keep = call(
        functools.partial(last_inner_kernel, rows),
        "last_inner",
        vmem(x, across, downward, load, inverse, halo, *vias, weights, above, below, *early) + [("any", late[1])],
        [field, field, ("vmem", rows_of(KEPT))],
        work,
    )
    volts, _ = call(
        functools.partial(last_outer_kernel, single, rows),
        "last_outer",
        vmem(x, across, downward, side, inverse, keep, halo, edge, *early, *got, core),
        [("hbm", (rows, cols)), field],
        [pltpu.VMEM((rows, cols), jnp.float32), pltpu.SemaphoreType.DMA((2 * CHUNKS,))],
        aliases={12: 1},
    )
    return volts[None]


def solution(mesh):
    placed = (
        P("layer", None, "tile", None),
        P("layer", None),
        P("layer", "tile", None),
        P("layer", "tile", None),
        P("layer", "tile"),
        P("layer", "tile"),
    )
    return jax.shard_map(
        local, mesh=mesh, in_specs=placed, out_specs=P("layer", "tile", None), check_vma=False
    )
```

```python
import functools

import jax
import jax.numpy as jnp
from jax import lax
from jax.experimental import pallas as pl
from jax.experimental.pallas import tpu as pltpu
from jax.sharding import PartitionSpec as P

OUTER = 2
SWEEPS = 3
VIA_UNIT = 2.0
LOWER_BOUND = 0.05
UPPER_BOUND = 2.0
LANES = 128
CHUNKS = 2


def chebyshev_terms(count):
    centre_value = 0.5 * (UPPER_BOUND + LOWER_BOUND)
    half_width = 0.5 * (UPPER_BOUND - LOWER_BOUND)
    sigma = centre_value / half_width
    rho_last = 1.0 / sigma
    terms = [(0.0, 1.0 / centre_value)]
    for index in range(1, count):
        rho_next = 1.0 / (2.0 * sigma - rho_last)
        terms.append((rho_next * rho_last, 2.0 * rho_next / half_width))
        rho_last = rho_next
    return terms


FACTORS = chebyshev_terms(SWEEPS)


def column_right(row):
    lane = lax.broadcasted_iota(jnp.int32, row.shape, 1)
    turned = pltpu.roll(row, LANES - 1, 1)
    return jnp.where(lane == LANES - 1, pltpu.roll(turned, row.shape[0] - 1, 0), turned)


def column_left(row):
    lane = lax.broadcasted_iota(jnp.int32, row.shape, 1)
    turned = pltpu.roll(row, 1, 1)
    return jnp.where(lane == 0, pltpu.roll(turned, 1, 0), turned)


def beside(x, across):
    return across * column_right(x) + column_left(across * x)


def place():
    return lax.axis_index("tile"), lax.axis_index("layer")


def marked(cells, row, value):
    return jnp.where(cells == row, value, 0.0)


def pick(x_ref, cells, rows):
    total = jnp.zeros(cells.shape, jnp.float32)
    for row in range(rows):
        total = total + marked(cells, row, x_ref[row])
    return total


def weight_of(counts):
    return VIA_UNIT * counts.astype(jnp.float32)


def chunks_of(cols, count):
    width = cols // count
    return [(first, width) for first in range(0, cols, width)]


def unpack_field_kernel(field_ref, out_ref):
    rows, cols = field_ref.shape[1:]
    for top in range(0, rows, 8):
        for start in range(0, cols, LANES):
            out_ref[pl.ds(top, 8), start // LANES, :] = field_ref[0, pl.ds(top, 8), pl.ds(start, LANES)]


def unpack_index_kernel(index_ref, table_ref, across_ref, down_ref):
    rows, cols = index_ref.shape[2:]
    tile, _ = place()
    last_tile = tile == lax.axis_size("tile") - 1
    table = jnp.broadcast_to(table_ref[...], (8, LANES))
    lane = lax.broadcasted_iota(jnp.int32, (8, LANES), 1)
    sub = lax.broadcasted_iota(jnp.int32, (8, LANES), 0)
    for top in range(0, rows, 8):
        part = pl.ds(top, 8)
        for start in range(0, cols, LANES):
            here, line = pl.ds(start, LANES), start // LANES
            across = jnp.take_along_axis(table, index_ref[0, 0, part, here], axis=1, mode="promise_in_bounds")
            if start + LANES == cols:
                across = jnp.where(lane == LANES - 1, 0.0, across)
            across_ref[part, line, :] = across
            down = jnp.take_along_axis(table, index_ref[0, 1, part, here], axis=1, mode="promise_in_bounds")
            if top + 8 == rows:
                down = jnp.where((sub == 7) & last_tile, 0.0, down)
            down_ref[part, line, :] = down


def links_kernel(single, rows, x_ref, own_ref, count_ref, low_ref, after_ref, *out_refs):
    for out_ref, cells in zip(out_refs, chosen(single, own_ref[...], low_ref[...])):
        out_ref[0] = pick(x_ref, cells, rows)
    out_refs[0][1] = weight_of(count_ref[...])


def via_terms(own_ref, count_ref, low_ref, low_weight, from_above, from_below):
    _, layer = place()
    on_top = layer == lax.axis_size("layer") - 1
    own_weight = weight_of(count_ref[...])
    low_weight = jnp.where(layer == 0, 0.0, low_weight)
    fixed_source = jnp.where(on_top, own_weight, 0.0)
    own, low = own_ref[...], low_ref[...]

    def via(row):
        return marked(own, row, own_weight) + marked(low, row, low_weight)

    def fixed(row):
        return marked(own, row, fixed_source)

    if from_above is None:
        return via, fixed, None
    own_source = jnp.where(on_top, 0.0, own_weight * from_above)
    low_source = low_weight * from_below

    def moving(row):
        return marked(own, row, own_source) + marked(low, row, low_source)

    return via, fixed, moving


def send_by_parity(first_ref, second_ref, slot, top, bottom):
    tile, _ = place()
    even = lax.rem(tile, 2) == 0
    first_ref[slot] = jnp.where(even, bottom, top)
    second_ref[slot] = jnp.where(even, top, bottom)


def taken_by_parity(first_ref, second_ref, slot):
    tile, _ = place()
    even = lax.rem(tile, 2) == 0
    first, second = first_ref[slot], second_ref[slot]
    return jnp.where(even, second, first), jnp.where(even, first, second)


def edge_flow(x_ref, across_ref, down_ref, row):
    return beside(x_ref[row], across_ref[row]) + down_ref[row] * x_ref[row + 1] + down_ref[row - 1] * x_ref[row - 1]


def edge_ends(rows):
    return (0, 1, 0), (rows - 1, rows - 2, rows - 2)


def edges(x_ref, across_ref, down_ref, right_side, inverses, rows):
    found = []
    for (edge, within, link), inverse in zip(edge_ends(rows), inverses):
        x = x_ref[within]
        flow = edge_flow(x_ref, across_ref, down_ref, within)
        later = x + FACTORS[0][1] * (inverse * (right_side(within) + flow) - x)
        found.append((right_side(edge) + down_ref[link] * x, right_side(edge) + down_ref[link] * later))
    return tuple(zip(*found))


def still_edges_kernel(x_ref, across_ref, down_ref, first_ref, second_ref):
    rows = x_ref.shape[0]
    for slot, ref in enumerate((x_ref, across_ref, down_ref)):
        send_by_parity(first_ref, second_ref, slot, ref[0], ref[rows - 1])


def first_edges_kernel(
    rows, x_ref, across_ref, down_ref, loads_ref, own_ref, count_ref, low_ref, above_ref, below_ref, first_ref, second_ref
):
    via, fixed, moving = via_terms(own_ref, count_ref, low_ref, below_ref[1], above_ref[0], below_ref[0])

    def right_side(row):
        return fixed(row) + moving(row) - loads_ref[row]

    def diagonal(row, links):
        across = across_ref[row]
        total = across + column_left(across)
        for link in links:
            total = total + down_ref[link]
        return total + via(row)

    inverses = 1.0 / diagonal(1, (0, 1)), 1.0 / diagonal(rows - 2, (rows - 3, rows - 2))
    for slot, pair in enumerate(edges(x_ref, across_ref, down_ref, right_side, inverses, rows)):
        send_by_parity(first_ref, second_ref, slot, *pair)
    send_by_parity(first_ref, second_ref, 2, diagonal(0, (0,)), diagonal(rows - 1, (rows - 2,)))


def next_early_kernel(
    single,
    rows,
    x_ref,
    across_ref,
    down_ref,
    loads_ref,
    inverse_ref,
    own_ref,
    count_ref,
    low_ref,
    weight_ref,
    after_ref,
    first_ref,
    second_ref,
    *factor_refs,
):
    _, layer = place()
    _, fixed, _ = via_terms(own_ref, count_ref, low_ref, weight_ref[1], None, None)

    def right_side(row):
        return fixed(row) - loads_ref[row]

    send_by_parity(first_ref, second_ref, 0, x_ref[0], x_ref[rows - 1])
    inverses = inverse_ref[1], inverse_ref[rows - 2]
    for slot, pair in enumerate(edges(x_ref, across_ref, down_ref, right_side, inverses, rows)):
        send_by_parity(first_ref, second_ref, 1 + slot, *pair)
    if single:
        cells = jnp.where(layer == 0, own_ref[...], low_ref[...])
        weight = jnp.where(layer == 0, weight_of(count_ref[...]), weight_ref[1])
        send_by_parity(first_ref, second_ref, 3, marked(cells, 0, 1.0), marked(cells, rows - 1, 1.0))
        factors = []
        for (edge, within, link), inverse in zip(edge_ends(rows), inverses):
            share = FACTORS[0][1] * inverse * down_ref[link]
            factors.append(marked(cells, edge, weight) + marked(cells, within, weight * share))
        send_by_parity(*factor_refs, 0, *factors)


def next_late_kernel(
    rows, down_ref, inverse_ref, own_ref, count_ref, low_ref, weight_ref, above_ref, below_ref, first_ref, second_ref
):
    _, _, moving = via_terms(own_ref, count_ref, low_ref, weight_ref[1], above_ref[0], below_ref[0])
    found = []
    for edge, within, link in edge_ends(rows):
        change = moving(edge)
        share = FACTORS[0][1] * inverse_ref[within] * down_ref[link]
        found.append((change, change + share * moving(within)))
    for slot, pair in enumerate(zip(*found)):
        send_by_parity(first_ref, second_ref, slot, *pair)


def next_late_single_kernel(first_factor_ref, second_factor_ref, volts_ref, first_ref, second_ref):
    first_ref[0] = first_factor_ref[0] * volts_ref[0]
    second_ref[0] = second_factor_ref[0] * volts_ref[0]


def relaxed(x, flow, side, inverse, previous, sweep):
    keep, gain = FACTORS[sweep]
    update = gain * (inverse * (side + flow) - x)
    if sweep > 0:
        update = update + keep * previous
    return x + update, update


def chosen(single, own, low):
    _, layer = place()
    return [jnp.where(layer == 0, own, low)] if single else [own, low]


def inner_rows(
    rows, outside, x_ref, across_ref, down_ref, side_ref, inverse_ref, work, update_ref, core_ref, keep_ref
):
    sources = [x_ref, *work]
    targets = [*work, core_ref]
    for sweep in range(SWEEPS):
        source, target = sources[sweep], targets[sweep]
        for row in range(sweep, rows - sweep):
            x = source[row]
            flow = beside(x, across_ref[row])
            if row == 0:
                flow = flow + outside[0]
            else:
                flow = flow + down_ref[row - 1] * source[row - 1]
            if row == rows - 1:
                flow = flow + outside[1]
            else:
                flow = flow + down_ref[row] * source[row + 1]
            previous = update_ref[row] if sweep > 0 else None
            value, update = relaxed(x, flow, side_ref[row], inverse_ref[row], previous, sweep)
            target[row] = value
            if sweep < SWEEPS - 1:
                update_ref[row] = update
                for side, depth in ((0, row), (1, rows - 1 - row)):
                    slot = 3 * (2 * sweep + side)
                    if depth == sweep:
                        keep_ref[slot] = value
                        keep_ref[slot + 2] = update
                    if depth == sweep + 1:
                        keep_ref[slot + 1] = value


def outer_rows(side, rows, halo, link, inverse_edge, x_ref, across_ref, down_ref, side_ref, inverse_ref, keep_ref):
    edge_x, edge_q, edge_across = halo

    def row_of(depth):
        return depth if side == 0 else rows - 1 - depth

    def link_out(depth):
        if depth == 0:
            return link
        return down_ref[depth - 1] if side == 0 else down_ref[rows - 1 - depth]

    def link_in(depth):
        return down_ref[depth] if side == 0 else down_ref[rows - 2 - depth]

    values = {-1: edge_x, 0: x_ref[row_of(0)]}
    updates = {}
    for sweep in range(SWEEPS):
        found, changed = {}, {}
        if sweep < SWEEPS - 1:
            x = values[-1]
            flow = beside(x, edge_across) + link * values[0]
            found[-1], changed[-1] = relaxed(x, flow, edge_q[sweep], inverse_edge, updates.get(-1), sweep)
        for depth in range(sweep):
            row = row_of(depth)
            x = values[depth]
            flow = beside(x, across_ref[row]) + link_out(depth) * values[depth - 1] + link_in(depth) * values[depth + 1]
            found[depth], changed[depth] = relaxed(x, flow, side_ref[row], inverse_ref[row], updates[depth], sweep)
        if sweep < SWEEPS - 1:
            slot = 3 * (2 * sweep + side)
            found[sweep] = keep_ref[slot]
            changed[sweep] = keep_ref[slot + 2]
            found[sweep + 1] = keep_ref[slot + 1]
        values, updates = found, changed
    return {row_of(depth): value for depth, value in values.items()}


KEPT = 6 * (SWEEPS - 1)


def first_inner_kernel(
    single,
    rows,
    x_ref,
    across_ref,
    down_ref,
    loads_ref,
    own_ref,
    count_ref,
    low_ref,
    above_ref,
    below_ref,
    first_ref,
    second_ref,
    after_ref,
    core_ref,
    side_ref,
    inverse_ref,
    keep_ref,
    halo_ref,
    picked_ref,
    *scratch,
):
    tile, _ = place()
    via, fixed, moving = via_terms(own_ref, count_ref, low_ref, below_ref[1], above_ref[0], below_ref[0])
    top_x, low_x = taken_by_parity(first_ref, second_ref, 0)
    top_across, low_across = taken_by_parity(first_ref, second_ref, 1)
    link, _ = taken_by_parity(first_ref, second_ref, 2)
    link = jnp.where(tile == 0, 0.0, link)
    for slot, value in enumerate((top_across, low_across, link, top_x, low_x)):
        halo_ref[slot] = value
    for row in range(rows):
        side_ref[row] = fixed(row) + moving(row) - loads_ref[row]
        across = across_ref[row]
        diagonal = across + column_left(across) + down_ref[row] + via(row)
        diagonal = diagonal + (down_ref[row - 1] if row > 0 else link)
        inverse_ref[row] = 1.0 / diagonal
    outside = link * top_x, down_ref[rows - 1] * low_x
    shared = (x_ref, across_ref, down_ref, side_ref, inverse_ref)
    inner_rows(rows, outside, *shared, scratch[:-1], scratch[-1], core_ref, keep_ref)
    for index, cells in enumerate(chosen(single, own_ref[...], low_ref[...])):
        total = jnp.zeros(cells.shape, jnp.float32)
        for row in range(SWEEPS - 1, rows - SWEEPS + 1):
            total = total + marked(cells, row, core_ref[row])
        picked_ref[index] = total


def first_outer_kernel(
    single,
    rows,
    x_ref,
    across_ref,
    down_ref,
    side_ref,
    inverse_ref,
    keep_ref,
    halo_ref,
    picked_ref,
    own_ref,
    low_ref,
    first_ref,
    second_ref,
    core_ref,
    next_ref,
    edge_ref,
    *sends,
):
    top_q0, low_q0 = taken_by_parity(first_ref, second_ref, 0)
    top_q1, low_q1 = taken_by_parity(first_ref, second_ref, 1)
    top_diag, low_diag = taken_by_parity(first_ref, second_ref, 2)
    link, low_link = halo_ref[2], down_ref[rows - 1]
    top_inverse = 1.0 / (top_diag + link)
    low_inverse = 1.0 / (low_diag + low_link)
    edge_ref[0] = top_inverse
    edge_ref[1] = low_inverse
    shared = (x_ref, across_ref, down_ref, side_ref, inverse_ref, keep_ref)
    outer = outer_rows(0, rows, (halo_ref[3], (top_q0, top_q1), halo_ref[0]), link, top_inverse, *shared)
    outer.update(
        outer_rows(1, rows, (halo_ref[4], (low_q0, low_q1), halo_ref[1]), low_link, low_inverse, *shared)
    )
    for row, value in outer.items():
        next_ref[row] = value
    for index, cells in enumerate(chosen(single, own_ref[...], low_ref[...])):
        total = picked_ref[index]
        for row, value in outer.items():
            total = total + marked(cells, row, value)
        sends[index][0] = total


def last_inner_kernel(
    rows,
    x_ref,
    across_ref,
    down_ref,
    loads_ref,
    inverse_ref,
    halo_ref,
    own_ref,
    count_ref,
    low_ref,
    weight_ref,
    above_ref,
    below_ref,
    first_ref,
    second_ref,
    after_ref,
    core_ref,
    side_ref,
    keep_ref,
    *scratch,
):
    _, fixed, moving = via_terms(own_ref, count_ref, low_ref, weight_ref[1], above_ref[0], below_ref[0])
    for row in range(rows):
        side_ref[row] = fixed(row) + moving(row) - loads_ref[row]
    top_x, low_x = taken_by_parity(first_ref, second_ref, 0)
    outside = halo_ref[2] * top_x, down_ref[rows - 1] * low_x
    shared = (x_ref, across_ref, down_ref, side_ref, inverse_ref)
    inner_rows(rows, outside, *shared, scratch[:-1], scratch[-1], core_ref, keep_ref)


def last_outer_kernel(
    single,
    rows,
    x_ref,
    across_ref,
    down_ref,
    side_ref,
    inverse_ref,
    keep_ref,
    halo_ref,
    edge_ref,
    early_first_ref,
    early_second_ref,
    first_ref,
    second_ref,
    core_ref,
    out_ref,
    next_ref,
    held,
    sems,
):
    early = [taken_by_parity(early_first_ref, early_second_ref, slot) for slot in range(4 if single else 3)]
    late = [taken_by_parity(first_ref, second_ref, slot) for slot in range(1 if single else 2)]
    leaving = []
    for side in range(2):
        if single:
            changes = early[3][side] * late[0][side], late[0][side]
        else:
            changes = late[0][side], late[1][side]
        sides = early[1][side] + changes[0], early[2][side] + changes[1]
        outer = outer_rows(
            side,
            rows,
            (early[0][side], sides, halo_ref[side]),
            halo_ref[2] if side == 0 else down_ref[rows - 1],
            edge_ref[side],
            *(x_ref, across_ref, down_ref, side_ref, inverse_ref, keep_ref),
        )
        for row, value in outer.items():
            next_ref[row] = value
        half = rows // 2
        for first, width in chunks_of(held.shape[1], CHUNKS):
            for top in range(side * half, side * half + half, 8):
                for start in range(first, first + width, LANES):
                    held[pl.ds(top, 8), pl.ds(start, LANES)] = next_ref[pl.ds(top, 8), start // LANES, :]
            part = pl.ds(side * half, half), pl.ds(first, width)
            copy = pltpu.make_async_copy(held.at[part], out_ref.at[part], sems.at[len(leaving)])
            copy.start()
            leaving.append(copy)
    for copy in leaving:
        copy.wait()


def call(kernel, name, ins, outs, scratch=(), aliases=None, work=None):
    spaces = {"vmem": pltpu.VMEM, "hbm": pltpu.HBM, "any": pl.ANY}
    return pl.pallas_call(
        kernel,
        out_shape=[jax.ShapeDtypeStruct(shape, jnp.float32) for _, shape in outs],
        in_specs=[pl.BlockSpec(memory_space=spaces[space]) for space, _ in ins],
        out_specs=[pl.BlockSpec(memory_space=spaces[space]) for space, _ in outs],
        scratch_shapes=list(scratch),
        input_output_aliases=aliases or {},
        compiler_params=pltpu.CompilerParams(vmem_limit_bytes=40 * 1024 * 1024),
        cost_estimate=work and pl.CostEstimate(flops=work, bytes_accessed=work, transcendentals=0),
        name=name,
    )(*(array for _, array in ins))


def routes(tiles, layers):
    def at(tile, layer):
        return tile * layers + layer % layers

    everywhere = [(tile, layer) for tile in range(tiles) for layer in range(layers)]
    up = [(at(t, l), at(t, l + 1)) for t, l in everywhere]
    down = [(at(t, l), at(t, l - 1)) for t, l in everywhere]
    first, second = [], []
    for t, l in everywhere:
        first.append((at(t, l), at(t ^ 1, l)))
        beyond = t + 1 if t % 2 else t - 1
        if 0 <= beyond < tiles:
            second.append((at(t, l), at(beyond, l)))
        else:
            second.append((at(t, l), at(t, l + 1)))
    return up, down, first, second


def local(class_index, class_conductance, loads, start_volts, via_cells, via_counts):
    rows, cols = loads.shape[1:]
    lines = cols // LANES
    tiles, layers = lax.axis_size("tile"), lax.axis_size("layer")
    up, down, first, second = routes(tiles, layers)
    single = layers == 2
    move = functools.partial(lax.ppermute, axis_name=("tile", "layer"))

    def rows_of(count):
        return (count, lines, LANES)

    def vmem(*arrays):
        return [("vmem", array) for array in arrays]

    def between_layers(sends):
        if single:
            got = move(sends[0], perm=up)
            return got, got
        return move(sends[1], perm=down), move(sends[0], perm=up)

    def beside_tile(sent):
        return move(sent[0], perm=first), move(sent[1], perm=second)

    field = ("vmem", rows_of(rows))
    work = [pltpu.VMEM(rows_of(rows), jnp.float32)] * SWEEPS
    pick_count = 1 if single else 2
    picks = [("vmem", rows_of(1))] * pick_count

    own = via_cells.reshape(lines, LANES)
    counts = via_counts.reshape(lines, LANES)
    low = move(own, perm=up)
    table = jnp.pad(class_conductance, ((0, 0), (0, LANES - class_conductance.shape[1])))
    across, downward = call(unpack_index_kernel, "unpack_index", vmem(class_index, table), [field] * 2)
    (x,) = call(unpack_field_kernel, "unpack_volts", vmem(start_volts), [field])
    still = call(still_edges_kernel, "still_edges", vmem(x, across, downward), [("vmem", rows_of(3))] * 2)
    vias = (own, counts, low)
    sends = call(
        functools.partial(links_kernel, single, rows),
        "links",
        vmem(x, own, counts, low) + [("any", still[0])],
        [("vmem", rows_of(2))] if single else [("vmem", rows_of(2)), ("vmem", rows_of(1))],
    )
    above, below = between_layers(sends)
    weights = below
    (load,) = call(unpack_field_kernel, "unpack_loads", vmem(loads), [field])
    early = beside_tile(still)
    sent = call(
        functools.partial(first_edges_kernel, rows),
        "first_edges",
        vmem(x, across, downward, load, *vias, above, below),
        [("vmem", rows_of(3))] * 2,
    )
    got = beside_tile(sent)
    core, side, inverse, keep, halo, picked = call(
        functools.partial(first_inner_kernel, single, rows),
        "first_inner",
        vmem(x, across, downward, load, *vias, above, below, *early) + [("any", sent[1])],
        [field, field, field, ("vmem", rows_of(KEPT)), ("vmem", rows_of(5)), ("vmem", rows_of(pick_count))],
        work,
    )
    x, edge, *sends = call(
        functools.partial(first_outer_kernel, single, rows),
        "first_outer",
        vmem(x, across, downward, side, inverse, keep, halo, picked, own, low, *got, core),
        [field, ("vmem", rows_of(2))] + picks,
        aliases={12: 0},
    )
    above, below = between_layers(sends)
    early_rows, late_rows = (4, 1) if single else (3, 2)
    sent = call(
        functools.partial(next_early_kernel, single, rows),
        "next_early",
        vmem(x, across, downward, load, inverse, *vias, weights) + [("any", sends[0])],
        [("vmem", rows_of(early_rows))] * 2 + [("vmem", rows_of(1))] * (2 if single else 0),
    )
    early = beside_tile(sent[:2])
    if single:
        late = call(
            next_late_single_kernel,
            "next_late",
            vmem(*sent[2:], above),
            [("vmem", rows_of(late_rows))] * 2,
            work=2 * 10**10,
        )
    else:
        late = call(
            functools.partial(next_late_kernel, rows),
            "next_late",
            vmem(downward, inverse, *vias, weights, above, below),
            [("vmem", rows_of(late_rows))] * 2,
            work=2 * 10**10,
        )
    got = beside_tile(late)
    core, side, keep = call(
        functools.partial(last_inner_kernel, rows),
        "last_inner",
        vmem(x, across, downward, load, inverse, halo, *vias, weights, above, below, *early) + [("any", late[1])],
        [field, field, ("vmem", rows_of(KEPT))],
        work,
    )
    volts, _ = call(
        functools.partial(last_outer_kernel, single, rows),
        "last_outer",
        vmem(x, across, downward, side, inverse, keep, halo, edge, *early, *got, core),
        [("hbm", (rows, cols)), field],
        [pltpu.VMEM((rows, cols), jnp.float32), pltpu.SemaphoreType.DMA((2 * CHUNKS,))],
        aliases={12: 1},
    )
    return volts[None]


def solution(mesh):
    placed = (
        P("layer", None, "tile", None),
        P("layer", None),
        P("layer", "tile", None),
        P("layer", "tile", None),
        P("layer", "tile"),
        P("layer", "tile"),
    )
    return jax.shard_map(
        local, mesh=mesh, in_specs=placed, out_specs=P("layer", "tile", None), check_vma=False
    )
```

```python
import functools

import jax
import jax.numpy as jnp
from jax import lax
from jax.experimental import pallas as pl
from jax.experimental.pallas import tpu as pltpu
from jax.sharding import PartitionSpec as P

OUTER = 2
SWEEPS = 3
VIA_UNIT = 2.0
LOWER_BOUND = 0.05
UPPER_BOUND = 2.0
LANES = 128
CHUNKS = 2


def chebyshev_terms(count):
    centre_value = 0.5 * (UPPER_BOUND + LOWER_BOUND)
    half_width = 0.5 * (UPPER_BOUND - LOWER_BOUND)
    sigma = centre_value / half_width
    rho_last = 1.0 / sigma
    terms = [(0.0, 1.0 / centre_value)]
    for index in range(1, count):
        rho_next = 1.0 / (2.0 * sigma - rho_last)
        terms.append((rho_next * rho_last, 2.0 * rho_next / half_width))
        rho_last = rho_next
    return terms


FACTORS = chebyshev_terms(SWEEPS)


def column_right(row):
    lane = lax.broadcasted_iota(jnp.int32, row.shape, 1)
    turned = pltpu.roll(row, LANES - 1, 1)
    return jnp.where(lane == LANES - 1, pltpu.roll(turned, row.shape[0] - 1, 0), turned)


def column_left(row):
    lane = lax.broadcasted_iota(jnp.int32, row.shape, 1)
    turned = pltpu.roll(row, 1, 1)
    return jnp.where(lane == 0, pltpu.roll(turned, 1, 0), turned)


def beside(x, across):
    return across * column_right(x) + column_left(across * x)


def place():
    return lax.axis_index("tile"), lax.axis_index("layer")


def marked(cells, row, value):
    return jnp.where(cells == row, value, 0.0)


def pick(x_ref, cells, rows):
    total = jnp.zeros(cells.shape, jnp.float32)
    for row in range(rows):
        total = total + marked(cells, row, x_ref[row])
    return total


def chunks_of(cols, count):
    width = cols // count
    return [(first, width) for first in range(0, cols, width)]


def unpack_field_kernel(field_ref, out_ref):
    rows, cols = field_ref.shape[1:]
    for top in range(0, rows, 8):
        for start in range(0, cols, LANES):
            out_ref[pl.ds(top, 8), start // LANES, :] = field_ref[0, pl.ds(top, 8), pl.ds(start, LANES)]


def unpack_index_kernel(index_ref, table_ref, across_ref, down_ref):
    rows, cols = index_ref.shape[2:]
    tile, _ = place()
    last_tile = tile == lax.axis_size("tile") - 1
    table = jnp.broadcast_to(table_ref[...], (8, LANES))
    lane = lax.broadcasted_iota(jnp.int32, (8, LANES), 1)
    sub = lax.broadcasted_iota(jnp.int32, (8, LANES), 0)
    for top in range(0, rows, 8):
        part = pl.ds(top, 8)
        for start in range(0, cols, LANES):
            here, line = pl.ds(start, LANES), start // LANES
            across = jnp.take_along_axis(table, index_ref[0, 0, part, here], axis=1, mode="promise_in_bounds")
            if start + LANES == cols:
                across = jnp.where(lane == LANES - 1, 0.0, across)
            across_ref[part, line, :] = across
            down = jnp.take_along_axis(table, index_ref[0, 1, part, here], axis=1, mode="promise_in_bounds")
            if top + 8 == rows:
                down = jnp.where((sub == 7) & last_tile, 0.0, down)
            down_ref[part, line, :] = down


def links_kernel(single, rows, x_ref, own_ref, own_weight_ref, low_ref, after_ref, *out_refs):
    for out_ref, cells in zip(out_refs, chosen(single, own_ref[...], low_ref[...])):
        out_ref[0] = pick(x_ref, cells, rows)
    out_refs[0][1] = own_weight_ref[...]


def via_terms(own_ref, own_weight_ref, low_ref, low_weight, from_above, from_below):
    _, layer = place()
    on_top = layer == lax.axis_size("layer") - 1
    own_weight = own_weight_ref[...]
    low_weight = jnp.where(layer == 0, 0.0, low_weight)
    fixed_source = jnp.where(on_top, own_weight, 0.0)
    own, low = own_ref[...], low_ref[...]

    def via(row):
        return marked(own, row, own_weight) + marked(low, row, low_weight)

    def fixed(row):
        return marked(own, row, fixed_source)

    if from_above is None:
        return via, fixed, None
    own_source = jnp.where(on_top, 0.0, own_weight * from_above)
    low_source = low_weight * from_below

    def moving(row):
        return marked(own, row, own_source) + marked(low, row, low_source)

    return via, fixed, moving


def send_by_parity(first_ref, second_ref, slot, top, bottom):
    tile, _ = place()
    even = lax.rem(tile, 2) == 0
    first_ref[slot] = jnp.where(even, bottom, top)
    second_ref[slot] = jnp.where(even, top, bottom)


def taken_by_parity(first_ref, second_ref, slot):
    tile, _ = place()
    even = lax.rem(tile, 2) == 0
    first, second = first_ref[slot], second_ref[slot]
    return jnp.where(even, second, first), jnp.where(even, first, second)


def edge_flow(x_ref, across_ref, down_ref, row):
    return beside(x_ref[row], across_ref[row]) + down_ref[row] * x_ref[row + 1] + down_ref[row - 1] * x_ref[row - 1]


def edge_ends(rows):
    return (0, 1, 0), (rows - 1, rows - 2, rows - 2)


def edges(x_ref, across_ref, down_ref, right_side, inverses, rows):
    found = []
    for (edge, within, link), inverse in zip(edge_ends(rows), inverses):
        x = x_ref[within]
        flow = edge_flow(x_ref, across_ref, down_ref, within)
        later = x + FACTORS[0][1] * (inverse * (right_side(within) + flow) - x)
        found.append((right_side(edge) + down_ref[link] * x, right_side(edge) + down_ref[link] * later))
    return tuple(zip(*found))


def still_edges_kernel(x_ref, across_ref, down_ref, own_ref, count_ref, first_ref, second_ref, cells_ref, weight_ref):
    rows = x_ref.shape[0]
    cells_ref[...] = own_ref[...]
    weight_ref[...] = VIA_UNIT * count_ref[...].astype(jnp.float32)
    for slot, ref in enumerate((x_ref, across_ref, down_ref)):
        send_by_parity(first_ref, second_ref, slot, ref[0], ref[rows - 1])


def first_edges_kernel(
    rows, x_ref, across_ref, down_ref, loads_ref, own_ref, own_weight_ref, low_ref, above_ref, below_ref, first_ref, second_ref
):
    via, fixed, moving = via_terms(own_ref, own_weight_ref, low_ref, below_ref[1], above_ref[0], below_ref[0])

    def right_side(row):
        return fixed(row) + moving(row) - loads_ref[row]

    def diagonal(row, links):
        across = across_ref[row]
        total = across + column_left(across)
        for link in links:
            total = total + down_ref[link]
        return total + via(row)

    inverses = 1.0 / diagonal(1, (0, 1)), 1.0 / diagonal(rows - 2, (rows - 3, rows - 2))
    for slot, pair in enumerate(edges(x_ref, across_ref, down_ref, right_side, inverses, rows)):
        send_by_parity(first_ref, second_ref, slot, *pair)
    send_by_parity(first_ref, second_ref, 2, diagonal(0, (0,)), diagonal(rows - 1, (rows - 2,)))


def next_early_kernel(
    single,
    rows,
    x_ref,
    across_ref,
    down_ref,
    loads_ref,
    inverse_ref,
    own_ref,
    own_weight_ref,
    low_ref,
    weight_ref,
    after_ref,
    first_ref,
    second_ref,
    *factor_refs,
):
    _, layer = place()
    _, fixed, _ = via_terms(own_ref, own_weight_ref, low_ref, weight_ref[1], None, None)

    def right_side(row):
        return fixed(row) - loads_ref[row]

    send_by_parity(first_ref, second_ref, 0, x_ref[0], x_ref[rows - 1])
    inverses = inverse_ref[1], inverse_ref[rows - 2]
    for slot, pair in enumerate(edges(x_ref, across_ref, down_ref, right_side, inverses, rows)):
        send_by_parity(first_ref, second_ref, 1 + slot, *pair)
    if single:
        cells = jnp.where(layer == 0, own_ref[...], low_ref[...])
        weight = jnp.where(layer == 0, own_weight_ref[...], weight_ref[1])
        send_by_parity(first_ref, second_ref, 3, marked(cells, 0, 1.0), marked(cells, rows - 1, 1.0))
        factors = []
        for (edge, within, link), inverse in zip(edge_ends(rows), inverses):
            share = FACTORS[0][1] * inverse * down_ref[link]
            factors.append(marked(cells, edge, weight) + marked(cells, within, weight * share))
        send_by_parity(*factor_refs, 0, *factors)


def next_late_kernel(
    rows, down_ref, inverse_ref, own_ref, own_weight_ref, low_ref, weight_ref, above_ref, below_ref, first_ref, second_ref
):
    _, _, moving = via_terms(own_ref, own_weight_ref, low_ref, weight_ref[1], above_ref[0], below_ref[0])
    found = []
    for edge, within, link in edge_ends(rows):
        change = moving(edge)
        share = FACTORS[0][1] * inverse_ref[within] * down_ref[link]
        found.append((change, change + share * moving(within)))
    for slot, pair in enumerate(zip(*found)):
        send_by_parity(first_ref, second_ref, slot, *pair)


def next_late_single_kernel(first_factor_ref, second_factor_ref, volts_ref, first_ref, second_ref):
    first_ref[0] = first_factor_ref[0] * volts_ref[0]
    second_ref[0] = second_factor_ref[0] * volts_ref[0]


def relaxed(x, flow, side, inverse, previous, sweep):
    keep, gain = FACTORS[sweep]
    update = gain * (inverse * (side + flow) - x)
    if sweep > 0:
        update = update + keep * previous
    return x + update, update


def chosen(single, own, low):
    _, layer = place()
    return [jnp.where(layer == 0, own, low)] if single else [own, low]


def inner_rows(
    rows, reach, outside, x_ref, across_ref, down_ref, side_ref, inverse_ref, work, update_ref, core_ref, keep_ref
):
    sources = [x_ref, *work]
    targets = [*work, core_ref]
    for sweep in range(SWEEPS):
        source, target = sources[sweep], targets[sweep]
        for row in range(sweep + reach, rows - sweep - reach):
            x = source[row]
            flow = beside(x, across_ref[row])
            if row == 0:
                flow = flow + outside[0]
            else:
                flow = flow + down_ref[row - 1] * source[row - 1]
            if row == rows - 1:
                flow = flow + outside[1]
            else:
                flow = flow + down_ref[row] * source[row + 1]
            previous = update_ref[row] if sweep > 0 else None
            value, update = relaxed(x, flow, side_ref[row], inverse_ref[row], previous, sweep)
            target[row] = value
            if sweep < SWEEPS - 1:
                update_ref[row] = update
                for side, depth in ((0, row), (1, rows - 1 - row)):
                    slot = 3 * (2 * sweep + side)
                    if depth == sweep + reach:
                        keep_ref[slot] = value
                        keep_ref[slot + 2] = update
                    if depth == sweep + reach + 1:
                        keep_ref[slot + 1] = value


def outer_rows(side, rows, reach, halo, link, inverse_edge, x_ref, across_ref, down_ref, side_ref, inverse_ref, keep_ref):
    edge_x, edge_q, edge_across = halo

    def row_of(depth):
        return depth if side == 0 else rows - 1 - depth

    def link_out(depth):
        if depth == 0:
            return link
        return down_ref[depth - 1] if side == 0 else down_ref[rows - 1 - depth]

    def link_in(depth):
        return down_ref[depth] if side == 0 else down_ref[rows - 2 - depth]

    values = {-1: edge_x}
    for depth in range(reach + 1):
        values[depth] = x_ref[row_of(depth)]
    updates = {}
    for sweep in range(SWEEPS):
        found, changed = {}, {}
        if sweep < SWEEPS - 1:
            x = values[-1]
            flow = beside(x, edge_across) + link * values[0]
            found[-1], changed[-1] = relaxed(x, flow, edge_q[sweep], inverse_edge, updates.get(-1), sweep)
        for depth in range(sweep + reach):
            row = row_of(depth)
            x = values[depth]
            flow = beside(x, across_ref[row]) + link_out(depth) * values[depth - 1] + link_in(depth) * values[depth + 1]
            found[depth], changed[depth] = relaxed(x, flow, side_ref[row], inverse_ref[row], updates.get(depth), sweep)
        if sweep < SWEEPS - 1:
            slot = 3 * (2 * sweep + side)
            found[sweep + reach] = keep_ref[slot]
            changed[sweep + reach] = keep_ref[slot + 2]
            found[sweep + reach + 1] = keep_ref[slot + 1]
        values, updates = found, changed
    return {row_of(depth): value for depth, value in values.items()}


KEPT = 6 * (SWEEPS - 1)


def first_inner_kernel(
    single,
    rows,
    x_ref,
    across_ref,
    down_ref,
    loads_ref,
    own_ref,
    own_weight_ref,
    low_ref,
    above_ref,
    below_ref,
    first_ref,
    second_ref,
    after_ref,
    core_ref,
    side_ref,
    inverse_ref,
    keep_ref,
    halo_ref,
    picked_ref,
    *scratch,
):
    tile, _ = place()
    via, fixed, moving = via_terms(own_ref, own_weight_ref, low_ref, below_ref[1], above_ref[0], below_ref[0])
    top_x, low_x = taken_by_parity(first_ref, second_ref, 0)
    top_across, low_across = taken_by_parity(first_ref, second_ref, 1)
    link, _ = taken_by_parity(first_ref, second_ref, 2)
    link = jnp.where(tile == 0, 0.0, link)
    for slot, value in enumerate((top_across, low_across, link, top_x, low_x)):
        halo_ref[slot] = value
    for row in range(rows):
        side_ref[row] = fixed(row) + moving(row) - loads_ref[row]
        across = across_ref[row]
        diagonal = across + column_left(across) + down_ref[row] + via(row)
        diagonal = diagonal + (down_ref[row - 1] if row > 0 else link)
        inverse_ref[row] = 1.0 / diagonal
    outside = link * top_x, down_ref[rows - 1] * low_x
    shared = (x_ref, across_ref, down_ref, side_ref, inverse_ref)
    inner_rows(rows, 0, outside, *shared, scratch[:-1], scratch[-1], core_ref, keep_ref)
    for index, cells in enumerate(chosen(single, own_ref[...], low_ref[...])):
        total = jnp.zeros(cells.shape, jnp.float32)
        for row in range(SWEEPS - 1, rows - SWEEPS + 1):
            total = total + marked(cells, row, core_ref[row])
        picked_ref[index] = total


def first_outer_kernel(
    single,
    rows,
    x_ref,
    across_ref,
    down_ref,
    side_ref,
    inverse_ref,
    keep_ref,
    halo_ref,
    picked_ref,
    own_ref,
    low_ref,
    first_ref,
    second_ref,
    core_ref,
    next_ref,
    edge_ref,
    *sends,
):
    top_q0, low_q0 = taken_by_parity(first_ref, second_ref, 0)
    top_q1, low_q1 = taken_by_parity(first_ref, second_ref, 1)
    top_diag, low_diag = taken_by_parity(first_ref, second_ref, 2)
    link, low_link = halo_ref[2], down_ref[rows - 1]
    top_inverse = 1.0 / (top_diag + link)
    low_inverse = 1.0 / (low_diag + low_link)
    edge_ref[0] = top_inverse
    edge_ref[1] = low_inverse
    shared = (x_ref, across_ref, down_ref, side_ref, inverse_ref, keep_ref)
    outer = outer_rows(0, rows, 0, (halo_ref[3], (top_q0, top_q1), halo_ref[0]), link, top_inverse, *shared)
    outer.update(
        outer_rows(1, rows, 0, (halo_ref[4], (low_q0, low_q1), halo_ref[1]), low_link, low_inverse, *shared)
    )
    for row, value in outer.items():
        next_ref[row] = value
    for index, cells in enumerate(chosen(single, own_ref[...], low_ref[...])):
        total = picked_ref[index]
        for row, value in outer.items():
            total = total + marked(cells, row, value)
        sends[index][0] = total


def last_inner_kernel(
    rows,
    x_ref,
    across_ref,
    down_ref,
    loads_ref,
    inverse_ref,
    own_ref,
    own_weight_ref,
    low_ref,
    weight_ref,
    above_ref,
    below_ref,
    after_ref,
    core_ref,
    side_ref,
    keep_ref,
    *scratch,
):
    _, fixed, moving = via_terms(own_ref, own_weight_ref, low_ref, weight_ref[1], above_ref[0], below_ref[0])
    for row in range(rows):
        side_ref[row] = fixed(row) + moving(row) - loads_ref[row]
    shared = (x_ref, across_ref, down_ref, side_ref, inverse_ref)
    inner_rows(rows, 1, None, *shared, scratch[:-1], scratch[-1], core_ref, keep_ref)


def last_outer_kernel(
    single,
    rows,
    x_ref,
    across_ref,
    down_ref,
    side_ref,
    inverse_ref,
    keep_ref,
    halo_ref,
    edge_ref,
    early_first_ref,
    early_second_ref,
    first_ref,
    second_ref,
    core_ref,
    out_ref,
    next_ref,
    held,
    sems,
):
    early = [taken_by_parity(early_first_ref, early_second_ref, slot) for slot in range(4 if single else 3)]
    late = [taken_by_parity(first_ref, second_ref, slot) for slot in range(1 if single else 2)]
    leaving = []
    for side in range(2):
        if single:
            changes = early[3][side] * late[0][side], late[0][side]
        else:
            changes = late[0][side], late[1][side]
        sides = early[1][side] + changes[0], early[2][side] + changes[1]
        outer = outer_rows(
            side,
            rows,
            1,
            (early[0][side], sides, halo_ref[side]),
            halo_ref[2] if side == 0 else down_ref[rows - 1],
            edge_ref[side],
            *(x_ref, across_ref, down_ref, side_ref, inverse_ref, keep_ref),
        )
        for row, value in outer.items():
            next_ref[row] = value
        half = rows // 2
        for first, width in chunks_of(held.shape[1], CHUNKS):
            for top in range(side * half, side * half + half, 8):
                for start in range(first, first + width, LANES):
                    held[pl.ds(top, 8), pl.ds(start, LANES)] = next_ref[pl.ds(top, 8), start // LANES, :]
            part = pl.ds(side * half, half), pl.ds(first, width)
            copy = pltpu.make_async_copy(held.at[part], out_ref.at[part], sems.at[len(leaving)])
            copy.start()
            leaving.append(copy)
    for copy in leaving:
        copy.wait()


def call(kernel, name, ins, outs, scratch=(), aliases=None, work=None):
    spaces = {"vmem": pltpu.VMEM, "hbm": pltpu.HBM, "any": pl.ANY}
    return pl.pallas_call(
        kernel,
        out_shape=[jax.ShapeDtypeStruct(shape, *(kind or [jnp.float32])) for _, shape, *kind in outs],
        in_specs=[pl.BlockSpec(memory_space=spaces[space]) for space, _ in ins],
        out_specs=[pl.BlockSpec(memory_space=spaces[space]) for space, *_ in outs],
        scratch_shapes=list(scratch),
        input_output_aliases=aliases or {},
        compiler_params=pltpu.CompilerParams(vmem_limit_bytes=40 * 1024 * 1024),
        cost_estimate=work and pl.CostEstimate(flops=work, bytes_accessed=work, transcendentals=0),
        name=name,
    )(*(array for _, array in ins))


def routes(tiles, layers):
    def at(tile, layer):
        return tile * layers + layer % layers

    everywhere = [(tile, layer) for tile in range(tiles) for layer in range(layers)]
    up = [(at(t, l), at(t, l + 1)) for t, l in everywhere]
    down = [(at(t, l), at(t, l - 1)) for t, l in everywhere]
    first, second = [], []
    for t, l in everywhere:
        first.append((at(t, l), at(t ^ 1, l)))
        beyond = t + 1 if t % 2 else t - 1
        if 0 <= beyond < tiles:
            second.append((at(t, l), at(beyond, l)))
        else:
            second.append((at(t, l), at(t, l + 1)))
    return up, down, first, second


def local(class_index, class_conductance, loads, start_volts, via_cells, via_counts):
    rows, cols = loads.shape[1:]
    lines = cols // LANES
    tiles, layers = lax.axis_size("tile"), lax.axis_size("layer")
    up, down, first, second = routes(tiles, layers)
    single = layers == 2
    move = functools.partial(lax.ppermute, axis_name=("tile", "layer"))

    def rows_of(count):
        return (count, lines, LANES)

    def vmem(*arrays):
        return [("vmem", array) for array in arrays]

    def between_layers(sends):
        if single:
            got = move(sends[0], perm=up)
            return got, got
        return move(sends[1], perm=down), move(sends[0], perm=up)

    def beside_tile(sent):
        across_chips = move(sent[1], perm=second)
        return move(sent[0], perm=first), across_chips

    field = ("vmem", rows_of(rows))
    work = [pltpu.VMEM(rows_of(rows), jnp.float32)] * SWEEPS
    pick_count = 1 if single else 2
    picks = [("vmem", rows_of(1))] * pick_count

    cells = via_cells.reshape(lines, LANES)
    counts = via_counts.reshape(lines, LANES)
    low = move(cells, perm=up)
    table = jnp.pad(class_conductance, ((0, 0), (0, LANES - class_conductance.shape[1])))
    across, downward = call(unpack_index_kernel, "unpack_index", vmem(class_index, table), [field] * 2)
    (x,) = call(unpack_field_kernel, "unpack_volts", vmem(start_volts), [field])
    *still, own, own_weight = call(
        still_edges_kernel,
        "still_edges",
        vmem(x, across, downward, cells, counts),
        [("vmem", rows_of(3))] * 2 + [("vmem", cells.shape, cells.dtype), ("vmem", cells.shape)],
    )
    vias = (own, own_weight, low)
    sends = call(
        functools.partial(links_kernel, single, rows),
        "links",
        vmem(x, *vias) + [("any", still[0])],
        [("vmem", rows_of(2))] if single else [("vmem", rows_of(2)), ("vmem", rows_of(1))],
    )
    above, below = between_layers(sends)
    weights = below
    (load,) = call(unpack_field_kernel, "unpack_loads", vmem(loads), [field])
    early = beside_tile(still)
    sent = call(
        functools.partial(first_edges_kernel, rows),
        "first_edges",
        vmem(x, across, downward, load, *vias, above, below),
        [("vmem", rows_of(3))] * 2,
    )
    got = beside_tile(sent)
    core, side, inverse, keep, halo, picked = call(
        functools.partial(first_inner_kernel, single, rows),
        "first_inner",
        vmem(x, across, downward, load, *vias, above, below, *early) + [("any", sent[1])],
        [field, field, field, ("vmem", rows_of(KEPT)), ("vmem", rows_of(5)), ("vmem", rows_of(pick_count))],
        work,
    )
    x, edge, *sends = call(
        functools.partial(first_outer_kernel, single, rows),
        "first_outer",
        vmem(x, across, downward, side, inverse, keep, halo, picked, own, low, *got, core),
        [field, ("vmem", rows_of(2))] + picks,
        aliases={12: 0},
    )
    above, below = between_layers(sends)
    early_rows, late_rows = (4, 1) if single else (3, 2)
    sent = call(
        functools.partial(next_early_kernel, single, rows),
        "next_early",
        vmem(x, across, downward, load, inverse, *vias, weights) + [("any", sends[0])],
        [("vmem", rows_of(early_rows))] * 2 + [("vmem", rows_of(1))] * (2 if single else 0),
    )
    early = beside_tile(sent[:2])
    if single:
        late = call(
            next_late_single_kernel,
            "next_late",
            vmem(*sent[2:], above),
            [("vmem", rows_of(late_rows))] * 2,
            work=2 * 10**10,
        )
    else:
        late = call(
            functools.partial(next_late_kernel, rows),
            "next_late",
            vmem(downward, inverse, *vias, weights, above, below),
            [("vmem", rows_of(late_rows))] * 2,
            work=2 * 10**10,
        )
    got = beside_tile(late)
    core, side, keep = call(
        functools.partial(last_inner_kernel, rows),
        "last_inner",
        vmem(x, across, downward, load, inverse, *vias, weights, above, below) + [("any", late[1])],
        [field, field, ("vmem", rows_of(KEPT))],
        work,
    )
    volts, _ = call(
        functools.partial(last_outer_kernel, single, rows),
        "last_outer",
        vmem(x, across, downward, side, inverse, keep, halo, edge, *early, *got, core),
        [("hbm", (rows, cols)), field],
        [pltpu.VMEM((rows, cols), jnp.float32), pltpu.SemaphoreType.DMA((2 * CHUNKS,))],
        aliases={12: 1},
    )
    return volts[None]


def solution(mesh):
    placed = (
        P("layer", None, "tile", None),
        P("layer", None),
        P("layer", "tile", None),
        P("layer", "tile", None),
        P("layer", "tile"),
        P("layer", "tile"),
    )
    return jax.shard_map(
        local, mesh=mesh, in_specs=placed, out_specs=P("layer", "tile", None), check_vma=False
    )
```

```python
import functools

import jax
import jax.numpy as jnp
from jax import lax
from jax.experimental import pallas as pl
from jax.experimental.pallas import tpu as pltpu
from jax.sharding import PartitionSpec as P

OUTER = 2
SWEEPS = 3
VIA_UNIT = 2.0
LOWER_BOUND = 0.05
UPPER_BOUND = 2.0
LANES = 128
CHUNKS = 2
FILL = 8


def chebyshev_terms(count):
    centre_value = 0.5 * (UPPER_BOUND + LOWER_BOUND)
    half_width = 0.5 * (UPPER_BOUND - LOWER_BOUND)
    sigma = centre_value / half_width
    rho_last = 1.0 / sigma
    terms = [(0.0, 1.0 / centre_value)]
    for index in range(1, count):
        rho_next = 1.0 / (2.0 * sigma - rho_last)
        terms.append((rho_next * rho_last, 2.0 * rho_next / half_width))
        rho_last = rho_next
    return terms


FACTORS = chebyshev_terms(SWEEPS)


def column_right(row):
    lane = lax.broadcasted_iota(jnp.int32, row.shape, 1)
    turned = pltpu.roll(row, LANES - 1, 1)
    return jnp.where(lane == LANES - 1, pltpu.roll(turned, row.shape[0] - 1, 0), turned)


def column_left(row):
    lane = lax.broadcasted_iota(jnp.int32, row.shape, 1)
    turned = pltpu.roll(row, 1, 1)
    return jnp.where(lane == 0, pltpu.roll(turned, 1, 0), turned)


def beside(x, across):
    return across * column_right(x) + column_left(across * x)


def place():
    return lax.axis_index("tile"), lax.axis_index("layer")


def marked(cells, row, value):
    return jnp.where(cells == row, value, 0.0)


def pick(x_ref, cells, rows):
    total = jnp.zeros(cells.shape, jnp.float32)
    for row in range(rows):
        total = total + marked(cells, row, x_ref[row])
    return total


def chunks_of(cols, count):
    width = cols // count
    return [(first, width) for first in range(0, cols, width)]


def unpack_field_kernel(field_ref, out_ref):
    rows, cols = field_ref.shape[1:]
    for top in range(0, rows, 8):
        for start in range(0, cols, LANES):
            out_ref[pl.ds(top, 8), start // LANES, :] = field_ref[0, pl.ds(top, 8), pl.ds(start, LANES)]


def unpack_index_kernel(index_ref, table_ref, across_ref, down_ref):
    rows, cols = index_ref.shape[2:]
    tile, _ = place()
    last_tile = tile == lax.axis_size("tile") - 1
    table = jnp.broadcast_to(table_ref[...], (8, LANES))
    lane = lax.broadcasted_iota(jnp.int32, (8, LANES), 1)
    sub = lax.broadcasted_iota(jnp.int32, (8, LANES), 0)
    for top in range(0, rows, 8):
        part = pl.ds(top, 8)
        for start in range(0, cols, LANES):
            here, line = pl.ds(start, LANES), start // LANES
            across = jnp.take_along_axis(table, index_ref[0, 0, part, here], axis=1, mode="promise_in_bounds")
            if start + LANES == cols:
                across = jnp.where(lane == LANES - 1, 0.0, across)
            across_ref[part, line, :] = across
            down = jnp.take_along_axis(table, index_ref[0, 1, part, here], axis=1, mode="promise_in_bounds")
            if top + 8 == rows:
                down = jnp.where((sub == 7) & last_tile, 0.0, down)
            down_ref[part, line, :] = down


def via_terms(own_ref, own_weight_ref, low_ref, low_weight, from_above, from_below):
    _, layer = place()
    on_top = layer == lax.axis_size("layer") - 1
    own_weight = own_weight_ref[...]
    low_weight = jnp.where(layer == 0, 0.0, low_weight)
    fixed_source = jnp.where(on_top, own_weight, 0.0)
    own, low = own_ref[...], low_ref[...]

    def via(row):
        return marked(own, row, own_weight) + marked(low, row, low_weight)

    def fixed(row):
        return marked(own, row, fixed_source)

    if from_above is None:
        return via, fixed, None
    own_source = jnp.where(on_top, 0.0, own_weight * from_above)
    low_source = low_weight * from_below

    def moving(row):
        return marked(own, row, own_source) + marked(low, row, low_source)

    return via, fixed, moving


def send_by_parity(first_ref, second_ref, slot, top, bottom):
    tile, _ = place()
    even = lax.rem(tile, 2) == 0
    part = pl.ds(slot * top.shape[0], top.shape[0])
    first_ref[part] = jnp.where(even, bottom, top)
    second_ref[part] = jnp.where(even, top, bottom)
    lengths = first_ref.shape[0], second_ref.shape[0]
    if slot == 0:
        longer = first_ref if lengths[0] > lengths[1] else second_ref
        longer[pl.ds(min(lengths), FILL)] = jnp.zeros((FILL, LANES), jnp.float32)


def taken_by_parity(first_ref, second_ref, slot, lines):
    tile, _ = place()
    even = lax.rem(tile, 2) == 0
    part = pl.ds(slot * lines, lines)
    first, second = first_ref[part], second_ref[part]
    return jnp.where(even, second, first), jnp.where(even, first, second)


def edge_flow(x_ref, across_ref, down_ref, row):
    return beside(x_ref[row], across_ref[row]) + down_ref[row] * x_ref[row + 1] + down_ref[row - 1] * x_ref[row - 1]


def edge_ends(rows):
    return (0, 1, 0), (rows - 1, rows - 2, rows - 2)


def edges(x_ref, across_ref, down_ref, right_side, inverses, rows):
    found = []
    for (edge, within, link), inverse in zip(edge_ends(rows), inverses):
        x = x_ref[within]
        flow = edge_flow(x_ref, across_ref, down_ref, within)
        later = x + FACTORS[0][1] * (inverse * (right_side(within) + flow) - x)
        found.append((right_side(edge) + down_ref[link] * x, right_side(edge) + down_ref[link] * later))
    return tuple(zip(*found))


def links_kernel(
    single, x_ref, across_ref, down_ref, own_ref, count_ref, low_ref, first_ref, second_ref, weight_ref, cells_ref, *sends
):
    rows = x_ref.shape[0]
    own, low = own_ref[...], low_ref[...]
    weight = VIA_UNIT * count_ref[...].astype(jnp.float32)
    cells_ref[...] = own
    weight_ref[...] = weight
    links = chosen(single, own, low)
    for send_ref, cells in zip(sends, links):
        send_ref[0] = pick(x_ref, cells, rows)
    sends[0][1] = weight
    for slot, ref in enumerate((x_ref, across_ref, down_ref)):
        send_by_parity(first_ref, second_ref, slot, ref[0], ref[rows - 1])
    if single:
        send_by_parity(first_ref, second_ref, 3, marked(links[0], 0, 1.0), marked(links[0], rows - 1, 1.0))


def first_edges_kernel(
    rows, x_ref, across_ref, down_ref, loads_ref, own_ref, own_weight_ref, low_ref, above_ref, below_ref, first_ref, second_ref
):
    via, fixed, moving = via_terms(own_ref, own_weight_ref, low_ref, below_ref[1], above_ref[0], below_ref[0])

    def right_side(row):
        return fixed(row) + moving(row) - loads_ref[row]

    def diagonal(row, links):
        across = across_ref[row]
        total = across + column_left(across)
        for link in links:
            total = total + down_ref[link]
        return total + via(row)

    inverses = 1.0 / diagonal(1, (0, 1)), 1.0 / diagonal(rows - 2, (rows - 3, rows - 2))
    for slot, pair in enumerate(edges(x_ref, across_ref, down_ref, right_side, inverses, rows)):
        send_by_parity(first_ref, second_ref, slot, *pair)
    send_by_parity(first_ref, second_ref, 2, diagonal(0, (0,)), diagonal(rows - 1, (rows - 2,)))


def next_early_kernel(
    single,
    rows,
    x_ref,
    across_ref,
    down_ref,
    loads_ref,
    inverse_ref,
    own_ref,
    own_weight_ref,
    low_ref,
    weight_ref,
    after_ref,
    first_ref,
    second_ref,
    *factor_refs,
):
    _, layer = place()
    _, fixed, _ = via_terms(own_ref, own_weight_ref, low_ref, weight_ref[1], None, None)

    def right_side(row):
        return fixed(row) - loads_ref[row]

    send_by_parity(first_ref, second_ref, 0, x_ref[0], x_ref[rows - 1])
    inverses = inverse_ref[1], inverse_ref[rows - 2]
    for slot, pair in enumerate(edges(x_ref, across_ref, down_ref, right_side, inverses, rows)):
        send_by_parity(first_ref, second_ref, 1 + slot, *pair)
    if single:
        cells = jnp.where(layer == 0, own_ref[...], low_ref[...])
        weight = jnp.where(layer == 0, own_weight_ref[...], weight_ref[1])
        factors = []
        for (edge, within, link), inverse in zip(edge_ends(rows), inverses):
            share = FACTORS[0][1] * inverse * down_ref[link]
            factors.append(marked(cells, edge, weight) + marked(cells, within, weight * share))
        for ref, factor in zip(factor_refs, factors):
            ref[...] = factor


def next_late_kernel(
    rows, down_ref, inverse_ref, own_ref, own_weight_ref, low_ref, weight_ref, above_ref, below_ref, first_ref, second_ref
):
    _, _, moving = via_terms(own_ref, own_weight_ref, low_ref, weight_ref[1], above_ref[0], below_ref[0])
    found = []
    for edge, within, link in edge_ends(rows):
        change = moving(edge)
        share = FACTORS[0][1] * inverse_ref[within] * down_ref[link]
        found.append((change, change + share * moving(within)))
    for slot, pair in enumerate(zip(*found)):
        send_by_parity(first_ref, second_ref, slot, *pair)


def next_late_single_kernel(top_ref, bottom_ref, volts_ref, first_ref, second_ref):
    volts = volts_ref[0]
    send_by_parity(first_ref, second_ref, 0, top_ref[...] * volts, bottom_ref[...] * volts)


def relaxed(x, flow, side, inverse, previous, sweep):
    keep, gain = FACTORS[sweep]
    update = gain * (inverse * (side + flow) - x)
    if sweep > 0:
        update = update + keep * previous
    return x + update, update


def chosen(single, own, low):
    _, layer = place()
    return [jnp.where(layer == 0, own, low)] if single else [own, low]


def inner_rows(
    rows, reach, outside, x_ref, across_ref, down_ref, side_ref, inverse_ref, work, update_ref, core_ref, keep_ref
):
    sources = [x_ref, *work]
    targets = [*work, core_ref]
    for sweep in range(SWEEPS):
        source, target = sources[sweep], targets[sweep]
        for row in range(sweep + reach, rows - sweep - reach):
            x = source[row]
            flow = beside(x, across_ref[row])
            if row == 0:
                flow = flow + outside[0]
            else:
                flow = flow + down_ref[row - 1] * source[row - 1]
            if row == rows - 1:
                flow = flow + outside[1]
            else:
                flow = flow + down_ref[row] * source[row + 1]
            previous = update_ref[row] if sweep > 0 else None
            value, update = relaxed(x, flow, side_ref[row], inverse_ref[row], previous, sweep)
            target[row] = value
            if sweep < SWEEPS - 1:
                update_ref[row] = update
                for side, depth in ((0, row), (1, rows - 1 - row)):
                    slot = 3 * (2 * sweep + side)
                    if depth == sweep + reach:
                        keep_ref[slot] = value
                        keep_ref[slot + 2] = update
                    if depth == sweep + reach + 1:
                        keep_ref[slot + 1] = value


def outer_rows(side, rows, reach, halo, link, inverse_edge, x_ref, across_ref, down_ref, side_ref, inverse_ref, keep_ref):
    edge_x, edge_q, edge_across = halo

    def row_of(depth):
        return depth if side == 0 else rows - 1 - depth

    def link_out(depth):
        if depth == 0:
            return link
        return down_ref[depth - 1] if side == 0 else down_ref[rows - 1 - depth]

    def link_in(depth):
        return down_ref[depth] if side == 0 else down_ref[rows - 2 - depth]

    values = {-1: edge_x}
    for depth in range(reach + 1):
        values[depth] = x_ref[row_of(depth)]
    updates = {}
    for sweep in range(SWEEPS):
        found, changed = {}, {}
        if sweep < SWEEPS - 1:
            x = values[-1]
            flow = beside(x, edge_across) + link * values[0]
            found[-1], changed[-1] = relaxed(x, flow, edge_q[sweep], inverse_edge, updates.get(-1), sweep)
        for depth in range(sweep + reach):
            row = row_of(depth)
            x = values[depth]
            flow = beside(x, across_ref[row]) + link_out(depth) * values[depth - 1] + link_in(depth) * values[depth + 1]
            found[depth], changed[depth] = relaxed(x, flow, side_ref[row], inverse_ref[row], updates.get(depth), sweep)
        if sweep < SWEEPS - 1:
            slot = 3 * (2 * sweep + side)
            found[sweep + reach] = keep_ref[slot]
            changed[sweep + reach] = keep_ref[slot + 2]
            found[sweep + reach + 1] = keep_ref[slot + 1]
        values, updates = found, changed
    return {row_of(depth): value for depth, value in values.items()}


KEPT = 6 * (SWEEPS - 1)


def first_inner_kernel(
    single,
    rows,
    x_ref,
    across_ref,
    down_ref,
    loads_ref,
    own_ref,
    own_weight_ref,
    low_ref,
    above_ref,
    below_ref,
    first_ref,
    second_ref,
    after_ref,
    core_ref,
    side_ref,
    inverse_ref,
    keep_ref,
    halo_ref,
    picked_ref,
    *scratch,
):
    tile, _ = place()
    via, fixed, moving = via_terms(own_ref, own_weight_ref, low_ref, below_ref[1], above_ref[0], below_ref[0])
    top_x, low_x = taken_by_parity(first_ref, second_ref, 0, x_ref.shape[1])
    top_across, low_across = taken_by_parity(first_ref, second_ref, 1, x_ref.shape[1])
    link, _ = taken_by_parity(first_ref, second_ref, 2, x_ref.shape[1])
    link = jnp.where(tile == 0, 0.0, link)
    held = [top_across, low_across, link, top_x, low_x]
    if single:
        held.extend(taken_by_parity(first_ref, second_ref, 3, x_ref.shape[1]))
    for slot, value in enumerate(held):
        halo_ref[slot] = value
    for row in range(rows):
        side_ref[row] = fixed(row) + moving(row) - loads_ref[row]
        across = across_ref[row]
        diagonal = across + column_left(across) + down_ref[row] + via(row)
        diagonal = diagonal + (down_ref[row - 1] if row > 0 else link)
        inverse_ref[row] = 1.0 / diagonal
    outside = link * top_x, down_ref[rows - 1] * low_x
    shared = (x_ref, across_ref, down_ref, side_ref, inverse_ref)
    inner_rows(rows, 0, outside, *shared, scratch[:-1], scratch[-1], core_ref, keep_ref)
    for index, cells in enumerate(chosen(single, own_ref[...], low_ref[...])):
        total = jnp.zeros(cells.shape, jnp.float32)
        for row in range(SWEEPS - 1, rows - SWEEPS + 1):
            total = total + marked(cells, row, core_ref[row])
        picked_ref[index] = total


def first_outer_kernel(
    single,
    rows,
    x_ref,
    across_ref,
    down_ref,
    side_ref,
    inverse_ref,
    keep_ref,
    halo_ref,
    picked_ref,
    own_ref,
    low_ref,
    first_ref,
    second_ref,
    core_ref,
    next_ref,
    edge_ref,
    *sends,
):
    top_q0, low_q0 = taken_by_parity(first_ref, second_ref, 0, x_ref.shape[1])
    top_q1, low_q1 = taken_by_parity(first_ref, second_ref, 1, x_ref.shape[1])
    top_diag, low_diag = taken_by_parity(first_ref, second_ref, 2, x_ref.shape[1])
    link, low_link = halo_ref[2], down_ref[rows - 1]
    top_inverse = 1.0 / (top_diag + link)
    low_inverse = 1.0 / (low_diag + low_link)
    edge_ref[0] = top_inverse
    edge_ref[1] = low_inverse
    shared = (x_ref, across_ref, down_ref, side_ref, inverse_ref, keep_ref)
    outer = outer_rows(0, rows, 0, (halo_ref[3], (top_q0, top_q1), halo_ref[0]), link, top_inverse, *shared)
    outer.update(
        outer_rows(1, rows, 0, (halo_ref[4], (low_q0, low_q1), halo_ref[1]), low_link, low_inverse, *shared)
    )
    for row, value in outer.items():
        next_ref[row] = value
    for index, cells in enumerate(chosen(single, own_ref[...], low_ref[...])):
        total = picked_ref[index]
        for row, value in outer.items():
            total = total + marked(cells, row, value)
        sends[index][0] = total


def last_inner_kernel(
    rows,
    x_ref,
    across_ref,
    down_ref,
    loads_ref,
    inverse_ref,
    own_ref,
    own_weight_ref,
    low_ref,
    weight_ref,
    above_ref,
    below_ref,
    after_ref,
    core_ref,
    side_ref,
    keep_ref,
    *scratch,
):
    _, fixed, moving = via_terms(own_ref, own_weight_ref, low_ref, weight_ref[1], above_ref[0], below_ref[0])
    for row in range(rows):
        side_ref[row] = fixed(row) + moving(row) - loads_ref[row]
    shared = (x_ref, across_ref, down_ref, side_ref, inverse_ref)
    inner_rows(rows, 1, None, *shared, scratch[:-1], scratch[-1], core_ref, keep_ref)


def last_outer_kernel(
    single,
    rows,
    x_ref,
    across_ref,
    down_ref,
    side_ref,
    inverse_ref,
    keep_ref,
    halo_ref,
    edge_ref,
    early_first_ref,
    early_second_ref,
    first_ref,
    second_ref,
    core_ref,
    out_ref,
    next_ref,
    held,
    sems,
):
    lines = x_ref.shape[1]
    early = [taken_by_parity(early_first_ref, early_second_ref, slot, lines) for slot in range(3)]
    late = [taken_by_parity(first_ref, second_ref, slot, lines) for slot in range(1 if single else 2)]
    leaving = []
    for side in range(2):
        if single:
            changes = halo_ref[5 + side] * late[0][side], late[0][side]
        else:
            changes = late[0][side], late[1][side]
        sides = early[1][side] + changes[0], early[2][side] + changes[1]
        outer = outer_rows(
            side,
            rows,
            1,
            (early[0][side], sides, halo_ref[side]),
            halo_ref[2] if side == 0 else down_ref[rows - 1],
            edge_ref[side],
            *(x_ref, across_ref, down_ref, side_ref, inverse_ref, keep_ref),
        )
        for row, value in outer.items():
            next_ref[row] = value
        half = rows // 2
        for first, width in chunks_of(held.shape[1], CHUNKS):
            for top in range(side * half, side * half + half, 8):
                for start in range(first, first + width, LANES):
                    held[pl.ds(top, 8), pl.ds(start, LANES)] = next_ref[pl.ds(top, 8), start // LANES, :]
            part = pl.ds(side * half, half), pl.ds(first, width)
            copy = pltpu.make_async_copy(held.at[part], out_ref.at[part], sems.at[len(leaving)])
            copy.start()
            leaving.append(copy)
    for copy in leaving:
        copy.wait()


def call(kernel, name, ins, outs, scratch=(), aliases=None, work=None):
    spaces = {"vmem": pltpu.VMEM, "hbm": pltpu.HBM, "any": pl.ANY}
    return pl.pallas_call(
        kernel,
        out_shape=[jax.ShapeDtypeStruct(shape, *(kind or [jnp.float32])) for _, shape, *kind in outs],
        in_specs=[pl.BlockSpec(memory_space=spaces[space]) for space, _ in ins],
        out_specs=[pl.BlockSpec(memory_space=spaces[space]) for space, *_ in outs],
        scratch_shapes=list(scratch),
        input_output_aliases=aliases or {},
        compiler_params=pltpu.CompilerParams(vmem_limit_bytes=40 * 1024 * 1024),
        cost_estimate=work and pl.CostEstimate(flops=work, bytes_accessed=work, transcendentals=0),
        name=name,
    )(*(array for _, array in ins))


def routes(tiles, layers):
    def at(tile, layer):
        return tile * layers + layer % layers

    everywhere = [(tile, layer) for tile in range(tiles) for layer in range(layers)]
    up = [(at(t, l), at(t, l + 1)) for t, l in everywhere]
    down = [(at(t, l), at(t, l - 1)) for t, l in everywhere]
    first, second = [], []
    for t, l in everywhere:
        first.append((at(t, l), at(t ^ 1, l)))
        beyond = t + 1 if t % 2 else t - 1
        if 0 <= beyond < tiles:
            second.append((at(t, l), at(beyond, l)))
        else:
            second.append((at(t, l), at(t, l + 1)))
    return up, down, first, second


def local(class_index, class_conductance, loads, start_volts, via_cells, via_counts):
    rows, cols = loads.shape[1:]
    lines = cols // LANES
    tiles, layers = lax.axis_size("tile"), lax.axis_size("layer")
    up, down, first, second = routes(tiles, layers)
    single = layers == 2
    move = functools.partial(lax.ppermute, axis_name=("tile", "layer"))

    def rows_of(count):
        return (count, lines, LANES)

    def messages(count, longer):
        return [("vmem", (count * lines + (FILL if longer == side else 0), LANES)) for side in range(2)]

    def vmem(*arrays):
        return [("vmem", array) for array in arrays]

    def between_layers(sends):
        if single:
            got = move(sends[0], perm=up)
            return got, got
        return move(sends[1], perm=down), move(sends[0], perm=up)

    def beside_tile(sent):
        across_chips = move(sent[1], perm=second)
        return move(sent[0], perm=first), across_chips

    field = ("vmem", rows_of(rows))
    work = [pltpu.VMEM(rows_of(rows), jnp.float32)] * SWEEPS
    pick_count = 1 if single else 2
    picks = [("vmem", rows_of(1))] * pick_count

    cells = via_cells.reshape(lines, LANES)
    counts = via_counts.reshape(lines, LANES)
    low = move(cells, perm=up)
    table = jnp.pad(class_conductance, ((0, 0), (0, LANES - class_conductance.shape[1])))
    across, downward = call(unpack_index_kernel, "unpack_index", vmem(class_index, table), [field] * 2)
    (x,) = call(unpack_field_kernel, "unpack_volts", vmem(start_volts), [field])
    first_sent, second_sent, own_weight, own, *sends = call(
        functools.partial(links_kernel, single),
        "links",
        vmem(x, across, downward, cells, counts, low),
        messages(4 if single else 3, 0)
        + [("vmem", cells.shape), ("vmem", cells.shape, cells.dtype), ("vmem", rows_of(2))]
        + ([] if single else [("vmem", rows_of(1))]),
    )
    vias = (own, own_weight, low)
    above, below = between_layers(sends)
    weights = below
    (load,) = call(unpack_field_kernel, "unpack_loads", vmem(loads), [field])
    early = beside_tile((first_sent, second_sent))
    sent = call(
        functools.partial(first_edges_kernel, rows),
        "first_edges",
        vmem(x, across, downward, load, *vias, above, below),
        messages(3, 1),
        work=2 * 10**10,
    )
    got = beside_tile(sent)
    core, side, inverse, keep, halo, picked = call(
        functools.partial(first_inner_kernel, single, rows),
        "first_inner",
        vmem(x, across, downward, load, *vias, above, below, *early) + [("any", sent[1])],
        [field, field, field, ("vmem", rows_of(KEPT)), ("vmem", rows_of(7 if single else 5)), ("vmem", rows_of(pick_count))],
        work,
    )
    x, edge, *sends = call(
        functools.partial(first_outer_kernel, single, rows),
        "first_outer",
        vmem(x, across, downward, side, inverse, keep, halo, picked, own, low, *got, core),
        [field, ("vmem", rows_of(2))] + picks,
        aliases={12: 0},
    )
    above, below = between_layers(sends)
    sent = call(
        functools.partial(next_early_kernel, single, rows),
        "next_early",
        vmem(x, across, downward, load, inverse, *vias, weights) + [("any", sends[0])],
        messages(3, 0) + [("vmem", cells.shape)] * (2 if single else 0),
    )
    early = beside_tile(sent[:2])
    if single:
        late = call(
            next_late_single_kernel,
            "next_late",
            vmem(*sent[2:], above),
            messages(1, 1),
            work=2 * 10**10,
        )
    else:
        late = call(
            functools.partial(next_late_kernel, rows),
            "next_late",
            vmem(downward, inverse, *vias, weights, above, below),
            messages(2, 1),
            work=2 * 10**10,
        )
    got = beside_tile(late)
    core, side, keep = call(
        functools.partial(last_inner_kernel, rows),
        "last_inner",
        vmem(x, across, downward, load, inverse, *vias, weights, above, below) + [("any", late[1])],
        [field, field, ("vmem", rows_of(KEPT))],
        work,
    )
    volts, _ = call(
        functools.partial(last_outer_kernel, single, rows),
        "last_outer",
        vmem(x, across, downward, side, inverse, keep, halo, edge, *early, *got, core),
        [("hbm", (rows, cols)), field],
        [pltpu.VMEM((rows, cols), jnp.float32), pltpu.SemaphoreType.DMA((2 * CHUNKS,))],
        aliases={12: 1},
    )
    return volts[None]


def solution(mesh):
    placed = (
        P("layer", None, "tile", None),
        P("layer", None),
        P("layer", "tile", None),
        P("layer", "tile", None),
        P("layer", "tile"),
        P("layer", "tile"),
    )
    return jax.shard_map(
        local, mesh=mesh, in_specs=placed, out_specs=P("layer", "tile", None), check_vma=False
    )
```

```python
import functools

import jax
import jax.numpy as jnp
from jax import lax
from jax.experimental import pallas as pl
from jax.experimental.pallas import tpu as pltpu
from jax.sharding import PartitionSpec as P

OUTER = 2
SWEEPS = 3
VIA_UNIT = 2.0
LOWER_BOUND = 0.05
UPPER_BOUND = 2.0
LANES = 128
CHUNKS = 4
FILL = 8


def chebyshev_terms(count):
    centre_value = 0.5 * (UPPER_BOUND + LOWER_BOUND)
    half_width = 0.5 * (UPPER_BOUND - LOWER_BOUND)
    sigma = centre_value / half_width
    rho_last = 1.0 / sigma
    terms = [(0.0, 1.0 / centre_value)]
    for index in range(1, count):
        rho_next = 1.0 / (2.0 * sigma - rho_last)
        terms.append((rho_next * rho_last, 2.0 * rho_next / half_width))
        rho_last = rho_next
    return terms


FACTORS = chebyshev_terms(SWEEPS)


def column_right(row):
    lane = lax.broadcasted_iota(jnp.int32, row.shape, 1)
    turned = pltpu.roll(row, LANES - 1, 1)
    return jnp.where(lane == LANES - 1, pltpu.roll(turned, row.shape[0] - 1, 0), turned)


def column_left(row):
    lane = lax.broadcasted_iota(jnp.int32, row.shape, 1)
    turned = pltpu.roll(row, 1, 1)
    return jnp.where(lane == 0, pltpu.roll(turned, 1, 0), turned)


def beside(x, across):
    return across * column_right(x) + column_left(across * x)


def place():
    return lax.axis_index("tile"), lax.axis_index("layer")


def marked(cells, row, value):
    return jnp.where(cells == row, value, 0.0)


def pick(x_ref, cells, rows):
    total = jnp.zeros(cells.shape, jnp.float32)
    for row in range(rows):
        total = total + marked(cells, row, x_ref[row])
    return total


def chunks_of(cols, count):
    width = cols // count
    return [(first, width) for first in range(0, cols, width)]


def unpack_field_kernel(field_ref, out_ref):
    rows, cols = field_ref.shape[1:]
    for top in range(0, rows, 8):
        for start in range(0, cols, LANES):
            out_ref[pl.ds(top, 8), start // LANES, :] = field_ref[0, pl.ds(top, 8), pl.ds(start, LANES)]


def unpack_volts_kernel(volts_ref, class_ref, x_ref, table_ref, held, class_held, sems):
    rows, cols = held.shape
    chunks = chunks_of(cols, CHUNKS)
    pairs = [(volts_ref.at[0, :, pl.ds(*chunk)], held.at[:, pl.ds(*chunk)]) for chunk in chunks]
    pairs.append((class_ref, class_held))
    arriving = [pltpu.make_async_copy(*pair, sems.at[number]) for number, pair in enumerate(pairs)]
    for copy in arriving:
        copy.start()
    for (first, width), copy in zip(chunks, arriving):
        copy.wait()
        for top in range(0, rows, 8):
            part = pl.ds(top, 8)
            for start in range(first, first + width, LANES):
                x_ref[part, start // LANES, :] = held[part, pl.ds(start, LANES)]
    arriving[-1].wait()
    table_ref[...] = jnp.zeros(table_ref.shape, jnp.float32)
    count = class_held.shape[1]
    table_ref[:, pl.ds(0, count)] = jnp.broadcast_to(class_held[...], (8, count))


def unpack_index_kernel(index_ref, table_ref, across_ref, down_ref):
    rows, cols = index_ref.shape[2:]
    tile, _ = place()
    last_tile = tile == lax.axis_size("tile") - 1
    table = table_ref[...]
    lane = lax.broadcasted_iota(jnp.int32, (8, LANES), 1)
    sub = lax.broadcasted_iota(jnp.int32, (8, LANES), 0)
    for top in range(0, rows, 8):
        part = pl.ds(top, 8)
        for start in range(0, cols, LANES):
            here, line = pl.ds(start, LANES), start // LANES
            across = jnp.take_along_axis(table, index_ref[0, 0, part, here], axis=1, mode="promise_in_bounds")
            if start + LANES == cols:
                across = jnp.where(lane == LANES - 1, 0.0, across)
            across_ref[part, line, :] = across
            down = jnp.take_along_axis(table, index_ref[0, 1, part, here], axis=1, mode="promise_in_bounds")
            if top + 8 == rows:
                down = jnp.where((sub == 7) & last_tile, 0.0, down)
            down_ref[part, line, :] = down


def via_terms(own_ref, own_weight_ref, low_ref, low_weight, from_above, from_below):
    _, layer = place()
    on_top = layer == lax.axis_size("layer") - 1
    own_weight = own_weight_ref[...]
    low_weight = jnp.where(layer == 0, 0.0, low_weight)
    fixed_source = jnp.where(on_top, own_weight, 0.0)
    own, low = own_ref[...], low_ref[...]

    def via(row):
        return marked(own, row, own_weight) + marked(low, row, low_weight)

    def fixed(row):
        return marked(own, row, fixed_source)

    if from_above is None:
        return via, fixed, None
    own_source = jnp.where(on_top, 0.0, own_weight * from_above)
    low_source = low_weight * from_below

    def moving(row):
        return marked(own, row, own_source) + marked(low, row, low_source)

    return via, fixed, moving


def send_by_parity(first_ref, second_ref, slot, top, bottom):
    tile, _ = place()
    even = lax.rem(tile, 2) == 0
    part = pl.ds(slot * top.shape[0], top.shape[0])
    first_ref[part] = jnp.where(even, bottom, top)
    second_ref[part] = jnp.where(even, top, bottom)
    lengths = first_ref.shape[0], second_ref.shape[0]
    if slot == 0:
        longer = first_ref if lengths[0] > lengths[1] else second_ref
        longer[pl.ds(min(lengths), FILL)] = jnp.zeros((FILL, LANES), jnp.float32)


def taken_by_parity(first_ref, second_ref, slot, lines):
    tile, _ = place()
    even = lax.rem(tile, 2) == 0
    part = pl.ds(slot * lines, lines)
    first, second = first_ref[part], second_ref[part]
    return jnp.where(even, second, first), jnp.where(even, first, second)


def edge_flow(x_ref, across_ref, down_ref, row):
    return beside(x_ref[row], across_ref[row]) + down_ref[row] * x_ref[row + 1] + down_ref[row - 1] * x_ref[row - 1]


def edge_ends(rows):
    return (0, 1, 0), (rows - 1, rows - 2, rows - 2)


def edges(x_ref, across_ref, down_ref, right_side, inverses, rows):
    found = []
    for (edge, within, link), inverse in zip(edge_ends(rows), inverses):
        x = x_ref[within]
        flow = edge_flow(x_ref, across_ref, down_ref, within)
        later = x + FACTORS[0][1] * (inverse * (right_side(within) + flow) - x)
        found.append((right_side(edge) + down_ref[link] * x, right_side(edge) + down_ref[link] * later))
    return tuple(zip(*found))


def links_kernel(
    single, x_ref, across_ref, down_ref, own_ref, count_ref, low_ref, first_ref, second_ref, weight_ref, cells_ref, *sends
):
    rows = x_ref.shape[0]
    own, low = own_ref[...], low_ref[...]
    weight = VIA_UNIT * count_ref[...].astype(jnp.float32)
    cells_ref[...] = own
    weight_ref[...] = weight
    links = chosen(single, own, low)
    for send_ref, cells in zip(sends, links):
        send_ref[0] = pick(x_ref, cells, rows)
    sends[0][1] = weight
    for slot, ref in enumerate((x_ref, across_ref, down_ref)):
        send_by_parity(first_ref, second_ref, slot, ref[0], ref[rows - 1])
    if single:
        send_by_parity(first_ref, second_ref, 3, marked(links[0], 0, 1.0), marked(links[0], rows - 1, 1.0))


def first_edges_kernel(
    rows, x_ref, across_ref, down_ref, loads_ref, own_ref, own_weight_ref, low_ref, above_ref, below_ref, first_ref, second_ref
):
    via, fixed, moving = via_terms(own_ref, own_weight_ref, low_ref, below_ref[1], above_ref[0], below_ref[0])

    def right_side(row):
        return fixed(row) + moving(row) - loads_ref[row]

    def diagonal(row, links):
        across = across_ref[row]
        total = across + column_left(across)
        for link in links:
            total = total + down_ref[link]
        return total + via(row)

    inverses = 1.0 / diagonal(1, (0, 1)), 1.0 / diagonal(rows - 2, (rows - 3, rows - 2))
    for slot, pair in enumerate(edges(x_ref, across_ref, down_ref, right_side, inverses, rows)):
        send_by_parity(first_ref, second_ref, slot, *pair)
    send_by_parity(first_ref, second_ref, 2, diagonal(0, (0,)), diagonal(rows - 1, (rows - 2,)))


def next_early_kernel(
    single,
    rows,
    x_ref,
    across_ref,
    down_ref,
    loads_ref,
    inverse_ref,
    own_ref,
    own_weight_ref,
    low_ref,
    weight_ref,
    after_ref,
    first_ref,
    second_ref,
    *factor_refs,
):
    _, layer = place()
    _, fixed, _ = via_terms(own_ref, own_weight_ref, low_ref, weight_ref[1], None, None)

    def right_side(row):
        return fixed(row) - loads_ref[row]

    send_by_parity(first_ref, second_ref, 0, x_ref[0], x_ref[rows - 1])
    inverses = inverse_ref[1], inverse_ref[rows - 2]
    for slot, pair in enumerate(edges(x_ref, across_ref, down_ref, right_side, inverses, rows)):
        send_by_parity(first_ref, second_ref, 1 + slot, *pair)
    if single:
        cells = jnp.where(layer == 0, own_ref[...], low_ref[...])
        weight = jnp.where(layer == 0, own_weight_ref[...], weight_ref[1])
        factors = []
        for (edge, within, link), inverse in zip(edge_ends(rows), inverses):
            share = FACTORS[0][1] * inverse * down_ref[link]
            factors.append(marked(cells, edge, weight) + marked(cells, within, weight * share))
        for ref, factor in zip(factor_refs, factors):
            ref[...] = factor


def next_late_kernel(
    rows, down_ref, inverse_ref, own_ref, own_weight_ref, low_ref, weight_ref, above_ref, below_ref, first_ref, second_ref
):
    _, _, moving = via_terms(own_ref, own_weight_ref, low_ref, weight_ref[1], above_ref[0], below_ref[0])
    found = []
    for edge, within, link in edge_ends(rows):
        change = moving(edge)
        share = FACTORS[0][1] * inverse_ref[within] * down_ref[link]
        found.append((change, change + share * moving(within)))
    for slot, pair in enumerate(zip(*found)):
        send_by_parity(first_ref, second_ref, slot, *pair)


def next_late_single_kernel(top_ref, bottom_ref, volts_ref, first_ref, second_ref):
    volts = volts_ref[0]
    send_by_parity(first_ref, second_ref, 0, top_ref[...] * volts, bottom_ref[...] * volts)


def relaxed(x, flow, side, inverse, previous, sweep):
    keep, gain = FACTORS[sweep]
    update = gain * (inverse * (side + flow) - x)
    if sweep > 0:
        update = update + keep * previous
    return x + update, update


def chosen(single, own, low):
    _, layer = place()
    return [jnp.where(layer == 0, own, low)] if single else [own, low]


def inner_rows(
    rows, reach, outside, x_ref, across_ref, down_ref, side_ref, inverse_ref, work, update_ref, core_ref, keep_ref
):
    sources = [x_ref, *work]
    targets = [*work, core_ref]
    for sweep in range(SWEEPS):
        source, target = sources[sweep], targets[sweep]
        for row in range(sweep + reach, rows - sweep - reach):
            x = source[row]
            flow = beside(x, across_ref[row])
            if row == 0:
                flow = flow + outside[0]
            else:
                flow = flow + down_ref[row - 1] * source[row - 1]
            if row == rows - 1:
                flow = flow + outside[1]
            else:
                flow = flow + down_ref[row] * source[row + 1]
            previous = update_ref[row] if sweep > 0 else None
            value, update = relaxed(x, flow, side_ref[row], inverse_ref[row], previous, sweep)
            target[row] = value
            if sweep < SWEEPS - 1:
                update_ref[row] = update
                for side, depth in ((0, row), (1, rows - 1 - row)):
                    slot = 3 * (2 * sweep + side)
                    if depth == sweep + reach:
                        keep_ref[slot] = value
                        keep_ref[slot + 2] = update
                    if depth == sweep + reach + 1:
                        keep_ref[slot + 1] = value


def outer_rows(side, rows, reach, halo, link, inverse_edge, x_ref, across_ref, down_ref, side_ref, inverse_ref, keep_ref):
    edge_x, edge_q, edge_across = halo

    def row_of(depth):
        return depth if side == 0 else rows - 1 - depth

    def link_out(depth):
        if depth == 0:
            return link
        return down_ref[depth - 1] if side == 0 else down_ref[rows - 1 - depth]

    def link_in(depth):
        return down_ref[depth] if side == 0 else down_ref[rows - 2 - depth]

    values = {-1: edge_x}
    for depth in range(reach + 1):
        values[depth] = x_ref[row_of(depth)]
    updates = {}
    for sweep in range(SWEEPS):
        found, changed = {}, {}
        if sweep < SWEEPS - 1:
            x = values[-1]
            flow = beside(x, edge_across) + link * values[0]
            found[-1], changed[-1] = relaxed(x, flow, edge_q[sweep], inverse_edge, updates.get(-1), sweep)
        for depth in range(sweep + reach):
            row = row_of(depth)
            x = values[depth]
            flow = beside(x, across_ref[row]) + link_out(depth) * values[depth - 1] + link_in(depth) * values[depth + 1]
            found[depth], changed[depth] = relaxed(x, flow, side_ref[row], inverse_ref[row], updates.get(depth), sweep)
        if sweep < SWEEPS - 1:
            slot = 3 * (2 * sweep + side)
            found[sweep + reach] = keep_ref[slot]
            changed[sweep + reach] = keep_ref[slot + 2]
            found[sweep + reach + 1] = keep_ref[slot + 1]
        values, updates = found, changed
    return {row_of(depth): value for depth, value in values.items()}


KEPT = 6 * (SWEEPS - 1)


def first_inner_kernel(
    single,
    rows,
    x_ref,
    across_ref,
    down_ref,
    loads_ref,
    own_ref,
    own_weight_ref,
    low_ref,
    above_ref,
    below_ref,
    first_ref,
    second_ref,
    after_ref,
    core_ref,
    side_ref,
    inverse_ref,
    keep_ref,
    halo_ref,
    picked_ref,
    *scratch,
):
    tile, _ = place()
    via, fixed, moving = via_terms(own_ref, own_weight_ref, low_ref, below_ref[1], above_ref[0], below_ref[0])
    top_x, low_x = taken_by_parity(first_ref, second_ref, 0, x_ref.shape[1])
    top_across, low_across = taken_by_parity(first_ref, second_ref, 1, x_ref.shape[1])
    link, _ = taken_by_parity(first_ref, second_ref, 2, x_ref.shape[1])
    link = jnp.where(tile == 0, 0.0, link)
    held = [top_across, low_across, link, top_x, low_x]
    if single:
        held.extend(taken_by_parity(first_ref, second_ref, 3, x_ref.shape[1]))
    for slot, value in enumerate(held):
        halo_ref[slot] = value
    for row in range(rows):
        side_ref[row] = fixed(row) + moving(row) - loads_ref[row]
        across = across_ref[row]
        diagonal = across + column_left(across) + down_ref[row] + via(row)
        diagonal = diagonal + (down_ref[row - 1] if row > 0 else link)
        inverse_ref[row] = 1.0 / diagonal
    outside = link * top_x, down_ref[rows - 1] * low_x
    shared = (x_ref, across_ref, down_ref, side_ref, inverse_ref)
    inner_rows(rows, 0, outside, *shared, scratch[:-1], scratch[-1], core_ref, keep_ref)
    for index, cells in enumerate(chosen(single, own_ref[...], low_ref[...])):
        total = jnp.zeros(cells.shape, jnp.float32)
        for row in range(SWEEPS - 1, rows - SWEEPS + 1):
            total = total + marked(cells, row, core_ref[row])
        picked_ref[index] = total


def first_outer_kernel(
    single,
    rows,
    x_ref,
    across_ref,
    down_ref,
    side_ref,
    inverse_ref,
    keep_ref,
    halo_ref,
    picked_ref,
    own_ref,
    low_ref,
    first_ref,
    second_ref,
    core_ref,
    next_ref,
    edge_ref,
    *sends,
):
    top_q0, low_q0 = taken_by_parity(first_ref, second_ref, 0, x_ref.shape[1])
    top_q1, low_q1 = taken_by_parity(first_ref, second_ref, 1, x_ref.shape[1])
    top_diag, low_diag = taken_by_parity(first_ref, second_ref, 2, x_ref.shape[1])
    link, low_link = halo_ref[2], down_ref[rows - 1]
    top_inverse = 1.0 / (top_diag + link)
    low_inverse = 1.0 / (low_diag + low_link)
    edge_ref[0] = top_inverse
    edge_ref[1] = low_inverse
    shared = (x_ref, across_ref, down_ref, side_ref, inverse_ref, keep_ref)
    outer = outer_rows(0, rows, 0, (halo_ref[3], (top_q0, top_q1), halo_ref[0]), link, top_inverse, *shared)
    outer.update(
        outer_rows(1, rows, 0, (halo_ref[4], (low_q0, low_q1), halo_ref[1]), low_link, low_inverse, *shared)
    )
    for row, value in outer.items():
        next_ref[row] = value
    for index, cells in enumerate(chosen(single, own_ref[...], low_ref[...])):
        total = picked_ref[index]
        for row, value in outer.items():
            total = total + marked(cells, row, value)
        sends[index][0] = total


def last_inner_kernel(
    rows,
    x_ref,
    across_ref,
    down_ref,
    loads_ref,
    inverse_ref,
    own_ref,
    own_weight_ref,
    low_ref,
    weight_ref,
    above_ref,
    below_ref,
    after_ref,
    core_ref,
    side_ref,
    keep_ref,
    *scratch,
):
    _, fixed, moving = via_terms(own_ref, own_weight_ref, low_ref, weight_ref[1], above_ref[0], below_ref[0])
    for row in range(rows):
        side_ref[row] = fixed(row) + moving(row) - loads_ref[row]
    shared = (x_ref, across_ref, down_ref, side_ref, inverse_ref)
    inner_rows(rows, 1, None, *shared, scratch[:-1], scratch[-1], core_ref, keep_ref)


def last_middle_kernel(
    rows,
    x_ref,
    across_ref,
    down_ref,
    side_ref,
    inverse_ref,
    keep_ref,
    halo_ref,
    first_ref,
    second_ref,
    core_ref,
    kept_ref,
    next_ref,
):
    edge_x = taken_by_parity(first_ref, second_ref, 0, x_ref.shape[1])
    for side in range(2):
        outside = halo_ref[2] * edge_x[0] if side == 0 else down_ref[rows - 1] * edge_x[1]
        further = x_ref[0 if side == 0 else rows - 1], x_ref[1 if side == 0 else rows - 2]
        previous = None
        for sweep in range(SWEEPS):
            row = sweep if side == 0 else rows - 1 - sweep
            links = (row - 1, row) if side == 0 else (row, row - 1)
            x, within = further
            flow = beside(x, across_ref[row]) + (outside if sweep == 0 else down_ref[links[0]] * outside)
            flow = flow + down_ref[links[1]] * within
            value, update = relaxed(x, flow, side_ref[row], inverse_ref[row], previous, sweep)
            if sweep == SWEEPS - 1:
                next_ref[row] = value
                break
            slot = 3 * (2 * sweep + side)
            kept_ref[slot] = value
            kept_ref[slot + 1] = keep_ref[slot]
            kept_ref[slot + 2] = update
            further = keep_ref[slot], keep_ref[slot + 1]
            previous = keep_ref[slot + 2]
            outside = value


def last_outer_kernel(
    single,
    rows,
    x_ref,
    across_ref,
    down_ref,
    side_ref,
    inverse_ref,
    keep_ref,
    halo_ref,
    edge_ref,
    early_first_ref,
    early_second_ref,
    first_ref,
    second_ref,
    core_ref,
    out_ref,
    next_ref,
    held,
    sems,
):
    lines = x_ref.shape[1]
    early = [taken_by_parity(early_first_ref, early_second_ref, slot, lines) for slot in range(3)]
    late = [taken_by_parity(first_ref, second_ref, slot, lines) for slot in range(1 if single else 2)]
    leaving = []
    for side in range(2):
        if single:
            changes = halo_ref[5 + side] * late[0][side], late[0][side]
        else:
            changes = late[0][side], late[1][side]
        sides = early[1][side] + changes[0], early[2][side] + changes[1]
        outer = outer_rows(
            side,
            rows,
            0,
            (early[0][side], sides, halo_ref[side]),
            halo_ref[2] if side == 0 else down_ref[rows - 1],
            edge_ref[side],
            *(x_ref, across_ref, down_ref, side_ref, inverse_ref, keep_ref),
        )
        for row, value in outer.items():
            next_ref[row] = value
        half = rows // 2
        for first, width in chunks_of(held.shape[1], CHUNKS):
            for top in range(side * half, side * half + half, 8):
                for start in range(first, first + width, LANES):
                    held[pl.ds(top, 8), pl.ds(start, LANES)] = next_ref[pl.ds(top, 8), start // LANES, :]
            part = pl.ds(side * half, half), pl.ds(first, width)
            copy = pltpu.make_async_copy(held.at[part], out_ref.at[part], sems.at[len(leaving)])
            copy.start()
            leaving.append(copy)
    for copy in leaving:
        copy.wait()


def call(kernel, name, ins, outs, scratch=(), aliases=None, work=None):
    spaces = {"vmem": pltpu.VMEM, "hbm": pltpu.HBM, "any": pl.ANY}
    return pl.pallas_call(
        kernel,
        out_shape=[jax.ShapeDtypeStruct(shape, *(kind or [jnp.float32])) for _, shape, *kind in outs],
        in_specs=[pl.BlockSpec(memory_space=spaces[space]) for space, _ in ins],
        out_specs=[pl.BlockSpec(memory_space=spaces[space]) for space, *_ in outs],
        scratch_shapes=list(scratch),
        input_output_aliases=aliases or {},
        compiler_params=pltpu.CompilerParams(vmem_limit_bytes=40 * 1024 * 1024),
        cost_estimate=work and pl.CostEstimate(flops=work, bytes_accessed=work, transcendentals=0),
        name=name,
    )(*(pltpu.with_memory_space_constraint(array, pltpu.HBM) if space == "hbm" else array for space, array in ins))


def routes(tiles, layers):
    def at(tile, layer):
        return tile * layers + layer % layers

    everywhere = [(tile, layer) for tile in range(tiles) for layer in range(layers)]
    up = [(at(t, l), at(t, l + 1)) for t, l in everywhere]
    down = [(at(t, l), at(t, l - 1)) for t, l in everywhere]
    first, second = [], []
    for t, l in everywhere:
        first.append((at(t, l), at(t ^ 1, l)))
        beyond = t + 1 if t % 2 else t - 1
        if 0 <= beyond < tiles:
            second.append((at(t, l), at(beyond, l)))
        else:
            second.append((at(t, l), at(t, l + 1)))
    return up, down, first, second


def local(class_index, class_conductance, loads, start_volts, via_cells, via_counts):
    rows, cols = loads.shape[1:]
    lines = cols // LANES
    tiles, layers = lax.axis_size("tile"), lax.axis_size("layer")
    up, down, first, second = routes(tiles, layers)
    single = layers == 2
    move = functools.partial(lax.ppermute, axis_name=("tile", "layer"))

    def rows_of(count):
        return (count, lines, LANES)

    def messages(count, longer):
        return [("vmem", (count * lines + (FILL if longer == side else 0), LANES)) for side in range(2)]

    def vmem(*arrays):
        return [("vmem", array) for array in arrays]

    def between_layers(sends):
        if single:
            got = move(sends[0], perm=up)
            return got, got
        return move(sends[1], perm=down), move(sends[0], perm=up)

    def beside_tile(sent):
        across_chips = move(sent[1], perm=second)
        return move(sent[0], perm=first), across_chips

    field = ("vmem", rows_of(rows))
    work = [pltpu.VMEM(rows_of(rows), jnp.float32)] * SWEEPS
    pick_count = 1 if single else 2
    picks = [("vmem", rows_of(1))] * pick_count

    cells = via_cells.reshape(lines, LANES)
    counts = via_counts.reshape(lines, LANES)
    low = move(cells, perm=up)
    x, table = call(
        unpack_volts_kernel,
        "unpack_volts",
        [("hbm", start_volts), ("hbm", class_conductance)],
        [field, ("vmem", (8, LANES))],
        [
            pltpu.VMEM((rows, cols), jnp.float32),
            pltpu.VMEM(class_conductance.shape, jnp.float32),
            pltpu.SemaphoreType.DMA((CHUNKS + 1,)),
        ],
        work=1000000000,
    )
    across, downward = call(unpack_index_kernel, "unpack_index", vmem(class_index, table), [field] * 2)
    first_sent, second_sent, own_weight, own, *sends = call(
        functools.partial(links_kernel, single),
        "links",
        vmem(x, across, downward, cells, counts, low),
        messages(4 if single else 3, 0)
        + [("vmem", cells.shape), ("vmem", cells.shape, cells.dtype), ("vmem", rows_of(2))]
        + ([] if single else [("vmem", rows_of(1))]),
    )
    vias = (own, own_weight, low)
    above, below = between_layers(sends)
    weights = below
    (load,) = call(unpack_field_kernel, "unpack_loads", vmem(loads), [field])
    early = beside_tile((first_sent, second_sent))
    sent = call(
        functools.partial(first_edges_kernel, rows),
        "first_edges",
        vmem(x, across, downward, load, *vias, above, below),
        messages(3, 1),
        work=2 * 10**10,
    )
    got = beside_tile(sent)
    core, side, inverse, keep, halo, picked = call(
        functools.partial(first_inner_kernel, single, rows),
        "first_inner",
        vmem(x, across, downward, load, *vias, above, below, *early) + [("any", sent[1])],
        [field, field, field, ("vmem", rows_of(KEPT)), ("vmem", rows_of(7 if single else 5)), ("vmem", rows_of(pick_count))],
        work,
    )
    x, edge, *sends = call(
        functools.partial(first_outer_kernel, single, rows),
        "first_outer",
        vmem(x, across, downward, side, inverse, keep, halo, picked, own, low, *got, core),
        [field, ("vmem", rows_of(2))] + picks,
        aliases={12: 0},
    )
    above, below = between_layers(sends)
    sent = call(
        functools.partial(next_early_kernel, single, rows),
        "next_early",
        vmem(x, across, downward, load, inverse, *vias, weights) + [("any", sends[0])],
        messages(3, 0) + [("vmem", cells.shape)] * (2 if single else 0),
    )
    early = beside_tile(sent[:2])
    if single:
        late = call(
            next_late_single_kernel,
            "next_late",
            vmem(*sent[2:], above),
            messages(1, 1),
            work=2 * 10**10,
        )
    else:
        late = call(
            functools.partial(next_late_kernel, rows),
            "next_late",
            vmem(downward, inverse, *vias, weights, above, below),
            messages(2, 1),
            work=2 * 10**10,
        )
    got = beside_tile(late)
    core, side, keep = call(
        functools.partial(last_inner_kernel, rows),
        "last_inner",
        vmem(x, across, downward, load, inverse, *vias, weights, above, below) + [("any", late[1])],
        [field, field, ("vmem", rows_of(KEPT))],
        work,
    )
    keep, core = call(
        functools.partial(last_middle_kernel, rows),
        "last_middle",
        vmem(x, across, downward, side, inverse, keep, halo, *early, core),
        [("vmem", rows_of(KEPT)), field],
        aliases={9: 1},
    )
    volts, _ = call(
        functools.partial(last_outer_kernel, single, rows),
        "last_outer",
        vmem(x, across, downward, side, inverse, keep, halo, edge, *early, *got, core),
        [("hbm", (rows, cols)), field],
        [pltpu.VMEM((rows, cols), jnp.float32), pltpu.SemaphoreType.DMA((2 * CHUNKS,))],
        aliases={12: 1},
    )
    return volts[None]


def solution(mesh):
    placed = (
        P("layer", None, "tile", None),
        P("layer", None),
        P("layer", "tile", None),
        P("layer", "tile", None),
        P("layer", "tile"),
        P("layer", "tile"),
    )
    return jax.shard_map(
        local, mesh=mesh, in_specs=placed, out_specs=P("layer", "tile", None), check_vma=False
    )
```

```python
import functools

import jax
import jax.numpy as jnp
from jax import lax
from jax.experimental import pallas as pl
from jax.experimental.pallas import tpu as pltpu
from jax.sharding import PartitionSpec as P

OUTER = 2
SWEEPS = 3
VIA_UNIT = 2.0
LOWER_BOUND = 0.05
UPPER_BOUND = 2.0
LANES = 128
CHUNKS = 2
FILL = 8


def chebyshev_terms(count):
    centre_value = 0.5 * (UPPER_BOUND + LOWER_BOUND)
    half_width = 0.5 * (UPPER_BOUND - LOWER_BOUND)
    sigma = centre_value / half_width
    rho_last = 1.0 / sigma
    terms = [(0.0, 1.0 / centre_value)]
    for index in range(1, count):
        rho_next = 1.0 / (2.0 * sigma - rho_last)
        terms.append((rho_next * rho_last, 2.0 * rho_next / half_width))
        rho_last = rho_next
    return terms


FACTORS = chebyshev_terms(SWEEPS)


def column_right(row):
    lane = lax.broadcasted_iota(jnp.int32, row.shape, 1)
    turned = pltpu.roll(row, LANES - 1, 1)
    return jnp.where(lane == LANES - 1, pltpu.roll(turned, row.shape[0] - 1, 0), turned)


def column_left(row):
    lane = lax.broadcasted_iota(jnp.int32, row.shape, 1)
    turned = pltpu.roll(row, 1, 1)
    return jnp.where(lane == 0, pltpu.roll(turned, 1, 0), turned)


def beside(x, across):
    return across * column_right(x) + column_left(across * x)


def place():
    return lax.axis_index("tile"), lax.axis_index("layer")


def weight_of(count_ref):
    return VIA_UNIT * count_ref[...].astype(jnp.float32)


def marked(cells, row, value):
    return jnp.where(cells == row, value, 0.0)


def pick(x_ref, cells, rows):
    total = jnp.zeros(cells.shape, jnp.float32)
    for row in range(rows):
        total = total + marked(cells, row, x_ref[row])
    return total


def chunks_of(cols, count):
    width = cols // count
    return [(first, width) for first in range(0, cols, width)]


def unpack_field_kernel(field_ref, out_ref):
    rows, cols = field_ref.shape[1:]
    for top in range(0, rows, 8):
        for start in range(0, cols, LANES):
            out_ref[pl.ds(top, 8), start // LANES, :] = field_ref[0, pl.ds(top, 8), pl.ds(start, LANES)]


def table_kernel(class_ref, table_ref):
    count = class_ref.shape[1]
    table_ref[...] = jnp.zeros(table_ref.shape, jnp.float32)
    table_ref[:, pl.ds(0, count)] = jnp.broadcast_to(class_ref[...], (8, count))


def unpack_kernel(index_ref, volts_ref, own_ref, count_ref, table_ref, across_ref, down_ref, x_ref, cells_ref, weight_ref):
    unpack_field_kernel(volts_ref, x_ref)
    cells_ref[...] = own_ref[...]
    weight_ref[...] = weight_of(count_ref)
    rows, cols = index_ref.shape[2:]
    tile, _ = place()
    last_tile = tile == lax.axis_size("tile") - 1
    table = table_ref[...]
    lane = lax.broadcasted_iota(jnp.int32, (8, LANES), 1)
    sub = lax.broadcasted_iota(jnp.int32, (8, LANES), 0)
    for top in range(0, rows, 8):
        part = pl.ds(top, 8)
        for start in range(0, cols, LANES):
            here, line = pl.ds(start, LANES), start // LANES
            across = jnp.take_along_axis(table, index_ref[0, 0, part, here], axis=1, mode="promise_in_bounds")
            if start + LANES == cols:
                across = jnp.where(lane == LANES - 1, 0.0, across)
            across_ref[part, line, :] = across
            down = jnp.take_along_axis(table, index_ref[0, 1, part, here], axis=1, mode="promise_in_bounds")
            if top + 8 == rows:
                down = jnp.where((sub == 7) & last_tile, 0.0, down)
            down_ref[part, line, :] = down


def via_terms(own_ref, own_weight_ref, low_ref, low_weight, from_above, from_below):
    _, layer = place()
    on_top = layer == lax.axis_size("layer") - 1
    own_weight = own_weight_ref[...]
    low_weight = jnp.where(layer == 0, 0.0, low_weight)
    fixed_source = jnp.where(on_top, own_weight, 0.0)
    own, low = own_ref[...], low_ref[...]

    def via(row):
        return marked(own, row, own_weight) + marked(low, row, low_weight)

    def fixed(row):
        return marked(own, row, fixed_source)

    if from_above is None:
        return via, fixed, None
    own_source = jnp.where(on_top, 0.0, own_weight * from_above)
    low_source = low_weight * from_below

    def moving(row):
        return marked(own, row, own_source) + marked(low, row, low_source)

    return via, fixed, moving


def send_by_parity(first_ref, second_ref, slot, top, bottom):
    tile, _ = place()
    even = lax.rem(tile, 2) == 0
    part = pl.ds(slot * top.shape[0], top.shape[0])
    first_ref[part] = jnp.where(even, bottom, top)
    second_ref[part] = jnp.where(even, top, bottom)
    lengths = first_ref.shape[0], second_ref.shape[0]
    if slot == 0:
        longer = first_ref if lengths[0] > lengths[1] else second_ref
        longer[pl.ds(min(lengths), FILL)] = jnp.zeros((FILL, LANES), jnp.float32)


def taken_by_parity(first_ref, second_ref, slot, lines):
    tile, _ = place()
    even = lax.rem(tile, 2) == 0
    part = pl.ds(slot * lines, lines)
    first, second = first_ref[part], second_ref[part]
    return jnp.where(even, second, first), jnp.where(even, first, second)


def edge_flow(x_ref, across_ref, down_ref, row):
    return beside(x_ref[row], across_ref[row]) + down_ref[row] * x_ref[row + 1] + down_ref[row - 1] * x_ref[row - 1]


def edge_ends(rows):
    return (0, 1, 0), (rows - 1, rows - 2, rows - 2)


def edges(x_ref, across_ref, down_ref, right_side, inverses, rows):
    found = []
    for (edge, within, link), inverse in zip(edge_ends(rows), inverses):
        x = x_ref[within]
        flow = edge_flow(x_ref, across_ref, down_ref, within)
        later = x + FACTORS[0][1] * (inverse * (right_side(within) + flow) - x)
        found.append((right_side(edge) + down_ref[link] * x, right_side(edge) + down_ref[link] * later))
    return tuple(zip(*found))


def links_kernel(
    single, x_ref, across_ref, down_ref, own_ref, low_ref, first_ref, second_ref, *sends
):
    rows = x_ref.shape[0]
    links = chosen(single, own_ref[...], low_ref[...])
    for send_ref, cells in zip(sends, links):
        send_ref[0] = pick(x_ref, cells, rows)
    for slot, ref in enumerate((x_ref, across_ref, down_ref)):
        send_by_parity(first_ref, second_ref, slot, ref[0], ref[rows - 1])
    if single:
        send_by_parity(first_ref, second_ref, 3, marked(links[0], 0, 1.0), marked(links[0], rows - 1, 1.0))


def first_edges_kernel(
    rows,
    x_ref,
    across_ref,
    down_ref,
    loads_ref,
    own_ref,
    own_weight_ref,
    low_ref,
    low_count_ref,
    above_ref,
    below_ref,
    first_ref,
    second_ref,
):
    via, fixed, moving = via_terms(own_ref, own_weight_ref, low_ref, weight_of(low_count_ref), above_ref[0], below_ref[0])

    def right_side(row):
        return fixed(row) + moving(row) - loads_ref[row]

    def diagonal(row, links):
        across = across_ref[row]
        total = across + column_left(across)
        for link in links:
            total = total + down_ref[link]
        return total + via(row)

    inverses = 1.0 / diagonal(1, (0, 1)), 1.0 / diagonal(rows - 2, (rows - 3, rows - 2))
    for slot, pair in enumerate(edges(x_ref, across_ref, down_ref, right_side, inverses, rows)):
        send_by_parity(first_ref, second_ref, slot, *pair)
    send_by_parity(first_ref, second_ref, 2, diagonal(0, (0,)), diagonal(rows - 1, (rows - 2,)))


def next_early_kernel(
    single,
    rows,
    x_ref,
    across_ref,
    down_ref,
    loads_ref,
    inverse_ref,
    own_ref,
    own_weight_ref,
    low_ref,
    low_count_ref,
    after_ref,
    first_ref,
    second_ref,
    *factor_refs,
):
    _, layer = place()
    _, fixed, _ = via_terms(own_ref, own_weight_ref, low_ref, weight_of(low_count_ref), None, None)

    def right_side(row):
        return fixed(row) - loads_ref[row]

    send_by_parity(first_ref, second_ref, 0, x_ref[0], x_ref[rows - 1])
    inverses = inverse_ref[1], inverse_ref[rows - 2]
    for slot, pair in enumerate(edges(x_ref, across_ref, down_ref, right_side, inverses, rows)):
        send_by_parity(first_ref, second_ref, 1 + slot, *pair)
    if single:
        cells = jnp.where(layer == 0, own_ref[...], low_ref[...])
        weight = jnp.where(layer == 0, own_weight_ref[...], weight_of(low_count_ref))
        factors = []
        for (edge, within, link), inverse in zip(edge_ends(rows), inverses):
            share = FACTORS[0][1] * inverse * down_ref[link]
            factors.append(marked(cells, edge, weight) + marked(cells, within, weight * share))
        for ref, factor in zip(factor_refs, factors):
            ref[...] = factor


def next_late_kernel(
    rows, down_ref, inverse_ref, own_ref, own_weight_ref, low_ref, low_count_ref, above_ref, below_ref, first_ref, second_ref
):
    _, _, moving = via_terms(own_ref, own_weight_ref, low_ref, weight_of(low_count_ref), above_ref[0], below_ref[0])
    found = []
    for edge, within, link in edge_ends(rows):
        change = moving(edge)
        share = FACTORS[0][1] * inverse_ref[within] * down_ref[link]
        found.append((change, change + share * moving(within)))
    for slot, pair in enumerate(zip(*found)):
        send_by_parity(first_ref, second_ref, slot, *pair)


def next_late_single_kernel(top_ref, bottom_ref, volts_ref, first_ref, second_ref):
    volts = volts_ref[0]
    send_by_parity(first_ref, second_ref, 0, top_ref[...] * volts, bottom_ref[...] * volts)


def relaxed(x, flow, side, inverse, previous, sweep):
    keep, gain = FACTORS[sweep]
    update = gain * (inverse * (side + flow) - x)
    if sweep > 0:
        update = update + keep * previous
    return x + update, update


def chosen(single, own, low):
    _, layer = place()
    return [jnp.where(layer == 0, own, low)] if single else [own, low]


def inner_rows(
    rows, reach, outside, x_ref, across_ref, down_ref, side_ref, inverse_ref, work, update_ref, core_ref, keep_ref
):
    sources = [x_ref, *work]
    targets = [*work, core_ref]
    for sweep in range(SWEEPS):
        source, target = sources[sweep], targets[sweep]
        for row in range(sweep + reach, rows - sweep - reach):
            x = source[row]
            flow = beside(x, across_ref[row])
            if row == 0:
                flow = flow + outside[0]
            else:
                flow = flow + down_ref[row - 1] * source[row - 1]
            if row == rows - 1:
                flow = flow + outside[1]
            else:
                flow = flow + down_ref[row] * source[row + 1]
            previous = update_ref[row] if sweep > 0 else None
            value, update = relaxed(x, flow, side_ref[row], inverse_ref[row], previous, sweep)
            target[row] = value
            if sweep < SWEEPS - 1:
                update_ref[row] = update
                for side, depth in ((0, row), (1, rows - 1 - row)):
                    slot = 3 * (2 * sweep + side)
                    if depth == sweep + reach:
                        keep_ref[slot] = value
                        keep_ref[slot + 2] = update
                    if depth == sweep + reach + 1:
                        keep_ref[slot + 1] = value


def outer_rows(side, rows, reach, halo, link, inverse_edge, x_ref, across_ref, down_ref, side_ref, inverse_ref, keep_ref):
    edge_x, edge_q, edge_across = halo

    def row_of(depth):
        return depth if side == 0 else rows - 1 - depth

    def link_out(depth):
        if depth == 0:
            return link
        return down_ref[depth - 1] if side == 0 else down_ref[rows - 1 - depth]

    def link_in(depth):
        return down_ref[depth] if side == 0 else down_ref[rows - 2 - depth]

    values = {-1: edge_x}
    for depth in range(reach + 1):
        values[depth] = x_ref[row_of(depth)]
    updates = {}
    for sweep in range(SWEEPS):
        found, changed = {}, {}
        if sweep < SWEEPS - 1:
            x = values[-1]
            flow = beside(x, edge_across) + link * values[0]
            found[-1], changed[-1] = relaxed(x, flow, edge_q[sweep], inverse_edge, updates.get(-1), sweep)
        for depth in range(sweep + reach):
            row = row_of(depth)
            x = values[depth]
            flow = beside(x, across_ref[row]) + link_out(depth) * values[depth - 1] + link_in(depth) * values[depth + 1]
            found[depth], changed[depth] = relaxed(x, flow, side_ref[row], inverse_ref[row], updates.get(depth), sweep)
        if sweep < SWEEPS - 1:
            slot = 3 * (2 * sweep + side)
            found[sweep + reach] = keep_ref[slot]
            changed[sweep + reach] = keep_ref[slot + 2]
            found[sweep + reach + 1] = keep_ref[slot + 1]
        values, updates = found, changed
    return {row_of(depth): value for depth, value in values.items()}


KEPT = 6 * (SWEEPS - 1)


def first_inner_kernel(
    single,
    rows,
    x_ref,
    across_ref,
    down_ref,
    loads_ref,
    own_ref,
    own_weight_ref,
    low_ref,
    low_count_ref,
    above_ref,
    below_ref,
    first_ref,
    second_ref,
    after_ref,
    core_ref,
    side_ref,
    inverse_ref,
    keep_ref,
    halo_ref,
    picked_ref,
    *scratch,
):
    tile, _ = place()
    via, fixed, moving = via_terms(own_ref, own_weight_ref, low_ref, weight_of(low_count_ref), above_ref[0], below_ref[0])
    top_x, low_x = taken_by_parity(first_ref, second_ref, 0, x_ref.shape[1])
    top_across, low_across = taken_by_parity(first_ref, second_ref, 1, x_ref.shape[1])
    link, _ = taken_by_parity(first_ref, second_ref, 2, x_ref.shape[1])
    link = jnp.where(tile == 0, 0.0, link)
    held = [top_across, low_across, link, top_x, low_x]
    if single:
        held.extend(taken_by_parity(first_ref, second_ref, 3, x_ref.shape[1]))
    for slot, value in enumerate(held):
        halo_ref[slot] = value
    for row in range(rows):
        side_ref[row] = fixed(row) + moving(row) - loads_ref[row]
        across = across_ref[row]
        diagonal = across + column_left(across) + down_ref[row] + via(row)
        diagonal = diagonal + (down_ref[row - 1] if row > 0 else link)
        inverse_ref[row] = 1.0 / diagonal
    outside = link * top_x, down_ref[rows - 1] * low_x
    shared = (x_ref, across_ref, down_ref, side_ref, inverse_ref)
    inner_rows(rows, 0, outside, *shared, scratch[:-1], scratch[-1], core_ref, keep_ref)
    for index, cells in enumerate(chosen(single, own_ref[...], low_ref[...])):
        total = jnp.zeros(cells.shape, jnp.float32)
        for row in range(SWEEPS - 1, rows - SWEEPS + 1):
            total = total + marked(cells, row, core_ref[row])
        picked_ref[index] = total


def first_outer_kernel(
    single,
    rows,
    x_ref,
    across_ref,
    down_ref,
    side_ref,
    inverse_ref,
    keep_ref,
    halo_ref,
    picked_ref,
    own_ref,
    low_ref,
    first_ref,
    second_ref,
    core_ref,
    next_ref,
    edge_ref,
    *sends,
):
    top_q0, low_q0 = taken_by_parity(first_ref, second_ref, 0, x_ref.shape[1])
    top_q1, low_q1 = taken_by_parity(first_ref, second_ref, 1, x_ref.shape[1])
    top_diag, low_diag = taken_by_parity(first_ref, second_ref, 2, x_ref.shape[1])
    link, low_link = halo_ref[2], down_ref[rows - 1]
    top_inverse = 1.0 / (top_diag + link)
    low_inverse = 1.0 / (low_diag + low_link)
    edge_ref[0] = top_inverse
    edge_ref[1] = low_inverse
    shared = (x_ref, across_ref, down_ref, side_ref, inverse_ref, keep_ref)
    outer = outer_rows(0, rows, 0, (halo_ref[3], (top_q0, top_q1), halo_ref[0]), link, top_inverse, *shared)
    outer.update(
        outer_rows(1, rows, 0, (halo_ref[4], (low_q0, low_q1), halo_ref[1]), low_link, low_inverse, *shared)
    )
    for row, value in outer.items():
        next_ref[row] = value
    for index, cells in enumerate(chosen(single, own_ref[...], low_ref[...])):
        total = picked_ref[index]
        for row, value in outer.items():
            total = total + marked(cells, row, value)
        sends[index][0] = total


def last_inner_kernel(
    rows,
    x_ref,
    across_ref,
    down_ref,
    loads_ref,
    inverse_ref,
    own_ref,
    own_weight_ref,
    low_ref,
    low_count_ref,
    above_ref,
    below_ref,
    after_ref,
    core_ref,
    side_ref,
    keep_ref,
    *scratch,
):
    _, fixed, moving = via_terms(own_ref, own_weight_ref, low_ref, weight_of(low_count_ref), above_ref[0], below_ref[0])
    for row in range(rows):
        side_ref[row] = fixed(row) + moving(row) - loads_ref[row]
    shared = (x_ref, across_ref, down_ref, side_ref, inverse_ref)
    inner_rows(rows, 1, None, *shared, scratch[:-1], scratch[-1], core_ref, keep_ref)


def last_middle_kernel(
    rows,
    x_ref,
    across_ref,
    down_ref,
    side_ref,
    inverse_ref,
    keep_ref,
    halo_ref,
    first_ref,
    second_ref,
    core_ref,
    kept_ref,
    next_ref,
):
    edge_x = taken_by_parity(first_ref, second_ref, 0, x_ref.shape[1])
    for side in range(2):
        outside = halo_ref[2] * edge_x[0] if side == 0 else down_ref[rows - 1] * edge_x[1]
        further = x_ref[0 if side == 0 else rows - 1], x_ref[1 if side == 0 else rows - 2]
        previous = None
        for sweep in range(SWEEPS):
            row = sweep if side == 0 else rows - 1 - sweep
            links = (row - 1, row) if side == 0 else (row, row - 1)
            x, within = further
            flow = beside(x, across_ref[row]) + (outside if sweep == 0 else down_ref[links[0]] * outside)
            flow = flow + down_ref[links[1]] * within
            value, update = relaxed(x, flow, side_ref[row], inverse_ref[row], previous, sweep)
            if sweep == SWEEPS - 1:
                next_ref[row] = value
                break
            slot = 3 * (2 * sweep + side)
            kept_ref[slot] = value
            kept_ref[slot + 1] = keep_ref[slot]
            kept_ref[slot + 2] = update
            further = keep_ref[slot], keep_ref[slot + 1]
            previous = keep_ref[slot + 2]
            outside = value


def last_outer_kernel(
    single,
    rows,
    x_ref,
    across_ref,
    down_ref,
    side_ref,
    inverse_ref,
    keep_ref,
    halo_ref,
    edge_ref,
    early_first_ref,
    early_second_ref,
    first_ref,
    second_ref,
    core_ref,
    out_ref,
    next_ref,
    held,
    sems,
):
    lines = x_ref.shape[1]
    early = [taken_by_parity(early_first_ref, early_second_ref, slot, lines) for slot in range(3)]
    late = [taken_by_parity(first_ref, second_ref, slot, lines) for slot in range(1 if single else 2)]
    leaving = []
    for side in range(2):
        if single:
            changes = halo_ref[5 + side] * late[0][side], late[0][side]
        else:
            changes = late[0][side], late[1][side]
        sides = early[1][side] + changes[0], early[2][side] + changes[1]
        outer = outer_rows(
            side,
            rows,
            0,
            (early[0][side], sides, halo_ref[side]),
            halo_ref[2] if side == 0 else down_ref[rows - 1],
            edge_ref[side],
            *(x_ref, across_ref, down_ref, side_ref, inverse_ref, keep_ref),
        )
        for row, value in outer.items():
            next_ref[row] = value
        half = rows // 2
        for first, width in chunks_of(held.shape[1], CHUNKS):
            for top in range(side * half, side * half + half, 8):
                for start in range(first, first + width, LANES):
                    held[pl.ds(top, 8), pl.ds(start, LANES)] = next_ref[pl.ds(top, 8), start // LANES, :]
            part = pl.ds(side * half, half), pl.ds(first, width)
            copy = pltpu.make_async_copy(held.at[part], out_ref.at[part], sems.at[len(leaving)])
            copy.start()
            leaving.append(copy)
    for copy in leaving:
        copy.wait()


def call(kernel, name, ins, outs, scratch=(), aliases=None, work=None):
    spaces = {"vmem": pltpu.VMEM, "hbm": pltpu.HBM, "any": pl.ANY}
    return pl.pallas_call(
        kernel,
        out_shape=[jax.ShapeDtypeStruct(shape, *(kind or [jnp.float32])) for _, shape, *kind in outs],
        in_specs=[pl.BlockSpec(memory_space=spaces[space]) for space, _ in ins],
        out_specs=[pl.BlockSpec(memory_space=spaces[space]) for space, *_ in outs],
        scratch_shapes=list(scratch),
        input_output_aliases=aliases or {},
        compiler_params=pltpu.CompilerParams(vmem_limit_bytes=40 * 1024 * 1024),
        cost_estimate=work and pl.CostEstimate(flops=work, bytes_accessed=work, transcendentals=0),
        name=name,
    )(*(pltpu.with_memory_space_constraint(array, pltpu.HBM) if space == "hbm" else array for space, array in ins))


def routes(tiles, layers):
    def at(tile, layer):
        return tile * layers + layer % layers

    everywhere = [(tile, layer) for tile in range(tiles) for layer in range(layers)]
    up = [(at(t, l), at(t, l + 1)) for t, l in everywhere]
    down = [(at(t, l), at(t, l - 1)) for t, l in everywhere]
    first, second = [], []
    for t, l in everywhere:
        first.append((at(t, l), at(t ^ 1, l)))
        beyond = t + 1 if t % 2 else t - 1
        if 0 <= beyond < tiles:
            second.append((at(t, l), at(beyond, l)))
        else:
            second.append((at(t, l), at(t, l + 1)))
    return up, down, first, second


def local(class_index, class_conductance, loads, start_volts, via_cells, via_counts):
    rows, cols = loads.shape[1:]
    lines = cols // LANES
    tiles, layers = lax.axis_size("tile"), lax.axis_size("layer")
    up, down, first, second = routes(tiles, layers)
    single = layers == 2
    move = functools.partial(lax.ppermute, axis_name=("tile", "layer"))

    def rows_of(count):
        return (count, lines, LANES)

    def messages(count, longer):
        return [("vmem", (count * lines + (FILL if longer == side else 0), LANES)) for side in range(2)]

    def vmem(*arrays):
        return [("vmem", array) for array in arrays]

    def between_layers(sends):
        if single:
            got = move(sends[0], perm=up)
            return got, got
        return move(sends[1], perm=down), move(sends[0], perm=up)

    def beside_tile(sent):
        across_chips = move(sent[1], perm=second)
        return move(sent[0], perm=first), across_chips

    field = ("vmem", rows_of(rows))
    work = [pltpu.VMEM(rows_of(rows), jnp.float32)] * SWEEPS
    pick_count = 1 if single else 2
    picks = [("vmem", rows_of(1))] * pick_count

    cells = via_cells.reshape(lines, LANES)
    counts = via_counts.reshape(lines, LANES)
    low = move(cells, perm=up)
    low_count = move(counts, perm=up)
    (table,) = call(table_kernel, "table", vmem(class_conductance), [("vmem", (8, LANES))], work=10**9)
    across, downward, x, own, own_weight = call(
        unpack_kernel,
        "unpack",
        vmem(class_index, start_volts, cells, counts, table),
        [field] * 3 + [("vmem", cells.shape, cells.dtype), ("vmem", cells.shape)],
    )
    vias = (own, own_weight, low, low_count)
    first_sent, second_sent, *sends = call(
        functools.partial(links_kernel, single),
        "links",
        vmem(x, across, downward, own, low),
        messages(4 if single else 3, 1) + picks,
    )
    above, below = between_layers(sends)
    (load,) = call(unpack_field_kernel, "unpack_loads", vmem(loads), [field])
    early = beside_tile((first_sent, second_sent))
    sent = call(
        functools.partial(first_edges_kernel, rows),
        "first_edges",
        vmem(x, across, downward, load, *vias, above, below),
        messages(3, 0),
        work=2 * 10**10,
    )
    got = beside_tile(sent)
    core, side, inverse, keep, halo, picked = call(
        functools.partial(first_inner_kernel, single, rows),
        "first_inner",
        vmem(x, across, downward, load, *vias, above, below, *early) + [("any", sent[1])],
        [field, field, field, ("vmem", rows_of(KEPT)), ("vmem", rows_of(7 if single else 5)), ("vmem", rows_of(pick_count))],
        work,
    )
    x, edge, *sends = call(
        functools.partial(first_outer_kernel, single, rows),
        "first_outer",
        vmem(x, across, downward, side, inverse, keep, halo, picked, own, low, *got, core),
        [field, ("vmem", rows_of(2))] + picks,
        aliases={12: 0},
    )
    above, below = between_layers(sends)
    sent = call(
        functools.partial(next_early_kernel, single, rows),
        "next_early",
        vmem(x, across, downward, load, inverse, *vias) + [("any", sends[0])],
        messages(3, 1) + [("vmem", cells.shape)] * (2 if single else 0),
    )
    early = beside_tile(sent[:2])
    if single:
        late = call(
            next_late_single_kernel,
            "next_late",
            vmem(*sent[2:], above),
            messages(1, 1),
            work=2 * 10**10,
        )
    else:
        late = call(
            functools.partial(next_late_kernel, rows),
            "next_late",
            vmem(downward, inverse, *vias, above, below),
            messages(2, 1),
            work=2 * 10**10,
        )
    got = beside_tile(late)
    core, side, keep = call(
        functools.partial(last_inner_kernel, rows),
        "last_inner",
        vmem(x, across, downward, load, inverse, *vias, above, below) + [("any", late[1])],
        [field, field, ("vmem", rows_of(KEPT))],
        work,
    )
    keep, core = call(
        functools.partial(last_middle_kernel, rows),
        "last_middle",
        vmem(x, across, downward, side, inverse, keep, halo, *early, core),
        [("vmem", rows_of(KEPT)), field],
        aliases={9: 1},
    )
    volts, _ = call(
        functools.partial(last_outer_kernel, single, rows),
        "last_outer",
        vmem(x, across, downward, side, inverse, keep, halo, edge, *early, *got, core),
        [("hbm", (rows, cols)), field],
        [pltpu.VMEM((rows, cols), jnp.float32), pltpu.SemaphoreType.DMA((2 * CHUNKS,))],
        aliases={12: 1},
    )
    return volts[None]


def solution(mesh):
    placed = (
        P("layer", None, "tile", None),
        P("layer", None),
        P("layer", "tile", None),
        P("layer", "tile", None),
        P("layer", "tile"),
        P("layer", "tile"),
    )
    return jax.shard_map(
        local, mesh=mesh, in_specs=placed, out_specs=P("layer", "tile", None), check_vma=False
    )
```

```python
import functools

import jax
import jax.numpy as jnp
from jax import lax
from jax.experimental import pallas as pl
from jax.experimental.pallas import tpu as pltpu
from jax.sharding import PartitionSpec as P

OUTER = 2
SWEEPS = 3
VIA_UNIT = 2.0
LOWER_BOUND = 0.05
UPPER_BOUND = 2.0
LANES = 128
CHUNKS = 2
FILL = 8


def chebyshev_terms(count):
    centre_value = 0.5 * (UPPER_BOUND + LOWER_BOUND)
    half_width = 0.5 * (UPPER_BOUND - LOWER_BOUND)
    sigma = centre_value / half_width
    rho_last = 1.0 / sigma
    terms = [(0.0, 1.0 / centre_value)]
    for index in range(1, count):
        rho_next = 1.0 / (2.0 * sigma - rho_last)
        terms.append((rho_next * rho_last, 2.0 * rho_next / half_width))
        rho_last = rho_next
    return terms


FACTORS = chebyshev_terms(SWEEPS)


def column_right(row):
    lane = lax.broadcasted_iota(jnp.int32, row.shape, 1)
    turned = pltpu.roll(row, LANES - 1, 1)
    return jnp.where(lane == LANES - 1, pltpu.roll(turned, row.shape[0] - 1, 0), turned)


def column_left(row):
    lane = lax.broadcasted_iota(jnp.int32, row.shape, 1)
    turned = pltpu.roll(row, 1, 1)
    return jnp.where(lane == 0, pltpu.roll(turned, 1, 0), turned)


def beside(x, across):
    return across * column_right(x) + column_left(across * x)


def place():
    return lax.axis_index("tile"), lax.axis_index("layer")


def weight_of(count_ref):
    return VIA_UNIT * count_ref[...].astype(jnp.float32)


def marked(cells, row, value):
    return jnp.where(cells == row, value, 0.0)


def pick(x_ref, cells, rows):
    total = jnp.zeros(cells.shape, jnp.float32)
    for row in range(rows):
        total = total + marked(cells, row, x_ref[row])
    return total


def chunks_of(cols, count):
    width = cols // count
    return [(first, width) for first in range(0, cols, width)]


def unpack_field_kernel(field_ref, out_ref):
    rows, cols = field_ref.shape[1:]
    for top in range(0, rows, 8):
        for start in range(0, cols, LANES):
            out_ref[pl.ds(top, 8), start // LANES, :] = field_ref[0, pl.ds(top, 8), pl.ds(start, LANES)]


def table_kernel(class_ref, table_ref):
    count = class_ref.shape[1]
    table_ref[...] = jnp.zeros(table_ref.shape, jnp.float32)
    table_ref[:, pl.ds(0, count)] = jnp.broadcast_to(class_ref[...], (8, count))


def unpack_volts_kernel(volts_ref, after_ref, x_ref):
    unpack_field_kernel(volts_ref, x_ref)


def unpack_kernel(index_ref, own_ref, count_ref, table_ref, across_ref, down_ref, cells_ref, weight_ref):
    cells_ref[...] = own_ref[...]
    weight_ref[...] = weight_of(count_ref)
    rows, cols = index_ref.shape[2:]
    tile, _ = place()
    last_tile = tile == lax.axis_size("tile") - 1
    table = table_ref[...]
    lane = lax.broadcasted_iota(jnp.int32, (8, LANES), 1)
    sub = lax.broadcasted_iota(jnp.int32, (8, LANES), 0)
    for top in range(0, rows, 8):
        part = pl.ds(top, 8)
        for start in range(0, cols, LANES):
            here, line = pl.ds(start, LANES), start // LANES
            across = jnp.take_along_axis(table, index_ref[0, 0, part, here], axis=1, mode="promise_in_bounds")
            if start + LANES == cols:
                across = jnp.where(lane == LANES - 1, 0.0, across)
            across_ref[part, line, :] = across
            down = jnp.take_along_axis(table, index_ref[0, 1, part, here], axis=1, mode="promise_in_bounds")
            if top + 8 == rows:
                down = jnp.where((sub == 7) & last_tile, 0.0, down)
            down_ref[part, line, :] = down


def via_terms(own_ref, own_weight_ref, low_ref, low_weight, from_above, from_below):
    _, layer = place()
    on_top = layer == lax.axis_size("layer") - 1
    own_weight = own_weight_ref[...]
    low_weight = jnp.where(layer == 0, 0.0, low_weight)
    fixed_source = jnp.where(on_top, own_weight, 0.0)
    own, low = own_ref[...], low_ref[...]

    def via(row):
        return marked(own, row, own_weight) + marked(low, row, low_weight)

    def fixed(row):
        return marked(own, row, fixed_source)

    if from_above is None:
        return via, fixed, None
    own_source = jnp.where(on_top, 0.0, own_weight * from_above)
    low_source = low_weight * from_below

    def moving(row):
        return marked(own, row, own_source) + marked(low, row, low_source)

    return via, fixed, moving


def send_by_parity(first_ref, second_ref, slot, top, bottom):
    tile, _ = place()
    even = lax.rem(tile, 2) == 0
    part = pl.ds(slot * top.shape[0], top.shape[0])
    first_ref[part] = jnp.where(even, bottom, top)
    second_ref[part] = jnp.where(even, top, bottom)
    lengths = first_ref.shape[0], second_ref.shape[0]
    if slot == 0:
        longer = first_ref if lengths[0] > lengths[1] else second_ref
        longer[pl.ds(min(lengths), FILL)] = jnp.zeros((FILL, LANES), jnp.float32)


def taken_by_parity(first_ref, second_ref, slot, lines):
    tile, _ = place()
    even = lax.rem(tile, 2) == 0
    part = pl.ds(slot * lines, lines)
    first, second = first_ref[part], second_ref[part]
    return jnp.where(even, second, first), jnp.where(even, first, second)


def edge_flow(x_ref, across_ref, down_ref, row):
    return beside(x_ref[row], across_ref[row]) + down_ref[row] * x_ref[row + 1] + down_ref[row - 1] * x_ref[row - 1]


def edge_ends(rows):
    return (0, 1, 0), (rows - 1, rows - 2, rows - 2)


def edges(x_ref, across_ref, down_ref, right_side, inverses, rows):
    found = []
    for (edge, within, link), inverse in zip(edge_ends(rows), inverses):
        x = x_ref[within]
        flow = edge_flow(x_ref, across_ref, down_ref, within)
        later = x + FACTORS[0][1] * (inverse * (right_side(within) + flow) - x)
        found.append((right_side(edge) + down_ref[link] * x, right_side(edge) + down_ref[link] * later))
    return tuple(zip(*found))


def links_kernel(
    single, x_ref, across_ref, down_ref, own_ref, low_ref, first_ref, second_ref, *sends
):
    rows = x_ref.shape[0]
    links = chosen(single, own_ref[...], low_ref[...])
    for send_ref, cells in zip(sends, links):
        send_ref[0] = pick(x_ref, cells, rows)
    for slot, ref in enumerate((x_ref, across_ref, down_ref)):
        send_by_parity(first_ref, second_ref, slot, ref[0], ref[rows - 1])
    if single:
        send_by_parity(first_ref, second_ref, 3, marked(links[0], 0, 1.0), marked(links[0], rows - 1, 1.0))


def first_edges_kernel(
    rows,
    x_ref,
    across_ref,
    down_ref,
    loads_ref,
    own_ref,
    own_weight_ref,
    low_ref,
    low_count_ref,
    above_ref,
    below_ref,
    first_ref,
    second_ref,
):
    via, fixed, moving = via_terms(own_ref, own_weight_ref, low_ref, weight_of(low_count_ref), above_ref[0], below_ref[0])

    def right_side(row):
        return fixed(row) + moving(row) - loads_ref[row]

    def diagonal(row, links):
        across = across_ref[row]
        total = across + column_left(across)
        for link in links:
            total = total + down_ref[link]
        return total + via(row)

    inverses = 1.0 / diagonal(1, (0, 1)), 1.0 / diagonal(rows - 2, (rows - 3, rows - 2))
    for slot, pair in enumerate(edges(x_ref, across_ref, down_ref, right_side, inverses, rows)):
        send_by_parity(first_ref, second_ref, slot, *pair)
    send_by_parity(first_ref, second_ref, 2, diagonal(0, (0,)), diagonal(rows - 1, (rows - 2,)))


def next_early_kernel(
    single,
    rows,
    x_ref,
    across_ref,
    down_ref,
    loads_ref,
    inverse_ref,
    own_ref,
    own_weight_ref,
    low_ref,
    low_count_ref,
    after_ref,
    first_ref,
    second_ref,
    *factor_refs,
):
    _, layer = place()
    _, fixed, _ = via_terms(own_ref, own_weight_ref, low_ref, weight_of(low_count_ref), None, None)

    def right_side(row):
        return fixed(row) - loads_ref[row]

    send_by_parity(first_ref, second_ref, 0, x_ref[0], x_ref[rows - 1])
    inverses = inverse_ref[1], inverse_ref[rows - 2]
    for slot, pair in enumerate(edges(x_ref, across_ref, down_ref, right_side, inverses, rows)):
        send_by_parity(first_ref, second_ref, 1 + slot, *pair)
    if single:
        cells = jnp.where(layer == 0, own_ref[...], low_ref[...])
        weight = jnp.where(layer == 0, own_weight_ref[...], weight_of(low_count_ref))
        factors = []
        for (edge, within, link), inverse in zip(edge_ends(rows), inverses):
            share = FACTORS[0][1] * inverse * down_ref[link]
            factors.append(marked(cells, edge, weight) + marked(cells, within, weight * share))
        for ref, factor in zip(factor_refs, factors):
            ref[...] = factor


def next_late_kernel(
    rows, down_ref, inverse_ref, own_ref, own_weight_ref, low_ref, low_count_ref, above_ref, below_ref, first_ref, second_ref
):
    _, _, moving = via_terms(own_ref, own_weight_ref, low_ref, weight_of(low_count_ref), above_ref[0], below_ref[0])
    found = []
    for edge, within, link in edge_ends(rows):
        change = moving(edge)
        share = FACTORS[0][1] * inverse_ref[within] * down_ref[link]
        found.append((change, change + share * moving(within)))
    for slot, pair in enumerate(zip(*found)):
        send_by_parity(first_ref, second_ref, slot, *pair)


def next_late_single_kernel(top_ref, bottom_ref, volts_ref, first_ref, second_ref):
    volts = volts_ref[0]
    send_by_parity(first_ref, second_ref, 0, top_ref[...] * volts, bottom_ref[...] * volts)


def relaxed(x, flow, side, inverse, previous, sweep):
    keep, gain = FACTORS[sweep]
    update = gain * (inverse * (side + flow) - x)
    if sweep > 0:
        update = update + keep * previous
    return x + update, update


def chosen(single, own, low):
    _, layer = place()
    return [jnp.where(layer == 0, own, low)] if single else [own, low]


def inner_rows(
    rows, reach, outside, x_ref, across_ref, down_ref, side_ref, inverse_ref, work, update_ref, core_ref, keep_ref
):
    sources = [x_ref, *work]
    targets = [*work, core_ref]
    for sweep in range(SWEEPS):
        source, target = sources[sweep], targets[sweep]
        for row in range(sweep + reach, rows - sweep - reach):
            x = source[row]
            flow = beside(x, across_ref[row])
            if row == 0:
                flow = flow + outside[0]
            else:
                flow = flow + down_ref[row - 1] * source[row - 1]
            if row == rows - 1:
                flow = flow + outside[1]
            else:
                flow = flow + down_ref[row] * source[row + 1]
            previous = update_ref[row] if sweep > 0 else None
            value, update = relaxed(x, flow, side_ref[row], inverse_ref[row], previous, sweep)
            target[row] = value
            if sweep < SWEEPS - 1:
                update_ref[row] = update
                for side, depth in ((0, row), (1, rows - 1 - row)):
                    slot = 3 * (2 * sweep + side)
                    if depth == sweep + reach:
                        keep_ref[slot] = value
                        keep_ref[slot + 2] = update
                    if depth == sweep + reach + 1:
                        keep_ref[slot + 1] = value


def outer_rows(side, rows, reach, halo, link, inverse_edge, x_ref, across_ref, down_ref, side_ref, inverse_ref, keep_ref):
    edge_x, edge_q, edge_across = halo

    def row_of(depth):
        return depth if side == 0 else rows - 1 - depth

    def link_out(depth):
        if depth == 0:
            return link
        return down_ref[depth - 1] if side == 0 else down_ref[rows - 1 - depth]

    def link_in(depth):
        return down_ref[depth] if side == 0 else down_ref[rows - 2 - depth]

    values = {-1: edge_x}
    for depth in range(reach + 1):
        values[depth] = x_ref[row_of(depth)]
    updates = {}
    for sweep in range(SWEEPS):
        found, changed = {}, {}
        if sweep < SWEEPS - 1:
            x = values[-1]
            flow = beside(x, edge_across) + link * values[0]
            found[-1], changed[-1] = relaxed(x, flow, edge_q[sweep], inverse_edge, updates.get(-1), sweep)
        for depth in range(sweep + reach):
            row = row_of(depth)
            x = values[depth]
            flow = beside(x, across_ref[row]) + link_out(depth) * values[depth - 1] + link_in(depth) * values[depth + 1]
            found[depth], changed[depth] = relaxed(x, flow, side_ref[row], inverse_ref[row], updates.get(depth), sweep)
        if sweep < SWEEPS - 1:
            slot = 3 * (2 * sweep + side)
            found[sweep + reach] = keep_ref[slot]
            changed[sweep + reach] = keep_ref[slot + 2]
            found[sweep + reach + 1] = keep_ref[slot + 1]
        values, updates = found, changed
    return {row_of(depth): value for depth, value in values.items()}


KEPT = 6 * (SWEEPS - 1)


def first_inner_kernel(
    single,
    rows,
    x_ref,
    across_ref,
    down_ref,
    loads_ref,
    own_ref,
    own_weight_ref,
    low_ref,
    low_count_ref,
    above_ref,
    below_ref,
    first_ref,
    second_ref,
    after_ref,
    core_ref,
    side_ref,
    inverse_ref,
    keep_ref,
    halo_ref,
    picked_ref,
    *scratch,
):
    tile, _ = place()
    via, fixed, moving = via_terms(own_ref, own_weight_ref, low_ref, weight_of(low_count_ref), above_ref[0], below_ref[0])
    top_x, low_x = taken_by_parity(first_ref, second_ref, 0, x_ref.shape[1])
    top_across, low_across = taken_by_parity(first_ref, second_ref, 1, x_ref.shape[1])
    link, _ = taken_by_parity(first_ref, second_ref, 2, x_ref.shape[1])
    link = jnp.where(tile == 0, 0.0, link)
    held = [top_across, low_across, link, top_x, low_x]
    if single:
        held.extend(taken_by_parity(first_ref, second_ref, 3, x_ref.shape[1]))
    for slot, value in enumerate(held):
        halo_ref[slot] = value
    for row in range(rows):
        side_ref[row] = fixed(row) + moving(row) - loads_ref[row]
        across = across_ref[row]
        diagonal = across + column_left(across) + down_ref[row] + via(row)
        diagonal = diagonal + (down_ref[row - 1] if row > 0 else link)
        inverse_ref[row] = 1.0 / diagonal
    outside = link * top_x, down_ref[rows - 1] * low_x
    shared = (x_ref, across_ref, down_ref, side_ref, inverse_ref)
    inner_rows(rows, 0, outside, *shared, scratch[:-1], scratch[-1], core_ref, keep_ref)
    for index, cells in enumerate(chosen(single, own_ref[...], low_ref[...])):
        total = jnp.zeros(cells.shape, jnp.float32)
        for row in range(SWEEPS - 1, rows - SWEEPS + 1):
            total = total + marked(cells, row, core_ref[row])
        picked_ref[index] = total


def first_outer_kernel(
    single,
    rows,
    x_ref,
    across_ref,
    down_ref,
    side_ref,
    inverse_ref,
    keep_ref,
    halo_ref,
    picked_ref,
    own_ref,
    low_ref,
    first_ref,
    second_ref,
    core_ref,
    next_ref,
    edge_ref,
    *sends,
):
    top_q0, low_q0 = taken_by_parity(first_ref, second_ref, 0, x_ref.shape[1])
    top_q1, low_q1 = taken_by_parity(first_ref, second_ref, 1, x_ref.shape[1])
    top_diag, low_diag = taken_by_parity(first_ref, second_ref, 2, x_ref.shape[1])
    link, low_link = halo_ref[2], down_ref[rows - 1]
    top_inverse = 1.0 / (top_diag + link)
    low_inverse = 1.0 / (low_diag + low_link)
    edge_ref[0] = top_inverse
    edge_ref[1] = low_inverse
    shared = (x_ref, across_ref, down_ref, side_ref, inverse_ref, keep_ref)
    outer = outer_rows(0, rows, 0, (halo_ref[3], (top_q0, top_q1), halo_ref[0]), link, top_inverse, *shared)
    outer.update(
        outer_rows(1, rows, 0, (halo_ref[4], (low_q0, low_q1), halo_ref[1]), low_link, low_inverse, *shared)
    )
    for row, value in outer.items():
        next_ref[row] = value
    for index, cells in enumerate(chosen(single, own_ref[...], low_ref[...])):
        total = picked_ref[index]
        for row, value in outer.items():
            total = total + marked(cells, row, value)
        sends[index][0] = total


def last_inner_kernel(
    rows,
    x_ref,
    across_ref,
    down_ref,
    loads_ref,
    inverse_ref,
    own_ref,
    own_weight_ref,
    low_ref,
    low_count_ref,
    above_ref,
    below_ref,
    after_ref,
    core_ref,
    side_ref,
    keep_ref,
    *scratch,
):
    _, fixed, moving = via_terms(own_ref, own_weight_ref, low_ref, weight_of(low_count_ref), above_ref[0], below_ref[0])
    for row in range(rows):
        side_ref[row] = fixed(row) + moving(row) - loads_ref[row]
    shared = (x_ref, across_ref, down_ref, side_ref, inverse_ref)
    inner_rows(rows, 1, None, *shared, scratch[:-1], scratch[-1], core_ref, keep_ref)


def last_middle_kernel(
    rows,
    x_ref,
    across_ref,
    down_ref,
    side_ref,
    inverse_ref,
    keep_ref,
    halo_ref,
    first_ref,
    second_ref,
    core_ref,
    kept_ref,
    laid_ref,
    row_ref,
):
    edge_x = taken_by_parity(first_ref, second_ref, 0, x_ref.shape[1])
    for side in range(2):
        outside = halo_ref[2] * edge_x[0] if side == 0 else down_ref[rows - 1] * edge_x[1]
        further = x_ref[0 if side == 0 else rows - 1], x_ref[1 if side == 0 else rows - 2]
        previous = None
        for sweep in range(SWEEPS):
            row = sweep if side == 0 else rows - 1 - sweep
            links = (row - 1, row) if side == 0 else (row, row - 1)
            x, within = further
            flow = beside(x, across_ref[row]) + (outside if sweep == 0 else down_ref[links[0]] * outside)
            flow = flow + down_ref[links[1]] * within
            value, update = relaxed(x, flow, side_ref[row], inverse_ref[row], previous, sweep)
            if sweep == SWEEPS - 1:
                row_ref[side] = value
                break
            slot = 3 * (2 * sweep + side)
            kept_ref[slot] = value
            kept_ref[slot + 1] = keep_ref[slot]
            kept_ref[slot + 2] = update
            further = keep_ref[slot], keep_ref[slot + 1]
            previous = keep_ref[slot + 2]
            outside = value
    for top in range(0, rows, 8):
        for line in range(x_ref.shape[1]):
            laid_ref[pl.ds(top, 8), pl.ds(line * LANES, LANES)] = core_ref[pl.ds(top, 8), line, :]
    for side, row in enumerate((SWEEPS - 1, rows - SWEEPS)):
        for line in range(x_ref.shape[1]):
            laid_ref[pl.ds(row, 1), pl.ds(line * LANES, LANES)] = row_ref[side, pl.ds(line, 1), :]


def last_outer_kernel(
    single,
    rows,
    x_ref,
    across_ref,
    down_ref,
    side_ref,
    inverse_ref,
    keep_ref,
    halo_ref,
    edge_ref,
    early_first_ref,
    early_second_ref,
    first_ref,
    second_ref,
    laid_ref,
    out_ref,
    held,
    rim,
    sems,
):
    lines = x_ref.shape[1]
    early = [taken_by_parity(early_first_ref, early_second_ref, slot, lines) for slot in range(3)]
    late = [taken_by_parity(first_ref, second_ref, slot, lines) for slot in range(1 if single else 2)]
    leaving = []
    for side in range(2):
        if single:
            changes = halo_ref[5 + side] * late[0][side], late[0][side]
        else:
            changes = late[0][side], late[1][side]
        sides = early[1][side] + changes[0], early[2][side] + changes[1]
        outer = outer_rows(
            side,
            rows,
            0,
            (early[0][side], sides, halo_ref[side]),
            halo_ref[2] if side == 0 else down_ref[rows - 1],
            edge_ref[side],
            *(x_ref, across_ref, down_ref, side_ref, inverse_ref, keep_ref),
        )
        count = SWEEPS - 1
        base = 0 if side == 0 else rows - count
        for row, value in outer.items():
            rim[side, row - base] = value
        for line in range(lines):
            held[pl.ds(base, count), pl.ds(line * LANES, LANES)] = rim[side, :, line, :]
        part = pl.ds(side * (rows // 2), rows // 2)
        copy = pltpu.make_async_copy(held.at[part], out_ref.at[part], sems.at[side])
        copy.start()
        leaving.append(copy)
    for copy in leaving:
        copy.wait()


def call(kernel, name, ins, outs, scratch=(), aliases=None, work=None):
    spaces = {"vmem": pltpu.VMEM, "hbm": pltpu.HBM, "any": pl.ANY}
    return pl.pallas_call(
        kernel,
        out_shape=[jax.ShapeDtypeStruct(shape, *(kind or [jnp.float32])) for _, shape, *kind in outs],
        in_specs=[pl.BlockSpec(memory_space=spaces[space]) for space, _ in ins],
        out_specs=[pl.BlockSpec(memory_space=spaces[space]) for space, *_ in outs],
        scratch_shapes=list(scratch),
        input_output_aliases=aliases or {},
        compiler_params=pltpu.CompilerParams(vmem_limit_bytes=40 * 1024 * 1024),
        cost_estimate=work and pl.CostEstimate(flops=work, bytes_accessed=work, transcendentals=0),
        name=name,
    )(*(pltpu.with_memory_space_constraint(array, pltpu.HBM) if space == "hbm" else array for space, array in ins))


def routes(tiles, layers):
    def at(tile, layer):
        return tile * layers + layer % layers

    everywhere = [(tile, layer) for tile in range(tiles) for layer in range(layers)]
    up = [(at(t, l), at(t, l + 1)) for t, l in everywhere]
    down = [(at(t, l), at(t, l - 1)) for t, l in everywhere]
    first, second = [], []
    for t, l in everywhere:
        first.append((at(t, l), at(t ^ 1, l)))
        beyond = t + 1 if t % 2 else t - 1
        if 0 <= beyond < tiles:
            second.append((at(t, l), at(beyond, l)))
        else:
            second.append((at(t, l), at(t, l + 1)))
    return up, down, first, second


def local(class_index, class_conductance, loads, start_volts, via_cells, via_counts):
    rows, cols = loads.shape[1:]
    lines = cols // LANES
    tiles, layers = lax.axis_size("tile"), lax.axis_size("layer")
    up, down, first, second = routes(tiles, layers)
    single = layers == 2
    move = functools.partial(lax.ppermute, axis_name=("tile", "layer"))

    def rows_of(count):
        return (count, lines, LANES)

    def messages(count, longer):
        return [("vmem", (count * lines + (FILL if longer == side else 0), LANES)) for side in range(2)]

    def vmem(*arrays):
        return [("vmem", array) for array in arrays]

    def between_layers(sends):
        if single:
            got = move(sends[0], perm=up)
            return got, got
        return move(sends[1], perm=down), move(sends[0], perm=up)

    def beside_tile(sent):
        across_chips = move(sent[1], perm=second)
        return move(sent[0], perm=first), across_chips

    field = ("vmem", rows_of(rows))
    work = [pltpu.VMEM(rows_of(rows), jnp.float32)] * SWEEPS
    pick_count = 1 if single else 2
    picks = [("vmem", rows_of(1))] * pick_count

    cells = via_cells.reshape(lines, LANES)
    counts = via_counts.reshape(lines, LANES)
    low = move(cells, perm=up)
    low_count = move(counts, perm=up)
    (table,) = call(table_kernel, "table", vmem(class_conductance), [("vmem", (8, LANES))], work=3*10**8)
    across, downward, own, own_weight = call(
        unpack_kernel,
        "unpack",
        vmem(class_index, cells, counts, table),
        [field] * 2 + [("vmem", cells.shape, cells.dtype), ("vmem", cells.shape)],
        work=3*10**8,
    )
    (x,) = call(unpack_volts_kernel, "unpack_volts", vmem(start_volts) + [("any", across)], [field])
    vias = (own, own_weight, low, low_count)
    first_sent, second_sent, *sends = call(
        functools.partial(links_kernel, single),
        "links",
        vmem(x, across, downward, own, low),
        messages(4 if single else 3, 1) + picks,
    )
    above, below = between_layers(sends)
    (load,) = call(unpack_field_kernel, "unpack_loads", vmem(loads), [field])
    early = beside_tile((first_sent, second_sent))
    sent = call(
        functools.partial(first_edges_kernel, rows),
        "first_edges",
        vmem(x, across, downward, load, *vias, above, below),
        messages(3, 0),
        work=2 * 10**10,
    )
    got = beside_tile(sent)
    core, side, inverse, keep, halo, picked = call(
        functools.partial(first_inner_kernel, single, rows),
        "first_inner",
        vmem(x, across, downward, load, *vias, above, below, *early) + [("any", sent[1])],
        [field, field, field, ("vmem", rows_of(KEPT)), ("vmem", rows_of(7 if single else 5)), ("vmem", rows_of(pick_count))],
        work,
    )
    x, edge, *sends = call(
        functools.partial(first_outer_kernel, single, rows),
        "first_outer",
        vmem(x, across, downward, side, inverse, keep, halo, picked, own, low, *got, core),
        [field, ("vmem", rows_of(2))] + picks,
        aliases={12: 0},
    )
    above, below = between_layers(sends)
    sent = call(
        functools.partial(next_early_kernel, single, rows),
        "next_early",
        vmem(x, across, downward, load, inverse, *vias) + [("any", sends[0])],
        messages(3, 1) + [("vmem", cells.shape)] * (2 if single else 0),
    )
    early = beside_tile(sent[:2])
    if single:
        late = call(
            next_late_single_kernel,
            "next_late",
            vmem(*sent[2:], above),
            messages(1, 1),
            work=2 * 10**10,
        )
    else:
        late = call(
            functools.partial(next_late_kernel, rows),
            "next_late",
            vmem(downward, inverse, *vias, above, below),
            messages(2, 1),
            work=2 * 10**10,
        )
    got = beside_tile(late)
    core, side, keep = call(
        functools.partial(last_inner_kernel, rows),
        "last_inner",
        vmem(x, across, downward, load, inverse, *vias, above, below) + [("any", late[1])],
        [field, field, ("vmem", rows_of(KEPT))],
        work,
    )
    keep, laid = call(
        functools.partial(last_middle_kernel, rows),
        "last_middle",
        vmem(x, across, downward, side, inverse, keep, halo, *early, core),
        [("vmem", rows_of(KEPT)), ("vmem", (rows, cols))],
        [pltpu.VMEM(rows_of(2), jnp.float32)],
    )
    volts, _ = call(
        functools.partial(last_outer_kernel, single, rows),
        "last_outer",
        vmem(x, across, downward, side, inverse, keep, halo, edge, *early, *got, laid),
        [("hbm", (rows, cols)), ("vmem", (rows, cols))],
        [pltpu.VMEM((2, SWEEPS - 1, lines, LANES), jnp.float32), pltpu.SemaphoreType.DMA((2,))],
        aliases={12: 1},
    )
    return volts[None]


def solution(mesh):
    placed = (
        P("layer", None, "tile", None),
        P("layer", None),
        P("layer", "tile", None),
        P("layer", "tile", None),
        P("layer", "tile"),
        P("layer", "tile"),
    )
    return jax.shard_map(
        local, mesh=mesh, in_specs=placed, out_specs=P("layer", "tile", None), check_vma=False
    )
```

```python
import functools

import jax
import jax.numpy as jnp
from jax import lax
from jax.experimental import pallas as pl
from jax.experimental.pallas import tpu as pltpu
from jax.sharding import PartitionSpec as P

OUTER = 2
SWEEPS = 3
VIA_UNIT = 2.0
LOWER_BOUND = 0.05
UPPER_BOUND = 2.0
LANES = 128
CHUNKS = 2
FILL = 8


def chebyshev_terms(count):
    centre_value = 0.5 * (UPPER_BOUND + LOWER_BOUND)
    half_width = 0.5 * (UPPER_BOUND - LOWER_BOUND)
    sigma = centre_value / half_width
    rho_last = 1.0 / sigma
    terms = [(0.0, 1.0 / centre_value)]
    for index in range(1, count):
        rho_next = 1.0 / (2.0 * sigma - rho_last)
        terms.append((rho_next * rho_last, 2.0 * rho_next / half_width))
        rho_last = rho_next
    return terms


FACTORS = chebyshev_terms(SWEEPS)


def column_right(row):
    lane = lax.broadcasted_iota(jnp.int32, row.shape, 1)
    turned = pltpu.roll(row, LANES - 1, 1)
    return jnp.where(lane == LANES - 1, pltpu.roll(turned, row.shape[0] - 1, 0), turned)


def column_left(row):
    lane = lax.broadcasted_iota(jnp.int32, row.shape, 1)
    turned = pltpu.roll(row, 1, 1)
    return jnp.where(lane == 0, pltpu.roll(turned, 1, 0), turned)


def beside(x, across):
    return across * column_right(x) + column_left(across * x)


def place():
    return lax.axis_index("tile"), lax.axis_index("layer")


def weight_of(count_ref):
    return VIA_UNIT * count_ref[...].astype(jnp.float32)


def marked(cells, row, value):
    return jnp.where(cells == row, value, 0.0)


def pick(x_ref, cells, rows):
    total = jnp.zeros(cells.shape, jnp.float32)
    for row in range(rows):
        total = total + marked(cells, row, x_ref[row])
    return total


def chunks_of(cols, count):
    width = cols // count
    return [(first, width) for first in range(0, cols, width)]


def unpack_field_kernel(field_ref, out_ref):
    rows, cols = field_ref.shape[1:]
    for top in range(0, rows, 8):
        for start in range(0, cols, LANES):
            out_ref[pl.ds(top, 8), start // LANES, :] = field_ref[0, pl.ds(top, 8), pl.ds(start, LANES)]


def table_kernel(class_ref, table_ref):
    count = class_ref.shape[1]
    table_ref[...] = jnp.zeros(table_ref.shape, jnp.float32)
    table_ref[:, pl.ds(0, count)] = jnp.broadcast_to(class_ref[...], (8, count))


def unpack_loads_kernel(loads_ref, own_ref, weight_ref, out_ref):
    unpack_field_kernel(loads_ref, out_ref)
    _, layer = place()
    supplied = jnp.where(layer == lax.axis_size("layer") - 1, weight_ref[...], 0.0)
    cells = own_ref[...]
    for row in range(out_ref.shape[0]):
        out_ref[row] = out_ref[row] - marked(cells, row, supplied)


def unpack_volts_kernel(volts_ref, after_ref, x_ref):
    unpack_field_kernel(volts_ref, x_ref)


def unpack_kernel(index_ref, own_ref, count_ref, table_ref, across_ref, down_ref, cells_ref, weight_ref):
    cells_ref[...] = own_ref[...]
    weight_ref[...] = weight_of(count_ref)
    rows, cols = index_ref.shape[2:]
    tile, _ = place()
    last_tile = tile == lax.axis_size("tile") - 1
    table = table_ref[...]
    lane = lax.broadcasted_iota(jnp.int32, (8, LANES), 1)
    sub = lax.broadcasted_iota(jnp.int32, (8, LANES), 0)
    for top in range(0, rows, 8):
        part = pl.ds(top, 8)
        for start in range(0, cols, LANES):
            here, line = pl.ds(start, LANES), start // LANES
            across = jnp.take_along_axis(table, index_ref[0, 0, part, here], axis=1, mode="promise_in_bounds")
            if start + LANES == cols:
                across = jnp.where(lane == LANES - 1, 0.0, across)
            across_ref[part, line, :] = across
            down = jnp.take_along_axis(table, index_ref[0, 1, part, here], axis=1, mode="promise_in_bounds")
            if top + 8 == rows:
                down = jnp.where((sub == 7) & last_tile, 0.0, down)
            down_ref[part, line, :] = down


def via_terms(own_ref, own_weight_ref, low_ref, low_weight, from_above, from_below):
    _, layer = place()
    layers = lax.axis_size("layer")
    own_weight = own_weight_ref[...]
    low_weight = jnp.where(layer == 0, 0.0, low_weight)
    own, low = own_ref[...], low_ref[...]

    def via(row):
        return marked(own, row, own_weight) + marked(low, row, low_weight)

    if layers == 2:
        cells = jnp.where(layer == 0, own, low)
        source = jnp.where(layer == 0, own_weight, low_weight) * from_above

        def moving(row):
            return marked(cells, row, source)

        return via, moving
    own_source = jnp.where(layer == layers - 1, 0.0, own_weight * from_above)
    low_source = low_weight * from_below

    def moving(row):
        return marked(own, row, own_source) + marked(low, row, low_source)

    return via, moving


def send_by_parity(first_ref, second_ref, slot, top, bottom):
    tile, _ = place()
    even = lax.rem(tile, 2) == 0
    part = pl.ds(slot * top.shape[0], top.shape[0])
    first_ref[part] = jnp.where(even, bottom, top)
    second_ref[part] = jnp.where(even, top, bottom)
    lengths = first_ref.shape[0], second_ref.shape[0]
    if slot == 0:
        longer = first_ref if lengths[0] > lengths[1] else second_ref
        longer[pl.ds(min(lengths), FILL)] = jnp.zeros((FILL, LANES), jnp.float32)


def by_parity(work):
    tile, _ = place()
    even = lax.rem(tile, 2) == 0
    for side in range(2):
        pl.when(even if side == 1 else jnp.logical_not(even))(functools.partial(work, side))


def taken_by_parity(first_ref, second_ref, slot, lines):
    tile, _ = place()
    even = lax.rem(tile, 2) == 0
    part = pl.ds(slot * lines, lines)
    first, second = first_ref[part], second_ref[part]
    return jnp.where(even, second, first), jnp.where(even, first, second)


def edge_flow(x_ref, across_ref, down_ref, row):
    return beside(x_ref[row], across_ref[row]) + down_ref[row] * x_ref[row + 1] + down_ref[row - 1] * x_ref[row - 1]


def edge_ends(rows):
    return (0, 1, 0), (rows - 1, rows - 2, rows - 2)


def edges(x_ref, across_ref, down_ref, right_side, inverses, rows):
    found = []
    for (edge, within, link), inverse in zip(edge_ends(rows), inverses):
        x = x_ref[within]
        flow = edge_flow(x_ref, across_ref, down_ref, within)
        later = x + FACTORS[0][1] * (inverse * (right_side(within) + flow) - x)
        found.append((right_side(edge) + down_ref[link] * x, right_side(edge) + down_ref[link] * later))
    return tuple(zip(*found))


def links_kernel(
    single, x_ref, across_ref, down_ref, own_ref, low_ref, first_ref, second_ref, *sends
):
    rows = x_ref.shape[0]
    links = chosen(single, own_ref[...], low_ref[...])
    for send_ref, cells in zip(sends, links):
        send_ref[0] = pick(x_ref, cells, rows)
    for slot, ref in enumerate((x_ref, across_ref, down_ref)):
        send_by_parity(first_ref, second_ref, slot, ref[0], ref[rows - 1])
    if single:
        send_by_parity(first_ref, second_ref, 3, marked(links[0], 0, 1.0), marked(links[0], rows - 1, 1.0))


def first_edges_kernel(
    rows,
    x_ref,
    across_ref,
    down_ref,
    loads_ref,
    own_ref,
    own_weight_ref,
    low_ref,
    low_count_ref,
    above_ref,
    below_ref,
    first_ref,
    second_ref,
):
    via, moving = via_terms(own_ref, own_weight_ref, low_ref, weight_of(low_count_ref), above_ref[0], below_ref[0])

    def right_side(row):
        return moving(row) - loads_ref[row]

    def diagonal(row, links):
        across = across_ref[row]
        total = across + column_left(across)
        for link in links:
            total = total + down_ref[link]
        return total + via(row)

    inverses = 1.0 / diagonal(1, (0, 1)), 1.0 / diagonal(rows - 2, (rows - 3, rows - 2))
    for slot, pair in enumerate(edges(x_ref, across_ref, down_ref, right_side, inverses, rows)):
        send_by_parity(first_ref, second_ref, slot, *pair)
    send_by_parity(first_ref, second_ref, 2, diagonal(0, (0,)), diagonal(rows - 1, (rows - 2,)))


def next_early_kernel(
    single,
    rows,
    x_ref,
    across_ref,
    down_ref,
    loads_ref,
    inverse_ref,
    own_ref,
    own_weight_ref,
    low_ref,
    low_count_ref,
    after_ref,
    first_ref,
    second_ref,
    *factor_refs,
):
    _, layer = place()

    def right_side(row):
        return -loads_ref[row]

    send_by_parity(first_ref, second_ref, 0, x_ref[0], x_ref[rows - 1])
    inverses = inverse_ref[1], inverse_ref[rows - 2]
    for slot, pair in enumerate(edges(x_ref, across_ref, down_ref, right_side, inverses, rows)):
        send_by_parity(first_ref, second_ref, 1 + slot, *pair)
    if single:
        cells = jnp.where(layer == 0, own_ref[...], low_ref[...])
        weight = jnp.where(layer == 0, own_weight_ref[...], weight_of(low_count_ref))
        factors = []
        for (edge, within, link), inverse in zip(edge_ends(rows), inverses):
            share = FACTORS[0][1] * inverse * down_ref[link]
            factors.append(marked(cells, edge, weight) + marked(cells, within, weight * share))
        for ref, factor in zip(factor_refs, factors):
            ref[...] = factor


def next_late_kernel(
    rows, down_ref, inverse_ref, own_ref, own_weight_ref, low_ref, low_count_ref, above_ref, below_ref, first_ref, second_ref
):
    _, moving = via_terms(own_ref, own_weight_ref, low_ref, weight_of(low_count_ref), above_ref[0], below_ref[0])
    found = []
    for edge, within, link in edge_ends(rows):
        change = moving(edge)
        share = FACTORS[0][1] * inverse_ref[within] * down_ref[link]
        found.append((change, change + share * moving(within)))
    for slot, pair in enumerate(zip(*found)):
        send_by_parity(first_ref, second_ref, slot, *pair)


def next_late_single_kernel(top_ref, bottom_ref, volts_ref, first_ref, second_ref):
    volts = volts_ref[0]
    send_by_parity(first_ref, second_ref, 0, top_ref[...] * volts, bottom_ref[...] * volts)


def relaxed(x, flow, side, inverse, previous, sweep):
    keep, gain = FACTORS[sweep]
    update = gain * (inverse * (side + flow) - x)
    if sweep > 0:
        update = update + keep * previous
    return x + update, update


def chosen(single, own, low):
    _, layer = place()
    return [jnp.where(layer == 0, own, low)] if single else [own, low]


def inner_rows(
    rows, reach, outside, x_ref, across_ref, down_ref, side_ref, inverse_ref, work, update_ref, core_ref, keep_ref
):
    sources = [x_ref, *work]
    targets = [*work, core_ref]
    for sweep in range(SWEEPS):
        source, target = sources[sweep], targets[sweep]
        for row in range(sweep + reach, rows - sweep - reach):
            x = source[row]
            flow = beside(x, across_ref[row])
            if row == 0:
                flow = flow + outside[0]
            else:
                flow = flow + down_ref[row - 1] * source[row - 1]
            if row == rows - 1:
                flow = flow + outside[1]
            else:
                flow = flow + down_ref[row] * source[row + 1]
            previous = update_ref[row] if sweep > 0 else None
            value, update = relaxed(x, flow, side_ref[row], inverse_ref[row], previous, sweep)
            target[row] = value
            if sweep < SWEEPS - 1:
                update_ref[row] = update
                for side, depth in ((0, row), (1, rows - 1 - row)):
                    slot = 3 * (2 * sweep + side)
                    if depth == sweep + reach:
                        keep_ref[slot] = value
                        keep_ref[slot + 2] = update
                    if depth == sweep + reach + 1:
                        keep_ref[slot + 1] = value


def outer_rows(side, rows, reach, halo, link, inverse_edge, x_ref, across_ref, down_ref, side_ref, inverse_ref, keep_ref):
    edge_x, edge_q, edge_across = halo

    def row_of(depth):
        return depth if side == 0 else rows - 1 - depth

    def link_out(depth):
        if depth == 0:
            return link
        return down_ref[depth - 1] if side == 0 else down_ref[rows - 1 - depth]

    def link_in(depth):
        return down_ref[depth] if side == 0 else down_ref[rows - 2 - depth]

    values = {-1: edge_x}
    for depth in range(reach + 1):
        values[depth] = x_ref[row_of(depth)]
    updates = {}
    for sweep in range(SWEEPS):
        found, changed = {}, {}
        if sweep < SWEEPS - 1:
            x = values[-1]
            flow = beside(x, edge_across) + link * values[0]
            found[-1], changed[-1] = relaxed(x, flow, edge_q[sweep], inverse_edge, updates.get(-1), sweep)
        for depth in range(sweep + reach):
            row = row_of(depth)
            x = values[depth]
            flow = beside(x, across_ref[row]) + link_out(depth) * values[depth - 1] + link_in(depth) * values[depth + 1]
            found[depth], changed[depth] = relaxed(x, flow, side_ref[row], inverse_ref[row], updates.get(depth), sweep)
        if sweep < SWEEPS - 1:
            slot = 3 * (2 * sweep + side)
            found[sweep + reach] = keep_ref[slot]
            changed[sweep + reach] = keep_ref[slot + 2]
            found[sweep + reach + 1] = keep_ref[slot + 1]
        values, updates = found, changed
    return {row_of(depth): value for depth, value in values.items()}


KEPT = 6 * (SWEEPS - 1)


def first_inner_kernel(
    single,
    rows,
    x_ref,
    across_ref,
    down_ref,
    loads_ref,
    own_ref,
    own_weight_ref,
    low_ref,
    low_count_ref,
    above_ref,
    below_ref,
    first_ref,
    second_ref,
    after_ref,
    core_ref,
    side_ref,
    inverse_ref,
    keep_ref,
    halo_ref,
    picked_ref,
    *scratch,
):
    tile, _ = place()
    via, moving = via_terms(own_ref, own_weight_ref, low_ref, weight_of(low_count_ref), above_ref[0], below_ref[0])
    top_x, low_x = taken_by_parity(first_ref, second_ref, 0, x_ref.shape[1])
    top_across, low_across = taken_by_parity(first_ref, second_ref, 1, x_ref.shape[1])
    link, _ = taken_by_parity(first_ref, second_ref, 2, x_ref.shape[1])
    link = jnp.where(tile == 0, 0.0, link)
    held = [top_across, low_across, link, top_x, low_x]
    if single:
        held.extend(taken_by_parity(first_ref, second_ref, 3, x_ref.shape[1]))
    for slot, value in enumerate(held):
        halo_ref[slot] = value
    for row in range(rows):
        side_ref[row] = moving(row) - loads_ref[row]
        across = across_ref[row]
        diagonal = across + column_left(across) + down_ref[row] + via(row)
        diagonal = diagonal + (down_ref[row - 1] if row > 0 else link)
        inverse_ref[row] = 1.0 / diagonal
    outside = link * top_x, down_ref[rows - 1] * low_x
    shared = (x_ref, across_ref, down_ref, side_ref, inverse_ref)
    inner_rows(rows, 0, outside, *shared, scratch[:-1], scratch[-1], core_ref, keep_ref)
    for index, cells in enumerate(chosen(single, own_ref[...], low_ref[...])):
        total = jnp.zeros(cells.shape, jnp.float32)
        for row in range(SWEEPS - 1, rows - SWEEPS + 1):
            total = total + marked(cells, row, core_ref[row])
        picked_ref[index] = total


def first_rim(
    single,
    rows,
    side,
    x_ref,
    across_ref,
    down_ref,
    side_ref,
    inverse_ref,
    keep_ref,
    halo_ref,
    own_ref,
    low_ref,
    picked_ref,
    late_ref,
    next_ref,
    edge_ref,
    totals,
):
    lines = x_ref.shape[1]
    q0, q1, diagonal = (late_ref[pl.ds(slot * lines, lines)] for slot in range(3))
    link = halo_ref[2] if side == 0 else down_ref[rows - 1]
    inverse = 1.0 / (diagonal + link)
    edge_ref[side] = inverse
    shared = (x_ref, across_ref, down_ref, side_ref, inverse_ref, keep_ref)
    outer = outer_rows(side, rows, 0, (halo_ref[3 + side], (q0, q1), halo_ref[side]), link, inverse, *shared)
    for row, value in outer.items():
        next_ref[row] = value
    for index, cells in enumerate(chosen(single, own_ref[...], low_ref[...])):
        total = picked_ref[index]
        for row, value in outer.items():
            total = total + marked(cells, row, value)
        totals(index, total)


def first_near_kernel(single, rows, *refs):
    *ins, _, next_ref, edge_ref, found_ref = refs

    def found(index, total):
        found_ref[index] = total

    by_parity(lambda side: first_rim(single, rows, side, *ins, next_ref, edge_ref, found))


def first_far_kernel(single, rows, *refs):
    count = 1 if single else 2
    *ins, _, _, next_ref, edge_ref = refs[:-count]
    sends = refs[-count:]

    def found(index, total):
        sends[index][0] = total

    by_parity(lambda near: first_rim(single, rows, 1 - near, *ins, next_ref, edge_ref, found))


def last_inner_kernel(
    rows,
    x_ref,
    across_ref,
    down_ref,
    loads_ref,
    inverse_ref,
    own_ref,
    own_weight_ref,
    low_ref,
    low_count_ref,
    above_ref,
    below_ref,
    after_ref,
    core_ref,
    side_ref,
    keep_ref,
    *scratch,
):
    _, moving = via_terms(own_ref, own_weight_ref, low_ref, weight_of(low_count_ref), above_ref[0], below_ref[0])
    for row in range(rows):
        side_ref[row] = moving(row) - loads_ref[row]
    shared = (x_ref, across_ref, down_ref, side_ref, inverse_ref)
    inner_rows(rows, 1, None, *shared, scratch[:-1], scratch[-1], core_ref, keep_ref)


def last_middle_kernel(
    single,
    rows,
    x_ref,
    across_ref,
    down_ref,
    side_ref,
    inverse_ref,
    keep_ref,
    halo_ref,
    edge_ref,
    first_ref,
    second_ref,
    late_ref,
    core_ref,
    kept_ref,
    laid_ref,
    row_ref,
    rim,
):
    edge_x = taken_by_parity(first_ref, second_ref, 0, x_ref.shape[1])
    for side in range(2):
        outside = halo_ref[2] * edge_x[0] if side == 0 else down_ref[rows - 1] * edge_x[1]
        further = x_ref[0 if side == 0 else rows - 1], x_ref[1 if side == 0 else rows - 2]
        previous = None
        for sweep in range(SWEEPS):
            row = sweep if side == 0 else rows - 1 - sweep
            links = (row - 1, row) if side == 0 else (row, row - 1)
            x, within = further
            flow = beside(x, across_ref[row]) + (outside if sweep == 0 else down_ref[links[0]] * outside)
            flow = flow + down_ref[links[1]] * within
            value, update = relaxed(x, flow, side_ref[row], inverse_ref[row], previous, sweep)
            if sweep == SWEEPS - 1:
                row_ref[side] = value
                break
            slot = 3 * (2 * sweep + side)
            kept_ref[slot] = value
            kept_ref[slot + 1] = keep_ref[slot]
            kept_ref[slot + 2] = update
            further = keep_ref[slot], keep_ref[slot + 1]
            previous = keep_ref[slot + 2]
            outside = value
    for top in range(0, rows, 8):
        for line in range(x_ref.shape[1]):
            laid_ref[pl.ds(top, 8), pl.ds(line * LANES, LANES)] = core_ref[pl.ds(top, 8), line, :]
    for side, row in enumerate((SWEEPS - 1, rows - SWEEPS)):
        for line in range(x_ref.shape[1]):
            laid_ref[pl.ds(row, 1), pl.ds(line * LANES, LANES)] = row_ref[side, pl.ds(line, 1), :]
    known = (x_ref, across_ref, down_ref, side_ref, inverse_ref, kept_ref, halo_ref, edge_ref)
    by_parity(lambda near: rim_rows(single, rows, near, *known, first_ref, late_ref, laid_ref, rim))


def rim_rows(
    single,
    rows,
    side,
    x_ref,
    across_ref,
    down_ref,
    side_ref,
    inverse_ref,
    keep_ref,
    halo_ref,
    edge_ref,
    early_ref,
    late_ref,
    laid_ref,
    rim,
):
    lines = x_ref.shape[1]

    def row_of(ref, slot):
        return ref[pl.ds(slot * lines, lines)]

    if single:
        changes = halo_ref[5 + side] * row_of(late_ref, 0), row_of(late_ref, 0)
    else:
        changes = row_of(late_ref, 0), row_of(late_ref, 1)
    sides = row_of(early_ref, 1) + changes[0], row_of(early_ref, 2) + changes[1]
    outer = outer_rows(
        side,
        rows,
        0,
        (row_of(early_ref, 0), sides, halo_ref[side]),
        halo_ref[2] if side == 0 else down_ref[rows - 1],
        edge_ref[side],
        *(x_ref, across_ref, down_ref, side_ref, inverse_ref, keep_ref),
    )
    count = SWEEPS - 1
    base = 0 if side == 0 else rows - count
    for row, value in outer.items():
        rim[row - base] = value
    for line in range(lines):
        laid_ref[pl.ds(base, count), pl.ds(line * LANES, LANES)] = rim[:, line, :]


def last_far_kernel(single, rows, *refs):
    *ins, _, out_ref, laid_ref, rim, sems = refs
    half = rows // 2

    def work(near):
        copies = []
        for side in (near, 1 - near):
            if side != near:
                rim_rows(single, rows, side, *ins, laid_ref, rim)
            part = pl.ds(side * half, half)
            copy = pltpu.make_async_copy(laid_ref.at[part], out_ref.at[part], sems.at[side])
            copy.start()
            copies.append(copy)
        for copy in copies:
            copy.wait()

    by_parity(work)


def call(kernel, name, ins, outs, scratch=(), aliases=None, work=None):
    spaces = {"vmem": pltpu.VMEM, "hbm": pltpu.HBM, "any": pl.ANY}
    return pl.pallas_call(
        kernel,
        out_shape=[jax.ShapeDtypeStruct(shape, *(kind or [jnp.float32])) for _, shape, *kind in outs],
        in_specs=[pl.BlockSpec(memory_space=spaces[space]) for space, _ in ins],
        out_specs=[pl.BlockSpec(memory_space=spaces[space]) for space, *_ in outs],
        scratch_shapes=list(scratch),
        input_output_aliases=aliases or {},
        compiler_params=pltpu.CompilerParams(vmem_limit_bytes=40 * 1024 * 1024),
        cost_estimate=work and pl.CostEstimate(flops=work, bytes_accessed=work, transcendentals=0),
        name=name,
    )(*(pltpu.with_memory_space_constraint(array, pltpu.HBM) if space == "hbm" else array for space, array in ins))


def routes(tiles, layers):
    def at(tile, layer):
        return tile * layers + layer % layers

    everywhere = [(tile, layer) for tile in range(tiles) for layer in range(layers)]
    up = [(at(t, l), at(t, l + 1)) for t, l in everywhere]
    down = [(at(t, l), at(t, l - 1)) for t, l in everywhere]
    first, second = [], []
    for t, l in everywhere:
        first.append((at(t, l), at(t ^ 1, l)))
        beyond = t + 1 if t % 2 else t - 1
        if 0 <= beyond < tiles:
            second.append((at(t, l), at(beyond, l)))
        else:
            second.append((at(t, l), at(t, l + 1)))
    return up, down, first, second


def local(class_index, class_conductance, loads, start_volts, via_cells, via_counts):
    rows, cols = loads.shape[1:]
    lines = cols // LANES
    tiles, layers = lax.axis_size("tile"), lax.axis_size("layer")
    up, down, first, second = routes(tiles, layers)
    single = layers == 2
    move = functools.partial(lax.ppermute, axis_name=("tile", "layer"))

    def rows_of(count):
        return (count, lines, LANES)

    def messages(count, longer):
        return [("vmem", (count * lines + (FILL if longer == side else 0), LANES)) for side in range(2)]

    def vmem(*arrays):
        return [("vmem", array) for array in arrays]

    def between_layers(sends):
        if single:
            got = move(sends[0], perm=up)
            return got, got
        return move(sends[1], perm=down), move(sends[0], perm=up)

    def beside_tile(sent):
        across_chips = move(sent[1], perm=second)
        return move(sent[0], perm=first), across_chips

    field = ("vmem", rows_of(rows))
    work = [pltpu.VMEM(rows_of(rows), jnp.float32)] * SWEEPS
    pick_count = 1 if single else 2
    picks = [("vmem", rows_of(1))] * pick_count

    cells = via_cells.reshape(lines, LANES)
    counts = via_counts.reshape(lines, LANES)
    low = move(cells, perm=up)
    low_count = move(counts, perm=up)
    (table,) = call(table_kernel, "table", vmem(class_conductance), [("vmem", (8, LANES))], work=3*10**8)
    across, downward, own, own_weight = call(
        unpack_kernel,
        "unpack",
        vmem(class_index, cells, counts, table),
        [field] * 2 + [("vmem", cells.shape, cells.dtype), ("vmem", cells.shape)],
        work=3*10**8,
    )
    (x,) = call(unpack_volts_kernel, "unpack_volts", vmem(start_volts) + [("any", across)], [field])
    vias = (own, own_weight, low, low_count)
    first_sent, second_sent, *sends = call(
        functools.partial(links_kernel, single),
        "links",
        vmem(x, across, downward, own, low),
        messages(4 if single else 3, 1) + picks,
    )
    above, below = between_layers(sends)
    (load,) = call(unpack_loads_kernel, "unpack_loads", vmem(loads, own, own_weight), [field])
    early = beside_tile((first_sent, second_sent))
    sent = call(
        functools.partial(first_edges_kernel, rows),
        "first_edges",
        vmem(x, across, downward, load, *vias, above, below),
        messages(3, 0),
        work=2 * 10**10,
    )
    got = beside_tile(sent)
    core, side, inverse, keep, halo, picked = call(
        functools.partial(first_inner_kernel, single, rows),
        "first_inner",
        vmem(x, across, downward, load, *vias, above, below, *early) + [("any", sent[1])],
        [field, field, field, ("vmem", rows_of(KEPT)), ("vmem", rows_of(7 if single else 5)), ("vmem", rows_of(pick_count))],
        work,
    )
    known = vmem(x, across, downward, side, inverse, keep, halo, own, low)
    near_x, near_edge, near_picked = call(
        functools.partial(first_near_kernel, single, rows),
        "first_near",
        known + vmem(picked, got[0], core),
        [field, ("vmem", rows_of(2)), ("vmem", rows_of(pick_count))],
        aliases={11: 0},
    )
    x, edge, *sends = call(
        functools.partial(first_far_kernel, single, rows),
        "first_far",
        known + vmem(near_picked, got[1], near_x, near_edge),
        [field, ("vmem", rows_of(2))] + picks,
        aliases={11: 0, 12: 1},
    )
    above, below = between_layers(sends)
    sent = call(
        functools.partial(next_early_kernel, single, rows),
        "next_early",
        vmem(x, across, downward, load, inverse, *vias) + [("any", sends[0])],
        messages(3, 1) + [("vmem", cells.shape)] * (2 if single else 0),
    )
    early = beside_tile(sent[:2])
    if single:
        late = call(
            next_late_single_kernel,
            "next_late",
            vmem(*sent[2:], above),
            messages(1, 1),
            work=2 * 10**10,
        )
    else:
        late = call(
            functools.partial(next_late_kernel, rows),
            "next_late",
            vmem(downward, inverse, *vias, above, below),
            messages(2, 1),
            work=2 * 10**10,
        )
    got = beside_tile(late)
    core, side, keep = call(
        functools.partial(last_inner_kernel, rows),
        "last_inner",
        vmem(x, across, downward, load, inverse, *vias, above, below) + [("any", late[1])],
        [field, field, ("vmem", rows_of(KEPT))],
        work,
    )
    rim = pltpu.VMEM((SWEEPS - 1, lines, LANES), jnp.float32)
    keep, laid = call(
        functools.partial(last_middle_kernel, single, rows),
        "last_middle",
        vmem(x, across, downward, side, inverse, keep, halo, edge, *early, got[0], core),
        [("vmem", rows_of(KEPT)), ("vmem", (rows, cols))],
        [pltpu.VMEM(rows_of(2), jnp.float32), rim],
    )
    plane = ("vmem", (rows, cols))
    known = vmem(x, across, downward, side, inverse, keep, halo, edge)
    volts, _ = call(
        functools.partial(last_far_kernel, single, rows),
        "last_far",
        known + vmem(early[1], got[1], laid),
        [("hbm", (rows, cols)), plane],
        [rim, pltpu.SemaphoreType.DMA((2,))],
        aliases={10: 1},
    )
    return volts[None]


def solution(mesh):
    placed = (
        P("layer", None, "tile", None),
        P("layer", None),
        P("layer", "tile", None),
        P("layer", "tile", None),
        P("layer", "tile"),
        P("layer", "tile"),
    )
    return jax.shard_map(
        local, mesh=mesh, in_specs=placed, out_specs=P("layer", "tile", None), check_vma=False
    )
```

```python
import functools

import jax
import jax.numpy as jnp
from jax import lax
from jax.experimental import pallas as pl
from jax.experimental.pallas import tpu as pltpu
from jax.sharding import PartitionSpec as P

OUTER = 2
SWEEPS = 3
VIA_UNIT = 2.0
LOWER_BOUND = 0.05
UPPER_BOUND = 2.0
LANES = 128
CHUNKS = 2
FILL = 8


def chebyshev_terms(count):
    centre_value = 0.5 * (UPPER_BOUND + LOWER_BOUND)
    half_width = 0.5 * (UPPER_BOUND - LOWER_BOUND)
    sigma = centre_value / half_width
    rho_last = 1.0 / sigma
    terms = [(0.0, 1.0 / centre_value)]
    for index in range(1, count):
        rho_next = 1.0 / (2.0 * sigma - rho_last)
        terms.append((rho_next * rho_last, 2.0 * rho_next / half_width))
        rho_last = rho_next
    return terms


FACTORS = chebyshev_terms(SWEEPS)


def column_right(row):
    lane = lax.broadcasted_iota(jnp.int32, row.shape, 1)
    turned = pltpu.roll(row, LANES - 1, 1)
    return jnp.where(lane == LANES - 1, pltpu.roll(turned, row.shape[0] - 1, 0), turned)


def column_left(row):
    lane = lax.broadcasted_iota(jnp.int32, row.shape, 1)
    turned = pltpu.roll(row, 1, 1)
    return jnp.where(lane == 0, pltpu.roll(turned, 1, 0), turned)


def beside(x, across):
    return across * column_right(x) + column_left(across * x)


def place():
    return lax.axis_index("tile"), lax.axis_index("layer")


def weight_of(count_ref):
    return VIA_UNIT * count_ref[...].astype(jnp.float32)


def marked(cells, row, value):
    return jnp.where(cells == row, value, 0.0)


def pick(x_ref, cells, rows):
    total = jnp.zeros(cells.shape, jnp.float32)
    for row in range(rows):
        total = total + marked(cells, row, x_ref[row])
    return total


def chunks_of(cols, count):
    width = cols // count
    return [(first, width) for first in range(0, cols, width)]


def unpack_field_kernel(field_ref, out_ref):
    rows, cols = field_ref.shape[1:]
    for top in range(0, rows, 8):
        for start in range(0, cols, LANES):
            out_ref[pl.ds(top, 8), start // LANES, :] = field_ref[0, pl.ds(top, 8), pl.ds(start, LANES)]


def table_kernel(class_ref, table_ref):
    count = class_ref.shape[1]
    table_ref[...] = jnp.zeros(table_ref.shape, jnp.float32)
    table_ref[:, pl.ds(0, count)] = jnp.broadcast_to(class_ref[...], (8, count))


def unpack_loads_kernel(loads_ref, own_ref, weight_ref, out_ref):
    unpack_field_kernel(loads_ref, out_ref)
    _, layer = place()
    supplied = jnp.where(layer == lax.axis_size("layer") - 1, weight_ref[...], 0.0)
    cells = own_ref[...]
    for row in range(out_ref.shape[0]):
        out_ref[row] = out_ref[row] - marked(cells, row, supplied)


def unpack_volts_kernel(volts_ref, after_ref, x_ref):
    unpack_field_kernel(volts_ref, x_ref)


def unpack_kernel(index_ref, own_ref, count_ref, table_ref, across_ref, down_ref, cells_ref, weight_ref):
    cells_ref[...] = own_ref[...]
    weight_ref[...] = weight_of(count_ref)
    rows, cols = index_ref.shape[2:]
    tile, _ = place()
    last_tile = tile == lax.axis_size("tile") - 1
    table = table_ref[...]
    lane = lax.broadcasted_iota(jnp.int32, (8, LANES), 1)
    sub = lax.broadcasted_iota(jnp.int32, (8, LANES), 0)
    for top in range(0, rows, 8):
        part = pl.ds(top, 8)
        for start in range(0, cols, LANES):
            here, line = pl.ds(start, LANES), start // LANES
            across = jnp.take_along_axis(table, index_ref[0, 0, part, here], axis=1, mode="promise_in_bounds")
            if start + LANES == cols:
                across = jnp.where(lane == LANES - 1, 0.0, across)
            across_ref[part, line, :] = across
            down = jnp.take_along_axis(table, index_ref[0, 1, part, here], axis=1, mode="promise_in_bounds")
            if top + 8 == rows:
                down = jnp.where((sub == 7) & last_tile, 0.0, down)
            down_ref[part, line, :] = down


def via_terms(own_ref, own_weight_ref, low_ref, low_weight, from_above, from_below):
    _, layer = place()
    layers = lax.axis_size("layer")
    own_weight = own_weight_ref[...]
    low_weight = jnp.where(layer == 0, 0.0, low_weight)
    own, low = own_ref[...], low_ref[...]

    def via(row):
        return marked(own, row, own_weight) + marked(low, row, low_weight)

    if layers == 2:
        cells = jnp.where(layer == 0, own, low)
        source = jnp.where(layer == 0, own_weight, low_weight) * from_above

        def moving(row):
            return marked(cells, row, source)

        return via, moving
    own_source = jnp.where(layer == layers - 1, 0.0, own_weight * from_above)
    low_source = low_weight * from_below

    def moving(row):
        return marked(own, row, own_source) + marked(low, row, low_source)

    return via, moving


def send_by_parity(first_ref, second_ref, slot, top, bottom):
    tile, _ = place()
    even = lax.rem(tile, 2) == 0
    part = pl.ds(slot * top.shape[0], top.shape[0])
    first_ref[part] = jnp.where(even, bottom, top)
    second_ref[part] = jnp.where(even, top, bottom)
    lengths = first_ref.shape[0], second_ref.shape[0]
    if slot == 0:
        longer = first_ref if lengths[0] > lengths[1] else second_ref
        longer[pl.ds(min(lengths), FILL)] = jnp.zeros((FILL, LANES), jnp.float32)


def by_parity(work):
    tile, _ = place()
    even = lax.rem(tile, 2) == 0
    for side in range(2):
        pl.when(even if side == 1 else jnp.logical_not(even))(functools.partial(work, side))


def taken_by_parity(first_ref, second_ref, slot, lines):
    tile, _ = place()
    even = lax.rem(tile, 2) == 0
    part = pl.ds(slot * lines, lines)
    first, second = first_ref[part], second_ref[part]
    return jnp.where(even, second, first), jnp.where(even, first, second)


def edge_flow(x_ref, across_ref, down_ref, row):
    return beside(x_ref[row], across_ref[row]) + down_ref[row] * x_ref[row + 1] + down_ref[row - 1] * x_ref[row - 1]


def edge_ends(rows):
    return (0, 1, 0), (rows - 1, rows - 2, rows - 2)


def edges(x_ref, across_ref, down_ref, right_side, inverses, rows):
    found = []
    for (edge, within, link), inverse in zip(edge_ends(rows), inverses):
        x = x_ref[within]
        flow = edge_flow(x_ref, across_ref, down_ref, within)
        later = x + FACTORS[0][1] * (inverse * (right_side(within) + flow) - x)
        found.append((right_side(edge) + down_ref[link] * x, right_side(edge) + down_ref[link] * later))
    return tuple(zip(*found))


def links_kernel(
    single, x_ref, across_ref, down_ref, own_ref, low_ref, first_ref, second_ref, *sends
):
    rows = x_ref.shape[0]
    links = chosen(single, own_ref[...], low_ref[...])
    for send_ref, cells in zip(sends, links):
        send_ref[0] = pick(x_ref, cells, rows)
    for slot, ref in enumerate((x_ref, across_ref, down_ref)):
        send_by_parity(first_ref, second_ref, slot, ref[0], ref[rows - 1])
    if single:
        send_by_parity(first_ref, second_ref, 3, marked(links[0], 0, 1.0), marked(links[0], rows - 1, 1.0))


def first_edges_kernel(
    rows,
    x_ref,
    across_ref,
    down_ref,
    loads_ref,
    own_ref,
    own_weight_ref,
    low_ref,
    low_count_ref,
    above_ref,
    below_ref,
    first_ref,
    second_ref,
):
    via, moving = via_terms(own_ref, own_weight_ref, low_ref, weight_of(low_count_ref), above_ref[0], below_ref[0])

    def right_side(row):
        return moving(row) - loads_ref[row]

    def diagonal(row, links):
        across = across_ref[row]
        total = across + column_left(across)
        for link in links:
            total = total + down_ref[link]
        return total + via(row)

    inverses = 1.0 / diagonal(1, (0, 1)), 1.0 / diagonal(rows - 2, (rows - 3, rows - 2))
    for slot, pair in enumerate(edges(x_ref, across_ref, down_ref, right_side, inverses, rows)):
        send_by_parity(first_ref, second_ref, slot, *pair)
    send_by_parity(first_ref, second_ref, 2, diagonal(0, (0,)), diagonal(rows - 1, (rows - 2,)))


def next_early_kernel(
    single,
    rows,
    x_ref,
    across_ref,
    down_ref,
    loads_ref,
    inverse_ref,
    own_ref,
    own_weight_ref,
    low_ref,
    low_count_ref,
    after_ref,
    first_ref,
    second_ref,
    *factor_refs,
):
    _, layer = place()

    def right_side(row):
        return -loads_ref[row]

    send_by_parity(first_ref, second_ref, 0, x_ref[0], x_ref[rows - 1])
    inverses = inverse_ref[1], inverse_ref[rows - 2]
    for slot, pair in enumerate(edges(x_ref, across_ref, down_ref, right_side, inverses, rows)):
        send_by_parity(first_ref, second_ref, 1 + slot, *pair)
    if single:
        cells = jnp.where(layer == 0, own_ref[...], low_ref[...])
        weight = jnp.where(layer == 0, own_weight_ref[...], weight_of(low_count_ref))
        factors = []
        for (edge, within, link), inverse in zip(edge_ends(rows), inverses):
            share = FACTORS[0][1] * inverse * down_ref[link]
            factors.append(marked(cells, edge, weight) + marked(cells, within, weight * share))
        for ref, factor in zip(factor_refs, factors):
            ref[...] = factor


def next_late_kernel(
    rows, down_ref, inverse_ref, own_ref, own_weight_ref, low_ref, low_count_ref, above_ref, below_ref, first_ref, second_ref
):
    _, moving = via_terms(own_ref, own_weight_ref, low_ref, weight_of(low_count_ref), above_ref[0], below_ref[0])
    found = []
    for edge, within, link in edge_ends(rows):
        change = moving(edge)
        share = FACTORS[0][1] * inverse_ref[within] * down_ref[link]
        found.append((change, change + share * moving(within)))
    for slot, pair in enumerate(zip(*found)):
        send_by_parity(first_ref, second_ref, slot, *pair)


def next_late_single_kernel(top_ref, bottom_ref, volts_ref, first_ref, second_ref):
    volts = volts_ref[0]
    send_by_parity(first_ref, second_ref, 0, top_ref[...] * volts, bottom_ref[...] * volts)


def relaxed(x, flow, side, inverse, previous, sweep):
    keep, gain = FACTORS[sweep]
    update = gain * (inverse * (side + flow) - x)
    if sweep > 0:
        update = update + keep * previous
    return x + update, update


def chosen(single, own, low):
    _, layer = place()
    return [jnp.where(layer == 0, own, low)] if single else [own, low]


def inner_rows(
    rows, reach, outside, x_ref, across_ref, down_ref, side_ref, inverse_ref, work, update_ref, core_ref, keep_ref
):
    sources = [x_ref, *work]
    targets = [*work, core_ref]
    for sweep in range(SWEEPS):
        source, target = sources[sweep], targets[sweep]
        for row in range(sweep + reach, rows - sweep - reach):
            x = source[row]
            flow = beside(x, across_ref[row])
            if row == 0:
                flow = flow + outside[0]
            else:
                flow = flow + down_ref[row - 1] * source[row - 1]
            if row == rows - 1:
                flow = flow + outside[1]
            else:
                flow = flow + down_ref[row] * source[row + 1]
            previous = update_ref[row] if sweep > 0 else None
            value, update = relaxed(x, flow, side_ref[row], inverse_ref[row], previous, sweep)
            target[row] = value
            if sweep < SWEEPS - 1:
                update_ref[row] = update
                for side, depth in ((0, row), (1, rows - 1 - row)):
                    slot = 3 * (2 * sweep + side)
                    if depth == sweep + reach:
                        keep_ref[slot] = value
                        keep_ref[slot + 2] = update
                    if depth == sweep + reach + 1:
                        keep_ref[slot + 1] = value


def outer_rows(side, rows, reach, halo, link, inverse_edge, x_ref, across_ref, down_ref, side_ref, inverse_ref, keep_ref):
    edge_x, edge_q, edge_across = halo

    def row_of(depth):
        return depth if side == 0 else rows - 1 - depth

    def link_out(depth):
        if depth == 0:
            return link
        return down_ref[depth - 1] if side == 0 else down_ref[rows - 1 - depth]

    def link_in(depth):
        return down_ref[depth] if side == 0 else down_ref[rows - 2 - depth]

    values = {-1: edge_x}
    for depth in range(reach + 1):
        values[depth] = x_ref[row_of(depth)]
    updates = {}
    for sweep in range(SWEEPS):
        found, changed = {}, {}
        if sweep < SWEEPS - 1:
            x = values[-1]
            flow = beside(x, edge_across) + link * values[0]
            found[-1], changed[-1] = relaxed(x, flow, edge_q[sweep], inverse_edge, updates.get(-1), sweep)
        for depth in range(sweep + reach):
            row = row_of(depth)
            x = values[depth]
            flow = beside(x, across_ref[row]) + link_out(depth) * values[depth - 1] + link_in(depth) * values[depth + 1]
            found[depth], changed[depth] = relaxed(x, flow, side_ref[row], inverse_ref[row], updates.get(depth), sweep)
        if sweep < SWEEPS - 1:
            slot = 3 * (2 * sweep + side)
            found[sweep + reach] = keep_ref[slot]
            changed[sweep + reach] = keep_ref[slot + 2]
            found[sweep + reach + 1] = keep_ref[slot + 1]
        values, updates = found, changed
    return {row_of(depth): value for depth, value in values.items()}


KEPT = 6 * (SWEEPS - 1)


def first_inner_kernel(
    single,
    rows,
    x_ref,
    across_ref,
    down_ref,
    loads_ref,
    own_ref,
    own_weight_ref,
    low_ref,
    low_count_ref,
    above_ref,
    below_ref,
    first_ref,
    second_ref,
    after_ref,
    core_ref,
    side_ref,
    inverse_ref,
    keep_ref,
    halo_ref,
    picked_ref,
    *scratch,
):
    tile, _ = place()
    via, moving = via_terms(own_ref, own_weight_ref, low_ref, weight_of(low_count_ref), above_ref[0], below_ref[0])
    top_x, low_x = taken_by_parity(first_ref, second_ref, 0, x_ref.shape[1])
    top_across, low_across = taken_by_parity(first_ref, second_ref, 1, x_ref.shape[1])
    link, _ = taken_by_parity(first_ref, second_ref, 2, x_ref.shape[1])
    link = jnp.where(tile == 0, 0.0, link)
    held = [top_across, low_across, link, top_x, low_x]
    if single:
        held.extend(taken_by_parity(first_ref, second_ref, 3, x_ref.shape[1]))
    for slot, value in enumerate(held):
        halo_ref[slot] = value
    for row in range(rows):
        side_ref[row] = moving(row) - loads_ref[row]
        across = across_ref[row]
        diagonal = across + column_left(across) + down_ref[row] + via(row)
        diagonal = diagonal + (down_ref[row - 1] if row > 0 else link)
        inverse_ref[row] = 1.0 / diagonal
    outside = link * top_x, down_ref[rows - 1] * low_x
    shared = (x_ref, across_ref, down_ref, side_ref, inverse_ref)
    inner_rows(rows, 0, outside, *shared, scratch[:-1], scratch[-1], core_ref, keep_ref)
    for index, cells in enumerate(chosen(single, own_ref[...], low_ref[...])):
        total = jnp.zeros(cells.shape, jnp.float32)
        for row in range(SWEEPS - 1, rows - SWEEPS + 1):
            total = total + marked(cells, row, core_ref[row])
        picked_ref[index] = total


def first_rim(
    single,
    rows,
    side,
    x_ref,
    across_ref,
    down_ref,
    side_ref,
    inverse_ref,
    keep_ref,
    halo_ref,
    own_ref,
    low_ref,
    picked_ref,
    late_ref,
    next_ref,
    edge_ref,
    totals,
):
    lines = x_ref.shape[1]
    q0, q1, diagonal = (late_ref[pl.ds(slot * lines, lines)] for slot in range(3))
    link = halo_ref[2] if side == 0 else down_ref[rows - 1]
    inverse = 1.0 / (diagonal + link)
    edge_ref[side] = inverse
    shared = (x_ref, across_ref, down_ref, side_ref, inverse_ref, keep_ref)
    outer = outer_rows(side, rows, 0, (halo_ref[3 + side], (q0, q1), halo_ref[side]), link, inverse, *shared)
    for row, value in outer.items():
        next_ref[row] = value
    for index, cells in enumerate(chosen(single, own_ref[...], low_ref[...])):
        total = picked_ref[index]
        for row, value in outer.items():
            total = total + marked(cells, row, value)
        totals(index, total)


def first_near_kernel(single, rows, *refs):
    *ins, _, next_ref, edge_ref, found_ref = refs

    def found(index, total):
        found_ref[index] = total

    by_parity(lambda side: first_rim(single, rows, side, *ins, next_ref, edge_ref, found))


def first_far_kernel(single, rows, *refs):
    count = 1 if single else 2
    *ins, _, _, next_ref, edge_ref = refs[:-count]
    sends = refs[-count:]

    def found(index, total):
        sends[index][0] = total

    by_parity(lambda near: first_rim(single, rows, 1 - near, *ins, next_ref, edge_ref, found))


def last_inner_kernel(
    rows,
    x_ref,
    across_ref,
    down_ref,
    loads_ref,
    inverse_ref,
    own_ref,
    own_weight_ref,
    low_ref,
    low_count_ref,
    above_ref,
    below_ref,
    after_ref,
    core_ref,
    side_ref,
    keep_ref,
    *scratch,
):
    _, moving = via_terms(own_ref, own_weight_ref, low_ref, weight_of(low_count_ref), above_ref[0], below_ref[0])
    for row in range(rows):
        side_ref[row] = moving(row) - loads_ref[row]
    shared = (x_ref, across_ref, down_ref, side_ref, inverse_ref)
    inner_rows(rows, 1, None, *shared, scratch[:-1], scratch[-1], core_ref, keep_ref)


def last_middle_kernel(
    single,
    rows,
    x_ref,
    across_ref,
    down_ref,
    side_ref,
    inverse_ref,
    keep_ref,
    halo_ref,
    edge_ref,
    first_ref,
    second_ref,
    late_ref,
    core_ref,
    kept_ref,
    laid_ref,
    row_ref,
    rim,
):
    edge_x = taken_by_parity(first_ref, second_ref, 0, x_ref.shape[1])
    for side in range(2):
        outside = halo_ref[2] * edge_x[0] if side == 0 else down_ref[rows - 1] * edge_x[1]
        further = x_ref[0 if side == 0 else rows - 1], x_ref[1 if side == 0 else rows - 2]
        previous = None
        for sweep in range(SWEEPS):
            row = sweep if side == 0 else rows - 1 - sweep
            links = (row - 1, row) if side == 0 else (row, row - 1)
            x, within = further
            flow = beside(x, across_ref[row]) + (outside if sweep == 0 else down_ref[links[0]] * outside)
            flow = flow + down_ref[links[1]] * within
            value, update = relaxed(x, flow, side_ref[row], inverse_ref[row], previous, sweep)
            if sweep == SWEEPS - 1:
                row_ref[side] = value
                break
            slot = 3 * (2 * sweep + side)
            kept_ref[slot] = value
            kept_ref[slot + 1] = keep_ref[slot]
            kept_ref[slot + 2] = update
            further = keep_ref[slot], keep_ref[slot + 1]
            previous = keep_ref[slot + 2]
            outside = value
    for top in range(0, rows, 8):
        for line in range(x_ref.shape[1]):
            laid_ref[pl.ds(top, 8), pl.ds(line * LANES, LANES)] = core_ref[pl.ds(top, 8), line, :]
    for side, row in enumerate((SWEEPS - 1, rows - SWEEPS)):
        for line in range(x_ref.shape[1]):
            laid_ref[pl.ds(row, 1), pl.ds(line * LANES, LANES)] = row_ref[side, pl.ds(line, 1), :]
    known = (x_ref, across_ref, down_ref, side_ref, inverse_ref, kept_ref, halo_ref, edge_ref)
    by_parity(lambda near: rim_rows(single, rows, near, *known, first_ref, late_ref, laid_ref, rim))


def rim_rows(
    single,
    rows,
    side,
    x_ref,
    across_ref,
    down_ref,
    side_ref,
    inverse_ref,
    keep_ref,
    halo_ref,
    edge_ref,
    early_ref,
    late_ref,
    laid_ref,
    rim,
):
    lines = x_ref.shape[1]

    def row_of(ref, slot):
        return ref[pl.ds(slot * lines, lines)]

    if single:
        changes = halo_ref[5 + side] * row_of(late_ref, 0), row_of(late_ref, 0)
    else:
        changes = row_of(late_ref, 0), row_of(late_ref, 1)
    sides = row_of(early_ref, 1) + changes[0], row_of(early_ref, 2) + changes[1]
    outer = outer_rows(
        side,
        rows,
        0,
        (row_of(early_ref, 0), sides, halo_ref[side]),
        halo_ref[2] if side == 0 else down_ref[rows - 1],
        edge_ref[side],
        *(x_ref, across_ref, down_ref, side_ref, inverse_ref, keep_ref),
    )
    count = SWEEPS - 1
    base = 0 if side == 0 else rows - count
    for row, value in outer.items():
        rim[row - base] = value
    for line in range(lines):
        laid_ref[pl.ds(base, count), pl.ds(line * LANES, LANES)] = rim[:, line, :]


def last_far_kernel(single, rows, *refs):
    *ins, _, out_ref, laid_ref, rim, sems = refs
    half = rows // 2

    def work(near):
        copies = []
        for side in (near, 1 - near):
            if side != near:
                rim_rows(single, rows, side, *ins, laid_ref, rim)
            part = pl.ds(side * half, half)
            copy = pltpu.make_async_copy(laid_ref.at[part], out_ref.at[part], sems.at[side])
            copy.start()
            copies.append(copy)
        for copy in copies:
            copy.wait()

    by_parity(work)


def call(kernel, name, ins, outs, scratch=(), aliases=None, work=None):
    spaces = {"vmem": pltpu.VMEM, "hbm": pltpu.HBM, "any": pl.ANY}
    return pl.pallas_call(
        kernel,
        out_shape=[jax.ShapeDtypeStruct(shape, *(kind or [jnp.float32])) for _, shape, *kind in outs],
        in_specs=[pl.BlockSpec(memory_space=spaces[space]) for space, _ in ins],
        out_specs=[pl.BlockSpec(memory_space=spaces[space]) for space, *_ in outs],
        scratch_shapes=list(scratch),
        input_output_aliases=aliases or {},
        compiler_params=pltpu.CompilerParams(vmem_limit_bytes=40 * 1024 * 1024),
        cost_estimate=work and pl.CostEstimate(flops=work, bytes_accessed=work, transcendentals=0),
        name=name,
    )(*(pltpu.with_memory_space_constraint(array, pltpu.HBM) if space == "hbm" else array for space, array in ins))


def routes(tiles, layers):
    def at(tile, layer):
        return tile * layers + layer % layers

    everywhere = [(tile, layer) for tile in range(tiles) for layer in range(layers)]
    up = [(at(t, l), at(t, l + 1)) for t, l in everywhere]
    down = [(at(t, l), at(t, l - 1)) for t, l in everywhere]
    first, second = [], []
    for t, l in everywhere:
        first.append((at(t, l), at(t ^ 1, l)))
        beyond = t + 1 if t % 2 else t - 1
        if 0 <= beyond < tiles:
            second.append((at(t, l), at(beyond, l)))
        else:
            second.append((at(t, l), at(t, l + 1)))
    return up, down, first, second


def local(class_index, class_conductance, loads, start_volts, via_cells, via_counts):
    rows, cols = loads.shape[1:]
    lines = cols // LANES
    tiles, layers = lax.axis_size("tile"), lax.axis_size("layer")
    up, down, first, second = routes(tiles, layers)
    single = layers == 2
    move = functools.partial(lax.ppermute, axis_name=("tile", "layer"))

    def rows_of(count):
        return (count, lines, LANES)

    def messages(count, longer):
        return [("vmem", (count * lines + (FILL if longer == side else 0), LANES)) for side in range(2)]

    def vmem(*arrays):
        return [("vmem", array) for array in arrays]

    def between_layers(sends):
        if single:
            got = move(sends[0], perm=up)
            return got, got
        return move(sends[1], perm=down), move(sends[0], perm=up)

    def beside_tile(sent):
        across_chips = move(sent[1], perm=second)
        return move(sent[0], perm=first), across_chips

    field = ("vmem", rows_of(rows))
    work = [pltpu.VMEM(rows_of(rows), jnp.float32)] * SWEEPS
    pick_count = 1 if single else 2
    picks = [("vmem", rows_of(1))] * pick_count

    cells = via_cells.reshape(lines, LANES)
    counts = via_counts.reshape(lines, LANES)
    low = move(cells, perm=up)
    low_count = move(counts, perm=up)
    (table,) = call(table_kernel, "table", vmem(class_conductance), [("vmem", (8, LANES))], work=3*10**8)
    across, downward, own, own_weight = call(
        unpack_kernel,
        "unpack",
        vmem(class_index, cells, counts, table),
        [field] * 2 + [("vmem", cells.shape, cells.dtype), ("vmem", cells.shape)],
        work=3*10**8,
    )
    (x,) = call(unpack_volts_kernel, "unpack_volts", vmem(start_volts) + [("any", across)], [field])
    vias = (own, own_weight, low, low_count)
    first_sent, second_sent, *sends = call(
        functools.partial(links_kernel, single),
        "links",
        vmem(x, across, downward, own, low),
        messages(4 if single else 3, 1) + picks,
    )
    above, below = between_layers(sends)
    (load,) = call(unpack_loads_kernel, "unpack_loads", vmem(loads, own, own_weight), [field])
    early = beside_tile((first_sent, second_sent))
    sent = call(
        functools.partial(first_edges_kernel, rows),
        "first_edges",
        vmem(x, across, downward, load, *vias, above, below),
        messages(3, 0),
        work=2 * 10**10,
    )
    got = beside_tile(sent)
    core, side, inverse, keep, halo, picked = call(
        functools.partial(first_inner_kernel, single, rows),
        "first_inner",
        vmem(x, across, downward, load, *vias, above, below, *early) + [("any", sent[1])],
        [field, field, field, ("vmem", rows_of(KEPT)), ("vmem", rows_of(7 if single else 5)), ("vmem", rows_of(pick_count))],
        work,
    )
    known = vmem(x, across, downward, side, inverse, keep, halo, own, low)
    near_x, near_edge, near_picked = call(
        functools.partial(first_near_kernel, single, rows),
        "first_near",
        known + vmem(picked, got[0], core),
        [field, ("vmem", rows_of(2)), ("vmem", rows_of(pick_count))],
        aliases={11: 0},
    )
    x, edge, *sends = call(
        functools.partial(first_far_kernel, single, rows),
        "first_far",
        known + vmem(near_picked, got[1], near_x, near_edge),
        [field, ("vmem", rows_of(2))] + picks,
        aliases={11: 0, 12: 1},
    )
    above, below = between_layers(sends)
    sent = call(
        functools.partial(next_early_kernel, single, rows),
        "next_early",
        vmem(x, across, downward, load, inverse, *vias) + [("any", sends[0])],
        messages(3, 0) + [("vmem", cells.shape)] * (2 if single else 0),
    )
    early = beside_tile(sent[:2])
    if single:
        late = call(
            next_late_single_kernel,
            "next_late",
            vmem(*sent[2:], above),
            messages(1, 1),
            work=2 * 10**10,
        )
    else:
        late = call(
            functools.partial(next_late_kernel, rows),
            "next_late",
            vmem(downward, inverse, *vias, above, below),
            messages(2, 1),
            work=2 * 10**10,
        )
    got = beside_tile(late)
    core, side, keep = call(
        functools.partial(last_inner_kernel, rows),
        "last_inner",
        vmem(x, across, downward, load, inverse, *vias, above, below) + [("any", late[1])],
        [field, field, ("vmem", rows_of(KEPT))],
        work,
    )
    rim = pltpu.VMEM((SWEEPS - 1, lines, LANES), jnp.float32)
    keep, laid = call(
        functools.partial(last_middle_kernel, single, rows),
        "last_middle",
        vmem(x, across, downward, side, inverse, keep, halo, edge, *early, got[0], core),
        [("vmem", rows_of(KEPT)), ("vmem", (rows, cols))],
        [pltpu.VMEM(rows_of(2), jnp.float32), rim],
    )
    plane = ("vmem", (rows, cols))
    known = vmem(x, across, downward, side, inverse, keep, halo, edge)
    volts, _ = call(
        functools.partial(last_far_kernel, single, rows),
        "last_far",
        known + vmem(early[1], got[1], laid),
        [("hbm", (rows, cols)), plane],
        [rim, pltpu.SemaphoreType.DMA((2,))],
        aliases={10: 1},
    )
    return volts[None]


def solution(mesh):
    placed = (
        P("layer", None, "tile", None),
        P("layer", None),
        P("layer", "tile", None),
        P("layer", "tile", None),
        P("layer", "tile"),
        P("layer", "tile"),
    )
    return jax.shard_map(
        local, mesh=mesh, in_specs=placed, out_specs=P("layer", "tile", None), check_vma=False
    )
```
